32 devices in a mesh: prefill: 4 (over z), prefix: 4 (over y, x), tensor: 2 (over core).
Axes of the slice: x: 2, y: 2, z: 4, core: 2. Of those that a mesh axis runs over, the one named last changes fastest.
Arguments:
- hidden_in: bfloat16 [128, 4, 4608], P('prefill', None, 'prefix'), may hold values from -12 to 12
- pre_gain: float32 [4608], P('prefix'), may hold values from 0.1 to 1.9
- w_query: bfloat16 [4608, 4096], P('prefix', 'tensor'), may hold values from -0.1875 to 0.1875
- key_projection: bfloat16 [4608, 2048], P('prefix', 'tensor'), may hold values from -0.25 to 0.25
- value_projection: bfloat16 [4608, 2048], P('prefix', 'tensor'), may hold values from -0.09375 to 0.09375
- w_out: bfloat16 [4096, 4608], P('tensor', 'prefix'), may hold values from -0.125 to 0.125
- post_gain: float32 [4608], P('prefix'), may hold values from 0.1 to 1.9
- prompt_keys: bfloat16 [8192, 2048], P(('prefill', 'prefix'), 'tensor'), may hold values from -6 to 6
- prompt_values: bfloat16 [8192, 2048], P(('prefill', 'prefix'), 'tensor'), may hold values from -6 to 6
- suffix_key_cache: bfloat16 [128, 256, 2048], P(('prefill', 'prefix'), None, 'tensor'), may hold values from -12 to 12
- suffix_value_cache: bfloat16 [128, 256, 2048], P(('prefill', 'prefix'), None, 'tensor'), may hold values from -6 to 6
- suffix_len: int32 [128], P('prefill'), may hold values from 1 to 256, as said below
Outputs:
- hidden_out: bfloat16 [128, 4, 4608], P('prefill', None, 'prefix')
The draws below stay inside these ranges and needn't reach their ends.
Inputs may be any that keep to these rules, and one draw needn't show every extreme that they name: `suffix_len`: some row has exactly 256 valid entries.
All inputs are finite; a program needn't handle non-finite values.
Results may differ from the reference program's by a relative error of at most 0.0092.
Values may be sent and summed in bfloat16 or wider, within the bound.
No kernel may reach another device: no remote copies, remote signals or barrier semaphores. Data moves between devices by JAX's collectives and lax.ppermute only.
A program may use at most 128 MiB of HBM per device.

```python
import math
import jax
import jax.numpy as jnp
from jax import lax

MODEL_WIDTH = 4608
QUERY_HEADS = 32
KEY_VALUE_HEADS = 16
HEAD_SIZE = 128
SUFFIX_SLOTS = 256
DECODE_STEPS = 4
DECODED_ROWS = 128
PROMPT_TOKENS = 8192


def draw_hidden_in(key, part):
    key = jax.random.fold_in(key, 11)
    base_key, row_key, col_key = jax.random.split(key, 3)
    shape = (DECODED_ROWS, DECODE_STEPS, MODEL_WIDTH)
    base = jnp.clip(jax.random.normal(base_key, shape, jnp.float32), -4.0, 4.0)
    row_scale = jnp.exp(jax.random.uniform(row_key, (DECODED_ROWS, DECODE_STEPS, 1), jnp.float32, math.log(0.5), math.log(2.0)))
    ramp = jnp.arange(MODEL_WIDTH, dtype=jnp.float32) / MODEL_WIDTH
    col_scale = jnp.exp(math.log(10.0) * (ramp - 1.0) + jax.random.uniform(col_key, (MODEL_WIDTH,), jnp.float32, math.log(0.7), math.log(1.4)))
    return (base * row_scale * col_scale).astype(jnp.bfloat16)


def draw_suffix_len(key, part):
    key = jax.random.fold_in(key, 23)
    len_key, pick_key = jax.random.split(key)
    lengths = jax.random.randint(len_key, (DECODED_ROWS,), 1, SUFFIX_SLOTS + 1, dtype=jnp.int32)
    chosen = jax.random.randint(pick_key, (), 0, DECODED_ROWS, dtype=jnp.int32)
    return jnp.where(jnp.arange(DECODED_ROWS, dtype=jnp.int32) == chosen, SUFFIX_SLOTS, lengths).astype(jnp.int32)


def with_spikes(values, key, source, target, blocks, factor):
    def block_of(axis_at):
        return (jnp.arange(values.shape[axis_at]) // (values.shape[axis_at] // blocks)).reshape((-1,) + (1,) * (values.ndim - 1 - axis_at))

    first = jax.random.permutation(key, blocks)[block_of(target)]
    other_side = (block_of(target) + blocks // 2) % blocks
    return jnp.where((block_of(source) == first) | (block_of(source) == other_side), factor * values, values)


def block_levels(stream_key, shape, cuts, smallest, high):
    def one(position, shards_of):
        steps = jax.random.uniform(jax.random.fold_in(jax.random.fold_in(stream_key, 6), position), (shards_of,), jnp.float32, smallest / len(cuts), high / len(cuts))
        return jnp.repeat(jnp.exp(steps), shape[position] // shards_of).reshape((-1,) + (1,) * (len(shape) - position - 1))

    level = one(*cuts[0])
    for cut in cuts[1:]:
        level = level * one(*cut)
    return level


def noise(own_key, shape, deviation, reach, cuts=(), kind=jnp.bfloat16):
    values = jax.random.normal(own_key, shape, jnp.float32) * deviation
    if len(cuts) > 0:
        values = block_levels(own_key, shape, cuts, -0.22, 0.18) * values
    return jnp.clip(values, min=-reach, max=reach).astype(kind)


def gaussian_with(own_key, extent, spread, bound, cuts, heavy, kind=jnp.bfloat16):
    values = spread * jax.random.normal(own_key, extent, jnp.float32)
    if cuts:
        values = values * block_levels(own_key, extent, cuts, -0.22, 0.18)
    return jnp.clip(with_spikes(values, jax.random.fold_in(own_key, 3), *heavy), -bound, bound).astype(kind)


def setup_inputs(seed: int = 0) -> dict:
    streams_of = jax.random.split(jax.random.key(seed), 13)
    hidden_in = draw_hidden_in(jax.random.fold_in(streams_of[12], 71), 0)
    pre_gain = jnp.clip(1.0 + 0.18 * jax.random.normal(streams_of[1], (MODEL_WIDTH,), jnp.float32), 0.1, 1.9)
    w_query = noise(streams_of[2], (MODEL_WIDTH, QUERY_HEADS * HEAD_SIZE), (MODEL_WIDTH // 4) ** -0.5, 0.1875, ((0, 4), (1, 2)))
    key_projection = noise(streams_of[3], (MODEL_WIDTH, KEY_VALUE_HEADS * HEAD_SIZE), (MODEL_WIDTH // 8) ** -0.5, 0.25, ((0, 4), (1, 2)))
    value_projection = noise(streams_of[4], (MODEL_WIDTH, KEY_VALUE_HEADS * HEAD_SIZE), MODEL_WIDTH ** -0.5, 0.09375, ((0, 4), (1, 2)))
    w_out = gaussian_with(streams_of[5], (QUERY_HEADS * HEAD_SIZE, MODEL_WIDTH), (QUERY_HEADS * HEAD_SIZE) ** -0.5, 0.125, ((0, 2), (1, 4)), (0, 1, 4, 2.0))
    post_gain = jnp.clip(1.0 + 0.18 * jax.random.normal(streams_of[6], (MODEL_WIDTH,), jnp.float32), 0.1, 1.9)
    prompt_keys = noise(streams_of[7], (PROMPT_TOKENS, KEY_VALUE_HEADS * HEAD_SIZE), 1.0, 6.0, ((0, 16), (1, 2)))
    prompt_values = noise(streams_of[8], (PROMPT_TOKENS, KEY_VALUE_HEADS * HEAD_SIZE), 1.0, 6.0, ((0, 16), (1, 2)))
    suffix_key_cache = noise(streams_of[9], (DECODED_ROWS, SUFFIX_SLOTS, KEY_VALUE_HEADS * HEAD_SIZE), 2.0, 12.0, ((0, 16), (2, 2)))
    suffix_value_cache = noise(streams_of[10], (DECODED_ROWS, SUFFIX_SLOTS, KEY_VALUE_HEADS * HEAD_SIZE), 1.0, 6.0, ((0, 16), (2, 2)))
    suffix_len = draw_suffix_len(jax.random.fold_in(streams_of[12], 71), 0)
    return {"hidden_in": hidden_in, "pre_gain": pre_gain, "w_query": w_query, "key_projection": key_projection, "value_projection": value_projection, "w_out": w_out, "post_gain": post_gain, "prompt_keys": prompt_keys, "prompt_values": prompt_values, "suffix_key_cache": suffix_key_cache, "suffix_value_cache": suffix_value_cache, "suffix_len": suffix_len}


SOFTCAP = 50.0
EPSILON = 1e-06

def apply_rotation(values, token_positions, heads):
    width = values.shape[1] // heads
    half = width // 2
    freq = 10000.0 ** (-2.0 * jnp.arange(half, dtype=jnp.float32) / width)
    angle = token_positions[:, None] * freq[None, :]
    cosine = jnp.cos(angle)[:, None, :]
    sine = jnp.sin(angle)[:, None, :]
    parts = values.reshape(values.shape[0], heads, width)
    first = parts[:, :, :half]
    second = parts[:, :, half:]
    turned = jnp.concatenate([first * cosine - second * sine, second * cosine + first * sine], axis=2)
    return turned.reshape(values.shape[0], heads * width)

def soft_weight(scores):
    return jnp.exp(SOFTCAP * jnp.tanh(scores / SOFTCAP))

def reference(hidden_in, pre_gain, w_query, key_projection, value_projection, w_out, post_gain, prompt_keys, prompt_values, suffix_key_cache, suffix_value_cache, suffix_len):
    heads_per_group = QUERY_HEADS // KEY_VALUE_HEADS
    row_count = DECODED_ROWS * DECODE_STEPS
    signal = hidden_in.astype(jnp.float32).reshape(row_count, MODEL_WIDTH)
    normed = (signal * lax.rsqrt(lax.optimization_barrier(jnp.mean(signal * signal, axis=1, keepdims=True)) + EPSILON) * pre_gain).astype(jnp.bfloat16)
    step_ids = jnp.arange(DECODE_STEPS, dtype=jnp.int32)
    token_positions = (PROMPT_TOKENS + suffix_len[:, None] + step_ids[None, :]).reshape(-1).astype(jnp.float32)
    query_raw = jnp.dot(normed, w_query, preferred_element_type=jnp.float32)
    unrotated_key = jnp.dot(normed, key_projection, preferred_element_type=jnp.float32)
    value_raw = jnp.dot(normed, value_projection, preferred_element_type=jnp.float32)
    scale = (MODEL_WIDTH // QUERY_HEADS) ** (-0.5)
    query_vector = (apply_rotation(query_raw, token_positions, QUERY_HEADS) * scale).astype(jnp.bfloat16)
    latest_keys = apply_rotation(unrotated_key, token_positions, KEY_VALUE_HEADS).astype(jnp.bfloat16)
    latest_values = value_raw.astype(jnp.bfloat16)
    layer_block = 8 * DECODE_STEPS
    layer_blocks = query_vector.reshape(row_count // layer_block, layer_block, KEY_VALUE_HEADS, heads_per_group, HEAD_SIZE)
    key_head_rows = prompt_keys.astype(jnp.float32).reshape(PROMPT_TOKENS, KEY_VALUE_HEADS, HEAD_SIZE)
    value_head_rows = prompt_values.astype(jnp.float32).reshape(PROMPT_TOKENS, KEY_VALUE_HEADS, HEAD_SIZE)

    def prefix_block(block_queries):
        scores = jnp.einsum('nkgd,mkd->nkgm', block_queries.astype(jnp.float32), key_head_rows)
        weights = soft_weight(scores)
        rounded = lax.optimization_barrier(weights.astype(jnp.bfloat16))
        summed = jnp.einsum('nkgm,mkd->nkgd', rounded.astype(jnp.float32), value_head_rows)
        return (summed, lax.optimization_barrier(jnp.sum(weights, axis=3)))
    prompt_weight_sum, prompt_value_total = lax.map(prefix_block, layer_blocks)
    prompt_weight_sum = prompt_weight_sum.reshape(DECODED_ROWS, DECODE_STEPS, KEY_VALUE_HEADS, heads_per_group, HEAD_SIZE)
    prompt_value_total = prompt_value_total.reshape(DECODED_ROWS, DECODE_STEPS, KEY_VALUE_HEADS, heads_per_group)
    row_wise = query_vector.astype(jnp.float32).reshape(DECODED_ROWS, DECODE_STEPS, KEY_VALUE_HEADS, heads_per_group, HEAD_SIZE)
    cached_key_rows = suffix_key_cache.astype(jnp.float32).reshape(DECODED_ROWS, SUFFIX_SLOTS, KEY_VALUE_HEADS, HEAD_SIZE)
    cached_value_rows = suffix_value_cache.astype(jnp.float32).reshape(DECODED_ROWS, SUFFIX_SLOTS, KEY_VALUE_HEADS, HEAD_SIZE)
    valid = jnp.arange(SUFFIX_SLOTS, dtype=jnp.int32)[None, :] < suffix_len[:, None]
    cache_scores = jnp.einsum('bjkgd,bmkd->bjkgm', row_wise, cached_key_rows)
    cache_weights = jnp.where(valid[:, None, None, None, :], soft_weight(cache_scores), 0.0)
    cache_rounded = lax.optimization_barrier(cache_weights.astype(jnp.bfloat16))
    cache_sum = jnp.einsum('bjkgm,bmkd->bjkgd', cache_rounded.astype(jnp.float32), cached_value_rows)
    appended_keys = latest_keys.astype(jnp.float32).reshape(DECODED_ROWS, DECODE_STEPS, KEY_VALUE_HEADS, HEAD_SIZE)
    appended_values = latest_values.astype(jnp.float32).reshape(DECODED_ROWS, DECODE_STEPS, KEY_VALUE_HEADS, HEAD_SIZE)
    causal = step_ids[None, :] <= step_ids[:, None]
    new_scores = jnp.einsum('bjkgd,bikd->bjkgi', row_wise, appended_keys)
    new_weights = jnp.where(causal[None, :, None, None, :], soft_weight(new_scores), 0.0)
    new_rounded = lax.optimization_barrier(new_weights.astype(jnp.bfloat16))
    new_sum = jnp.einsum('bjkgi,bikd->bjkgd', new_rounded.astype(jnp.float32), appended_values)
    totals = prompt_value_total + lax.optimization_barrier(jnp.sum(cache_weights, axis=4)) + lax.optimization_barrier(jnp.sum(new_weights, axis=4))
    sums = prompt_weight_sum + cache_sum + new_sum
    mixed = (sums / totals[..., None]).reshape(row_count, QUERY_HEADS * HEAD_SIZE).astype(jnp.bfloat16)
    attended = jnp.dot(mixed, w_out, preferred_element_type=jnp.float32)
    branch = attended * lax.rsqrt(lax.optimization_barrier(jnp.mean(attended * attended, axis=1, keepdims=True)) + EPSILON) * post_gain
    return (signal + branch).astype(jnp.bfloat16).reshape(DECODED_ROWS, DECODE_STEPS, MODEL_WIDTH)
```

```python
import functools

import jax
import jax.numpy as jnp
from jax import lax
from jax.experimental import pallas as pl
from jax.experimental.pallas import tpu as pltpu
from jax.sharding import PartitionSpec as P

MODEL_WIDTH = 4608
QUERY_HEADS = 32
HEAD_SIZE = 128


SOFTCAP = 50.0
EPSILON = 1e-06
LOG2_E = 1.4426950408889634
LANES = 128
VMEM_LIMIT = 32 * 1024 * 1024


def apply_rotation(values, token_positions, heads):
    width = values.shape[1] // heads
    half = width // 2
    freq = 10000.0 ** (-2.0 * jnp.arange(half, dtype=jnp.float32) / width)
    angle = token_positions[:, None] * freq[None, :]
    cosine = jnp.cos(angle)[:, None, :]
    sine = jnp.sin(angle)[:, None, :]
    parts = values.reshape(values.shape[0], heads, width)
    first = parts[:, :, :half]
    second = parts[:, :, half:]
    turned = jnp.concatenate(
        [first * cosine - second * sine, second * cosine + first * sine], axis=2
    )
    return turned.reshape(values.shape[0], heads * width)


def soft_weight(scores):
    return jnp.exp(SOFTCAP * jnp.tanh(scores / SOFTCAP))


def shared_attention(queries, keys, values):
    count = queries.shape[0]
    kv_heads = keys.shape[1] // HEAD_SIZE
    heads_per_group = queries.shape[1] // keys.shape[1]
    grouped = queries.reshape(count, kv_heads, heads_per_group, HEAD_SIZE)
    key_head_rows = keys.reshape(keys.shape[0], kv_heads, HEAD_SIZE)
    value_head_rows = values.reshape(values.shape[0], kv_heads, HEAD_SIZE)
    scores = jnp.einsum(
        "nkgd,mkd->nkgm", grouped, key_head_rows, preferred_element_type=jnp.float32
    )
    weights = soft_weight(scores)
    totals = jnp.sum(weights, axis=3).reshape(count, kv_heads * heads_per_group)
    summed = jnp.einsum(
        "nkgm,mkd->nkgd",
        weights.astype(jnp.bfloat16),
        value_head_rows,
        preferred_element_type=jnp.float32,
    )
    return (summed.reshape(count, kv_heads * heads_per_group * HEAD_SIZE), totals)


def own_attention(
    queries, cached_key_rows, cached_value_rows, latest_keys, latest_values, lengths, steps
):
    members = lengths.shape[0]
    slots = cached_key_rows.shape[1]
    kv_heads = cached_key_rows.shape[2] // HEAD_SIZE
    heads_per_group = queries.shape[1] // cached_key_rows.shape[2]
    grouped = queries.reshape(members, steps, kv_heads, heads_per_group, HEAD_SIZE)
    cache_k = cached_key_rows.reshape(members, slots, kv_heads, HEAD_SIZE)
    cache_v = cached_value_rows.reshape(members, slots, kv_heads, HEAD_SIZE)
    valid = jnp.arange(slots, dtype=jnp.int32)[None, :] < lengths[:, None]
    cache_scores = jnp.einsum(
        "rjkgd,rmkd->rjkgm", grouped, cache_k, preferred_element_type=jnp.float32
    )
    cache_weights = jnp.where(valid[:, None, None, None, :], soft_weight(cache_scores), 0.0)
    new_k = latest_keys.reshape(members, steps, kv_heads, HEAD_SIZE)
    new_v = latest_values.reshape(members, steps, kv_heads, HEAD_SIZE)
    step_ids = jnp.arange(steps, dtype=jnp.int32)
    causal = step_ids[None, :] <= step_ids[:, None]
    new_scores = jnp.einsum("rjkgd,rikd->rjkgi", grouped, new_k, preferred_element_type=jnp.float32)
    new_weights = jnp.where(causal[None, :, None, None, :], soft_weight(new_scores), 0.0)
    totals = jnp.sum(cache_weights, axis=4) + jnp.sum(new_weights, axis=4)
    summed = jnp.einsum(
        "rjkgm,rmkd->rjkgd",
        cache_weights.astype(jnp.bfloat16),
        cache_v,
        preferred_element_type=jnp.float32,
    )
    summed = summed + jnp.einsum(
        "rjkgi,rikd->rjkgd",
        new_weights.astype(jnp.bfloat16),
        new_v,
        preferred_element_type=jnp.float32,
    )
    flat_rows = members * steps
    return (
        summed.reshape(flat_rows, kv_heads * heads_per_group * HEAD_SIZE),
        totals.reshape(flat_rows, kv_heads * heads_per_group),
    )


def per_device(
    hidden_in,
    pre_gain,
    w_query,
    key_projection,
    value_projection,
    w_out,
    post_gain,
    prompt_keys,
    prompt_values,
    suffix_key_cache,
    suffix_value_cache,
    suffix_len,
):
    group_rows, steps, local_width = hidden_in.shape
    members = suffix_key_cache.shape[0]
    query_cols = w_query.shape[1]
    kv_cols = key_projection.shape[1]
    heads = query_cols // HEAD_SIZE
    kv_heads = kv_cols // HEAD_SIZE
    own_count = members * steps
    prompt_total = prompt_keys.shape[0] * lax.axis_size("prefill") * lax.axis_size("prefix")
    signal = hidden_in.astype(jnp.float32).reshape(group_rows * steps, local_width)
    squares = lax.psum(jnp.sum(signal * signal, axis=1), "prefix")
    normed = (signal * lax.rsqrt(squares[:, None] / MODEL_WIDTH + EPSILON) * pre_gain).astype(
        jnp.bfloat16
    )
    weights_all = jnp.concatenate([w_query, key_projection, value_projection], axis=1)
    step_ids = jnp.arange(steps, dtype=jnp.int32)
    group_positions = (
        (prompt_total + suffix_len[:, None] + step_ids[None, :]).reshape(-1).astype(jnp.float32)
    )
    first_row = lax.axis_index("prefix") * members
    own_lengths = lax.dynamic_slice_in_dim(suffix_len, first_row, members)
    own_positions = lax.dynamic_slice_in_dim(group_positions, first_row * steps, own_count)
    scale = (MODEL_WIDTH // QUERY_HEADS) ** (-0.5)
    own_proj = lax.psum_scatter(
        jnp.dot(normed, weights_all, preferred_element_type=jnp.float32),
        "prefix",
        scatter_dimension=0,
        tiled=True,
    )
    own_queries = (apply_rotation(own_proj[:, :query_cols], own_positions, heads) * scale).astype(
        jnp.bfloat16
    )
    group_queries = lax.all_gather(own_queries, "prefix", axis=0, tiled=True)
    latest_keys = apply_rotation(
        own_proj[:, query_cols : query_cols + kv_cols], own_positions, kv_heads
    ).astype(jnp.bfloat16)
    latest_values = own_proj[:, query_cols + kv_cols :].astype(jnp.bfloat16)
    summed, totals = shared_attention(
        group_queries,
        lax.all_gather(prompt_keys, "prefill", axis=0, tiled=True),
        lax.all_gather(prompt_values, "prefill", axis=0, tiled=True),
    )
    prompt_totals = totals
    far_sums, far_totals = (
        lax.psum_scatter(summed, "prefix", scatter_dimension=0, tiled=True),
        lax.psum_scatter(prompt_totals, "prefix", scatter_dimension=0, tiled=True),
    )
    near_sums, near_totals = own_attention(
        own_queries,
        suffix_key_cache,
        suffix_value_cache,
        latest_keys,
        latest_values,
        own_lengths,
        steps,
    )
    totals = far_totals + near_totals
    sums = (far_sums + near_sums).reshape(own_count, heads, HEAD_SIZE)
    mixed = (sums / totals[:, :, None]).reshape(own_count, query_cols).astype(jnp.bfloat16)
    head_terms = jnp.dot(
        lax.all_gather(mixed, "prefix", axis=0, tiled=True),
        w_out,
        preferred_element_type=jnp.float32,
    )
    attended = lax.psum(head_terms, "tensor")
    out_squares = lax.psum(jnp.sum(attended * attended, axis=1), "prefix")
    branch = attended * lax.rsqrt(out_squares[:, None] / MODEL_WIDTH + EPSILON) * post_gain
    return (signal + branch).astype(jnp.bfloat16).reshape(group_rows, steps, local_width)


def paired(values, axis, mask):
    size = lax.axis_size(axis)
    return lax.ppermute(values, axis, [(i, i ^ mask) for i in range(size)])


def call(kernel, prefetch, operands, out_shape, in_specs, out_specs, grid, scratch, flops, moved):
    return pl.pallas_call(
        kernel,
        out_shape=out_shape,
        grid_spec=pltpu.PrefetchScalarGridSpec(
            num_scalar_prefetch=len(prefetch),
            grid=grid,
            in_specs=in_specs,
            out_specs=out_specs,
            scratch_shapes=scratch,
        ),
        compiler_params=pltpu.CompilerParams(vmem_limit_bytes=VMEM_LIMIT),
        cost_estimate=pl.CostEstimate(flops=flops, bytes_accessed=moved, transcendentals=0),
    )(*prefetch, *operands)


def whole(array):
    rank = len(array.shape)
    return pl.BlockSpec(array.shape, lambda *_: (0,) * rank)


def shape(dims, dtype):
    return jax.ShapeDtypeStruct(dims, dtype)


def dot_last(left, right):
    return lax.dot_general(left, right, (((1,), (1,)), ((), ())), preferred_element_type=jnp.float32)


def dot_first(left, right):
    return lax.dot_general(left, right, (((0,), (0,)), ((), ())), preferred_element_type=jnp.float32)


def capped_weight(scores):
    return jnp.exp2(jnp.tanh(scores * (1.0 / SOFTCAP)) * (SOFTCAP * LOG2_E))


def split_rows(rows):
    high = rows.astype(jnp.bfloat16).astype(jnp.float32)
    return jnp.concatenate([high, rows - high], axis=0).astype(jnp.bfloat16)


def joined_row(block, index):
    pair = block.astype(jnp.float32)
    return pair[index : index + 1] + pair[8 + index : 9 + index]


def down_rows(row):
    return jnp.broadcast_to(row, (LANES, row.shape[1])).T


def lower_half(tiles):
    return lax.broadcasted_iota(jnp.int32, tiles.shape, 1) < tiles.shape[1] // 2


def interleave(first, second):
    low = lower_half(first)
    half = first.shape[1] // 2
    return (
        jnp.where(low, first, pltpu.roll(second, half, 1)),
        jnp.where(low, pltpu.roll(first, half, 1), second),
    )


def rotated(values, cosine, sine):
    return values * cosine + pltpu.roll(values, HEAD_SIZE // 2, 1) * sine


def query_projection_kernel(place, x_ref, gain_ref, w_ref, *refs):
    *sent, own_ref, squares_ref, scaled = refs
    step = pl.program_id(0)
    rows = x_ref.shape[0]

    @pl.when(step == 0)
    def _():
        x = x_ref[...].astype(jnp.float32)
        scaled[...] = (x * gain_ref[...]).astype(jnp.bfloat16)
        total = jnp.sum(x * x, axis=1, keepdims=True)
        across = jnp.broadcast_to(total, (rows, LANES)).T[:8]
        squares_ref[...] = across
        tail = split_rows(across)
        for ref in sent:
            ref[rows:, :] = jnp.zeros((16, ref.shape[1]), jnp.bfloat16)
            ref[rows:, :rows] = tail

    product = jnp.dot(scaled[...], w_ref[...], preferred_element_type=jnp.float32)
    for index, ref in enumerate(sent):

        @pl.when(step == index)
        def _():
            ref[:rows, :] = product.astype(jnp.bfloat16)

    @pl.when(step == len(sent))
    def _():
        own_ref[...] = product


def query_projection(place, x, gain, weights, parts):
    rows, width = x.shape
    columns = weights.shape[1] // parts
    return call(
        query_projection_kernel,
        (place,),
        (x, gain, weights),
        [shape((rows + 16, columns), jnp.bfloat16)] * (parts - 1)
        + [shape((rows, columns), jnp.float32), shape((8, rows), jnp.float32)],
        [
            pl.BlockSpec((rows, width), lambda i, p: (0, 0)),
            pl.BlockSpec((1, width), lambda i, p: (0, 0)),
            pl.BlockSpec((width, columns), lambda i, p: (0, p[0] ^ ((i + 1) % parts))),
        ],
        [pl.BlockSpec((rows + 16, columns), lambda i, p: (0, 0))] * (parts - 1)
        + [
            pl.BlockSpec((rows, columns), lambda i, p: (0, 0)),
            pl.BlockSpec((8, rows), lambda i, p: (0, 0)),
        ],
        (parts,),
        [pltpu.VMEM((rows, width), jnp.bfloat16)],
        2 * rows * width * weights.shape[1],
        2 * width * weights.shape[1],
    )


def pair_projection_kernel(place, x_ref, gain_ref, k_ref, v_ref, *refs):
    *outs, scaled, product = refs
    rows = x_ref.shape[0]
    share = rows // len(outs)
    step = pl.program_id(0)

    @pl.when(step == 0)
    def _():
        scaled[...] = (x_ref[...].astype(jnp.float32) * gain_ref[...]).astype(jnp.bfloat16)

    for half, w_ref in enumerate((k_ref, v_ref)):
        product[...] = jnp.dot(scaled[...], w_ref[...], preferred_element_type=jnp.float32)
        for mask, ref in enumerate(outs):
            first = pl.multiple_of((place[0] ^ mask) * share, share)
            ref[half] = product[pl.ds(first, share), :].astype(ref.dtype)


def pair_projection(place, x, gain, key_weights, value_weights, parts):
    rows, width = x.shape
    columns = key_weights.shape[1]
    block = columns // 2
    share = rows // parts
    return call(
        pair_projection_kernel,
        (place,),
        (x, gain, key_weights, value_weights),
        [shape((2, share, columns), jnp.float32)]
        + [shape((2, share, columns), jnp.bfloat16)] * (parts - 1),
        [
            pl.BlockSpec((rows, width), lambda i, p: (0, 0)),
            pl.BlockSpec((1, width), lambda i, p: (0, 0)),
            pl.BlockSpec((width, block), lambda i, p: (0, i)),
            pl.BlockSpec((width, block), lambda i, p: (0, i)),
        ],
        [pl.BlockSpec((2, share, block), lambda i, p: (0, 0, i))] * parts,
        (2,),
        [pltpu.VMEM((rows, width), jnp.bfloat16), pltpu.VMEM((rows, block), jnp.float32)],
        4 * rows * width * columns,
        4 * width * columns,
    )


def query_rope_kernel(parts, place, own_ref, *refs):
    received, (squares_ref, cos_ref, sin_ref, query_ref, *rest) = refs[: parts - 1], refs[parts - 1 :]
    *suffix_refs, inverse_ref, held = rest
    rows, columns = own_ref.shape
    squares = squares_ref[0:1, :]
    total = own_ref[...]
    for ref in received:
        squares = squares + joined_row(ref[rows:, :rows], 0)
        total = total + ref[:rows, :].astype(jnp.float32)
    inverse = lax.rsqrt(down_rows(squares) / MODEL_WIDTH + EPSILON)
    inverse_ref[...] = inverse
    scale = (MODEL_WIDTH // QUERY_HEADS) ** (-0.5)
    cosine = cos_ref[...] * inverse * scale
    sine = sin_ref[...] * inverse * scale
    pair = 2 * HEAD_SIZE
    for head in range(columns // pair):
        tiles = []
        for member in range(2):
            at = head * pair + member * HEAD_SIZE
            turned = rotated(total[:, at : at + HEAD_SIZE], cosine, sine)
            tiles.append(turned.reshape(rows // 8, 8, HEAD_SIZE))
        even, odd = interleave(*tiles)
        held[head * 2 * rows : (head + 1) * 2 * rows, :] = jnp.stack([even, odd], axis=1).reshape(
            2 * rows, HEAD_SIZE
        )
    query_ref[...] = held[...].astype(jnp.bfloat16)
    share = 2 * rows // parts
    for mask, ref in enumerate(suffix_refs):
        for head in range(columns // pair):
            first = pl.multiple_of(head * 2 * rows + (place[0] ^ mask) * share, share)
            ref[head * share : (head + 1) * share, :] = held[pl.ds(first, share), :].astype(
                jnp.bfloat16
            )


def query_rope(place, own, received, squares, cosine, sine, parts):
    rows, columns = own.shape
    count = rows * columns // HEAD_SIZE
    operands = (own, *received, squares, cosine, sine)
    outs = (
        [shape((count, HEAD_SIZE), jnp.bfloat16)]
        + [shape((count // parts, HEAD_SIZE), jnp.bfloat16)] * parts
        + [shape((rows, LANES), jnp.float32)]
    )
    return call(
        functools.partial(query_rope_kernel, parts),
        (place,),
        operands,
        outs,
        [whole(a) for a in operands],
        [whole(a) for a in outs],
        (1,),
        [pltpu.VMEM((count, HEAD_SIZE), jnp.float32)],
        10 * rows * columns,
        12 * rows * columns,
    )


def prompt_kernel(parts, packed, place, q_ref, *refs):
    keys, values, outs = refs[:parts], refs[parts : 2 * parts], refs[2 * parts :]
    tokens, columns = keys[0].shape
    heads = columns // HEAD_SIZE
    count = q_ref.shape[0] // heads
    ones = jnp.ones((tokens, LANES), jnp.bfloat16)
    for head in range(heads):
        at = slice(head * HEAD_SIZE, (head + 1) * HEAD_SIZE)
        rows = slice(head * count, (head + 1) * count)
        query = q_ref[rows, :]
        total = None
        for k_ref, v_ref in zip(keys, values):
            weight = capped_weight(dot_last(query, k_ref[:, at])).astype(jnp.bfloat16)
            term = jnp.dot(
                weight,
                jnp.concatenate([v_ref[:, at], ones], axis=1),
                preferred_element_type=jnp.float32,
            )
            total = term if total is None else total + term
        outs[0][rows, :] = total[:, :HEAD_SIZE].astype(outs[0].dtype)
        weight_sum = total[:, HEAD_SIZE:]
        if packed:
            held = outs[1]
            for block in range(count // LANES):
                held[head * (count // LANES) + block, :] = weight_sum[
                    block * LANES : (block + 1) * LANES
                ].T[0]
        else:
            outs[1][rows, :] = weight_sum
    if packed:
        outs[0][heads * count :, :] = split_rows(outs[1][...])


def prompt_attention(place, queries, prompt_keys, keys, prompt_values, values, packed):
    parts = len(keys) + 1
    tokens, columns = keys[0].shape
    count = queries.shape[0]
    chosen = pl.BlockSpec((tokens, columns), lambda i, p: (0, p[0]))
    if packed:
        outs = shape((count + 16, HEAD_SIZE), jnp.bfloat16)
        out_specs = whole(outs)
        scratch = [pltpu.VMEM((8, LANES), jnp.float32)]
    else:
        outs = [shape((count, HEAD_SIZE), jnp.float32)] * 2
        out_specs = [whole(a) for a in outs]
        scratch = []
    return call(
        functools.partial(prompt_kernel, parts, packed),
        (place,),
        (queries, prompt_keys, *keys, prompt_values, *values),
        outs,
        [whole(queries), chosen]
        + [whole(a) for a in keys]
        + [chosen]
        + [whole(a) for a in values],
        out_specs,
        (1,),
        scratch,
        4 * count * parts * tokens * HEAD_SIZE,
        4 * parts * tokens * columns,
    )


def suffix_kernel(parts, place, lengths, *refs):
    queries, refs = refs[:parts], refs[parts:]
    latest, refs = refs[:parts], refs[parts:]
    (k_ref, v_ref, inverse_ref, cos_ref, sin_ref), refs = refs[:5], refs[5:]
    outs, refs = refs[: parts + 1], refs[parts + 1 :]
    query_held, spread, new_keys, new_values, result, sums, totals, packed = refs
    member = pl.program_id(0)
    members = pl.num_programs(0)
    slots, columns = k_ref.shape[1:]
    heads = columns // HEAD_SIZE
    near = heads // parts
    share = latest[0].shape[1]
    here = place[0]

    @pl.when(member == 0)
    def _():
        spread[...] = jnp.zeros(spread.shape, jnp.float32)
        packed[...] = jnp.zeros(packed.shape, jnp.float32)
        for mask in range(parts):
            query_held[mask] = queries[mask][...].astype(jnp.float32)
        rows = pl.ds(pl.multiple_of(here * share, share), share)
        inverse = inverse_ref[rows, :]
        cosine = cos_ref[rows, :] * inverse
        sine = sin_ref[rows, :] * inverse
        for head in range(heads):
            at = slice(head * HEAD_SIZE, (head + 1) * HEAD_SIZE)
            key = latest[0][0, :, at]
            value = latest[0][1, :, at]
            for ref in latest[1:]:
                key = key + ref[0, :, at].astype(jnp.float32)
                value = value + ref[1, :, at].astype(jnp.float32)
            new_keys[:, at] = rotated(key, cosine, sine)
            new_values[:, at] = value * inverse

    def places(mask, head):
        owner = here ^ mask
        row = pl.ds(pl.multiple_of((owner * near + head) * 8, 8), 8)
        column = pl.ds(pl.multiple_of((owner * near + head) * HEAD_SIZE, HEAD_SIZE), HEAD_SIZE)
        local = pl.ds(pl.multiple_of(head * members * 8 + member * 8, 8), 8)
        return row, column, local

    for mask in range(parts):
        for head in range(near):
            row, column, local = places(mask, head)
            spread[row, column] = query_held[mask, local, :]
    query = spread[...].astype(jnp.bfloat16)
    weight = capped_weight(dot_last(k_ref[0], query))
    valid = lax.broadcasted_iota(jnp.int32, weight.shape, 0) < lengths[here * members + member]
    weight = jnp.where(valid, weight, 0.0).astype(jnp.bfloat16)
    tile = pl.ds(pl.multiple_of((member // 2) * 8, 8), 8)
    new_weight = capped_weight(dot_last(new_keys[tile, :].astype(jnp.bfloat16), query))
    slot = lax.broadcasted_iota(jnp.int32, new_weight.shape, 0)
    decode_step = lax.broadcasted_iota(jnp.int32, new_weight.shape, 1) % 4
    valid = (slot // 4 == member % 2) & (slot % 4 <= decode_step)
    new_weight = jnp.where(valid, new_weight, 0.0).astype(jnp.bfloat16)
    result[:, :columns] = dot_first(weight, v_ref[0]) + dot_first(
        new_weight, new_values[tile, :].astype(jnp.bfloat16)
    )
    result[:, columns:] = dot_first(weight, jnp.ones((slots, LANES), jnp.bfloat16)) + dot_first(
        new_weight, jnp.ones((8, LANES), jnp.bfloat16)
    )
    for mask in range(parts):
        for head in range(near):
            row, column, local = places(mask, head)
            sums[mask, local, :] = result[row, column]
            totals[mask, local, :] = result[row, columns:]

    @pl.when(member == members - 1)
    def _():
        count = sums.shape[1]
        outs[0][...] = sums[0]
        outs[1][...] = totals[0]
        for mask in range(1, parts):
            ref = outs[mask + 1]
            ref[:count, :] = sums[mask].astype(jnp.bfloat16)
            packed[0, :] = totals[mask].T[0]
            ref[count:, :] = split_rows(packed[...])


def suffix_attention(
    place, lengths, queries, latest, cache_keys, cache_values, inverse, cosine, sine
):
    parts = len(queries)
    members, slots, columns = cache_keys.shape
    count = queries[0].shape[0]
    share = latest[0].shape[1]
    spread_rows = 8 * columns // HEAD_SIZE
    operands = (*queries, *latest, cache_keys, cache_values, inverse, cosine, sine)
    outs = [shape((count, HEAD_SIZE), jnp.float32)] * 2 + [
        shape((count + 16, HEAD_SIZE), jnp.bfloat16)
    ] * (parts - 1)
    cache = pl.BlockSpec((1, slots, columns), lambda i, p, n: (i, 0, 0))
    return call(
        functools.partial(suffix_kernel, parts),
        (place, lengths),
        operands,
        outs,
        [whole(a) for a in queries]
        + [whole(a) for a in latest]
        + [cache, cache, whole(inverse), whole(cosine), whole(sine)],
        [whole(a) for a in outs],
        (members,),
        [
            pltpu.VMEM((parts, count, HEAD_SIZE), jnp.float32),
            pltpu.VMEM((spread_rows, columns), jnp.float32),
            pltpu.VMEM((share, columns), jnp.float32),
            pltpu.VMEM((share, columns), jnp.float32),
            pltpu.VMEM((spread_rows, columns + LANES), jnp.float32),
            pltpu.VMEM((parts, count, HEAD_SIZE), jnp.float32),
            pltpu.VMEM((parts, count, HEAD_SIZE), jnp.float32),
            pltpu.VMEM((8, LANES), jnp.float32),
        ],
        4 * members * spread_rows * slots * columns,
        4 * members * slots * columns,
    )


def mix_kernel(parts, far, place, sum_ref, total_ref, *refs):
    prompt, refs = refs[:far], refs[far:]
    near_sum, near_total, *suffix = refs[: parts + 1]
    out_ref, sums, totals = refs[parts + 1 :]
    count = sum_ref.shape[0]
    rows = out_ref.shape[0]
    heads = count // (2 * rows)
    total = sum_ref[...]
    for ref in prompt:
        total = total + ref[:count, :].astype(jnp.float32)
    sums[...] = total
    for block in range(count // LANES):
        at = slice(block * LANES, (block + 1) * LANES)
        total = total_ref[at, :]
        for ref in prompt:
            total = total + down_rows(joined_row(ref[count:, :], block))
        totals[at, :] = total
    share = 2 * rows // parts
    for mask in range(parts):
        if mask == 0:
            near, near_weight = near_sum[...], near_total[...]
        else:
            ref = suffix[mask - 1]
            near = ref[: count // parts, :].astype(jnp.float32)
            near_weight = down_rows(joined_row(ref[count // parts :, :], 0))
        for head in range(heads):
            first = pl.multiple_of(head * 2 * rows + (place[0] ^ mask) * share, share)
            at = pl.ds(first, share)
            local = slice(head * share, (head + 1) * share)
            sums[at, :] = sums[at, :] + near[local]
            totals[at, :] = totals[at, :] + near_weight[local]
    mixed = sums[...] / totals[...]
    for head in range(heads):
        tiles = mixed[head * 2 * rows : (head + 1) * 2 * rows].reshape(rows // 8, 2, 8, HEAD_SIZE)
        for member, part in enumerate(interleave(tiles[:, 0], tiles[:, 1])):
            at = (2 * head + member) * HEAD_SIZE
            out_ref[:, at : at + HEAD_SIZE] = part.reshape(rows, HEAD_SIZE).astype(jnp.bfloat16)


def mix(place, sums, totals, prompt, suffix, rows):
    count = sums.shape[0]
    operands = (sums, totals, *prompt, *suffix)
    out = shape((rows, count // rows * HEAD_SIZE), jnp.bfloat16)
    return call(
        functools.partial(mix_kernel, len(suffix) - 1, len(prompt)),
        (place,),
        operands,
        out,
        [whole(a) for a in operands],
        whole(out),
        (1,),
        [pltpu.VMEM((count, HEAD_SIZE), jnp.float32)] * 2,
        10 * count * HEAD_SIZE,
        8 * count * HEAD_SIZE,
    )


def output_kernel(masks, started, place, *refs):
    inputs, refs = refs[: len(masks)], refs[len(masks) :]
    w_ref, out_ref = refs[0], refs[-1]
    step = pl.program_id(0)
    for index, ref in enumerate(inputs):

        @pl.when(step == index)
        def _():
            term = jnp.dot(ref[...], w_ref[...], preferred_element_type=jnp.float32)
            if index > 0:
                out_ref[...] += term
            elif started:
                out_ref[...] = refs[1][...] + term
            else:
                out_ref[...] = term


def output_projection(place, masks, mixed, weights, started=None):
    rows, depth = mixed[0].shape
    width = weights.shape[1]
    chosen = pl.BlockSpec(
        (depth, width), lambda i, p: (p[0] ^ (i + masks[0]), 0)
    )
    out = shape((rows, width), jnp.float32)
    more = () if started is None else (started,)
    return call(
        functools.partial(output_kernel, masks, started is not None),
        (place,),
        (*mixed, weights, *more),
        out,
        [whole(a) for a in mixed] + [chosen] + [whole(a) for a in more],
        whole(out),
        (len(masks),),
        [],
        2 * len(masks) * rows * depth * width,
        2 * len(masks) * depth * width,
    )


def attended_kernel(place, here_ref, there_ref, out_ref, squares_ref):
    attended = here_ref[...] + there_ref[...]
    out_ref[...] = attended
    total = jnp.sum(attended * attended, axis=1, keepdims=True)
    squares_ref[...] = jnp.broadcast_to(total, (total.shape[0], LANES)).T[:8]


def attended_squares(place, here, there):
    outs = [shape(here.shape, jnp.float32), shape((8, here.shape[0]), jnp.float32)]
    return call(
        attended_kernel,
        (place,),
        (here, there),
        outs,
        [whole(here), whole(there)],
        [whole(a) for a in outs],
        (1,),
        [],
        4 * here.size,
        12 * here.size,
    )


def finish_kernel(place, x_ref, attended_ref, gain_ref, *refs):
    *squares, out_ref = refs
    total = squares[0][0:1, :]
    for ref in squares[1:]:
        total = total + ref[0:1, :]
    inverse = lax.rsqrt(down_rows(total) / MODEL_WIDTH + EPSILON)
    for at in range(0, x_ref.shape[1], LANES):
        lanes = slice(at, at + LANES)
        branch = attended_ref[:, lanes] * inverse * gain_ref[:, lanes]
        out_ref[:, lanes] = (x_ref[:, lanes].astype(jnp.float32) + branch).astype(jnp.bfloat16)


def finish(place, x, attended, gain, squares):
    operands = (x, attended, gain, *squares)
    out = shape(x.shape, jnp.bfloat16)
    return call(
        finish_kernel,
        (place,),
        operands,
        out,
        [whole(a) for a in operands],
        whole(out),
        (1,),
        [],
        4 * x.size,
        8 * x.size,
    )


def by_heads(
    hidden_in,
    pre_gain,
    w_query,
    key_projection,
    value_projection,
    w_out,
    post_gain,
    prompt_keys,
    prompt_values,
    suffix_key_cache,
    suffix_value_cache,
    suffix_len,
):
    group_rows, steps, local_width = hidden_in.shape
    rows = group_rows * steps
    parts = lax.axis_size("prefix")
    groups = lax.axis_size("prefill")
    prompt_total = prompt_keys.shape[0] * groups * parts
    here = lax.axis_index("prefix")
    place = here.astype(jnp.int32).reshape(1)
    x = hidden_in.reshape(rows, local_width)
    gain = pre_gain.reshape(1, local_width)
    near = range(1, parts)
    far = range(1, groups)

    *sent, own, squares = query_projection(place, x, gain, w_query, parts)
    received = [paired(a, "prefix", m) for m, a in zip(near, sent)]

    columns = prompt_keys.shape[1] // parts

    def spread(cache):
        return [
            paired(
                lax.dynamic_slice_in_dim(cache, (here ^ m) * columns, columns, axis=1), "prefix", m
            )
            for m in near
        ]

    keys = spread(prompt_keys)
    values = spread(prompt_values)

    positions = (
        (prompt_total + suffix_len[:, None] + jnp.arange(steps, dtype=jnp.int32)[None, :])
        .reshape(-1)
        .astype(jnp.float32)
    )
    half = HEAD_SIZE // 2
    freq = 10000.0 ** (-2.0 * jnp.arange(half, dtype=jnp.float32) / HEAD_SIZE)
    angle = positions[:, None] * freq[None, :]
    cosine, sine = jnp.cos(angle), jnp.sin(angle)
    cosine = jnp.concatenate([cosine, cosine], axis=1)
    sine = jnp.concatenate([-sine, sine], axis=1)

    own_pair, *sent = pair_projection(place, x, gain, key_projection, value_projection, parts)
    latest = [own_pair] + [paired(a, "prefix", m) for m, a in zip(near, sent)]

    queries, *split_queries, inverse = query_rope(
        place, own, received, squares, cosine, sine, parts
    )
    far_queries = [paired(queries, "prefill", m) for m in far]
    suffix_queries = [split_queries[0]] + [
        paired(a, "prefix", m) for m, a in zip(near, split_queries[1:])
    ]

    def prompt(chunk, packed):
        return prompt_attention(place, chunk, prompt_keys, keys, prompt_values, values, packed)

    sums, totals = prompt(queries, False)
    prompt_results = [paired(prompt(q, True), "prefill", m) for m, q in zip(far, far_queries)]
    near_sums, near_totals, *sent = suffix_attention(
        place,
        suffix_len,
        suffix_queries,
        latest,
        suffix_key_cache,
        suffix_value_cache,
        inverse,
        cosine,
        sine,
    )
    suffix = [near_sums, near_totals] + [paired(a, "prefix", m) for m, a in zip(near, sent)]
    mixed = mix(place, sums, totals, prompt_results, suffix, rows)
    others = [paired(mixed, "prefix", m) for m in near]
    head_terms = output_projection(place, (0,), [mixed], w_out)
    head_terms = output_projection(place, tuple(near), others, w_out, head_terms)
    attended, squares = attended_squares(place, head_terms, paired(head_terms, "tensor", 1))
    squares = [squares] + [paired(squares, "prefix", m) for m in near]
    out = finish(place, x, attended, post_gain.reshape(1, local_width), squares)
    return out.reshape(group_rows, steps, local_width)


def heads_divide(mesh):
    sizes = [mesh.shape[name] for name in ("prefill", "prefix", "tensor")]
    key_heads = QUERY_HEADS // 2 // sizes[2]
    return key_heads % sizes[1] == 0 and sizes[1] == 4 and sizes[2] == 2 and sizes[0] in (2, 4)


def solution(mesh):
    return jax.shard_map(
        by_heads if heads_divide(mesh) else per_device,
        mesh=mesh,
        in_specs=(
            P("prefill", None, "prefix"),
            P("prefix"),
            P("prefix", "tensor"),
            P("prefix", "tensor"),
            P("prefix", "tensor"),
            P("tensor", "prefix"),
            P("prefix"),
            P(("prefill", "prefix"), "tensor"),
            P(("prefill", "prefix"), "tensor"),
            P(("prefill", "prefix"), None, "tensor"),
            P(("prefill", "prefix"), None, "tensor"),
            P("prefill"),
        ),
        out_specs=P("prefill", None, "prefix"),
        check_vma=False,
    )
```

```python
import functools

import jax
import jax.numpy as jnp
from jax import lax
from jax.experimental import pallas as pl
from jax.experimental.pallas import tpu as pltpu
from jax.sharding import PartitionSpec as P

MODEL_WIDTH = 4608
QUERY_HEADS = 32
HEAD_SIZE = 128


SOFTCAP = 50.0
EPSILON = 1e-06
LOG2_E = 1.4426950408889634
LANES = 128
VMEM_LIMIT = 32 * 1024 * 1024
LARGE_VMEM_LIMIT = 60 * 1024 * 1024


def apply_rotation(values, token_positions, heads):
    width = values.shape[1] // heads
    half = width // 2
    freq = 10000.0 ** (-2.0 * jnp.arange(half, dtype=jnp.float32) / width)
    angle = token_positions[:, None] * freq[None, :]
    cosine = jnp.cos(angle)[:, None, :]
    sine = jnp.sin(angle)[:, None, :]
    parts = values.reshape(values.shape[0], heads, width)
    first = parts[:, :, :half]
    second = parts[:, :, half:]
    turned = jnp.concatenate(
        [first * cosine - second * sine, second * cosine + first * sine], axis=2
    )
    return turned.reshape(values.shape[0], heads * width)


def soft_weight(scores):
    return jnp.exp(SOFTCAP * jnp.tanh(scores / SOFTCAP))


def shared_attention(queries, keys, values):
    count = queries.shape[0]
    kv_heads = keys.shape[1] // HEAD_SIZE
    heads_per_group = queries.shape[1] // keys.shape[1]
    grouped = queries.reshape(count, kv_heads, heads_per_group, HEAD_SIZE)
    key_head_rows = keys.reshape(keys.shape[0], kv_heads, HEAD_SIZE)
    value_head_rows = values.reshape(values.shape[0], kv_heads, HEAD_SIZE)
    scores = jnp.einsum(
        "nkgd,mkd->nkgm", grouped, key_head_rows, preferred_element_type=jnp.float32
    )
    weights = soft_weight(scores)
    totals = jnp.sum(weights, axis=3).reshape(count, kv_heads * heads_per_group)
    summed = jnp.einsum(
        "nkgm,mkd->nkgd",
        weights.astype(jnp.bfloat16),
        value_head_rows,
        preferred_element_type=jnp.float32,
    )
    return (summed.reshape(count, kv_heads * heads_per_group * HEAD_SIZE), totals)


def own_attention(
    queries, cached_key_rows, cached_value_rows, latest_keys, latest_values, lengths, steps
):
    members = lengths.shape[0]
    slots = cached_key_rows.shape[1]
    kv_heads = cached_key_rows.shape[2] // HEAD_SIZE
    heads_per_group = queries.shape[1] // cached_key_rows.shape[2]
    grouped = queries.reshape(members, steps, kv_heads, heads_per_group, HEAD_SIZE)
    cache_k = cached_key_rows.reshape(members, slots, kv_heads, HEAD_SIZE)
    cache_v = cached_value_rows.reshape(members, slots, kv_heads, HEAD_SIZE)
    valid = jnp.arange(slots, dtype=jnp.int32)[None, :] < lengths[:, None]
    cache_scores = jnp.einsum(
        "rjkgd,rmkd->rjkgm", grouped, cache_k, preferred_element_type=jnp.float32
    )
    cache_weights = jnp.where(valid[:, None, None, None, :], soft_weight(cache_scores), 0.0)
    new_k = latest_keys.reshape(members, steps, kv_heads, HEAD_SIZE)
    new_v = latest_values.reshape(members, steps, kv_heads, HEAD_SIZE)
    step_ids = jnp.arange(steps, dtype=jnp.int32)
    causal = step_ids[None, :] <= step_ids[:, None]
    new_scores = jnp.einsum("rjkgd,rikd->rjkgi", grouped, new_k, preferred_element_type=jnp.float32)
    new_weights = jnp.where(causal[None, :, None, None, :], soft_weight(new_scores), 0.0)
    totals = jnp.sum(cache_weights, axis=4) + jnp.sum(new_weights, axis=4)
    summed = jnp.einsum(
        "rjkgm,rmkd->rjkgd",
        cache_weights.astype(jnp.bfloat16),
        cache_v,
        preferred_element_type=jnp.float32,
    )
    summed = summed + jnp.einsum(
        "rjkgi,rikd->rjkgd",
        new_weights.astype(jnp.bfloat16),
        new_v,
        preferred_element_type=jnp.float32,
    )
    flat_rows = members * steps
    return (
        summed.reshape(flat_rows, kv_heads * heads_per_group * HEAD_SIZE),
        totals.reshape(flat_rows, kv_heads * heads_per_group),
    )


def per_device(
    hidden_in,
    pre_gain,
    w_query,
    key_projection,
    value_projection,
    w_out,
    post_gain,
    prompt_keys,
    prompt_values,
    suffix_key_cache,
    suffix_value_cache,
    suffix_len,
):
    group_rows, steps, local_width = hidden_in.shape
    members = suffix_key_cache.shape[0]
    query_cols = w_query.shape[1]
    kv_cols = key_projection.shape[1]
    heads = query_cols // HEAD_SIZE
    kv_heads = kv_cols // HEAD_SIZE
    own_count = members * steps
    prompt_total = prompt_keys.shape[0] * lax.axis_size("prefill") * lax.axis_size("prefix")
    signal = hidden_in.astype(jnp.float32).reshape(group_rows * steps, local_width)
    squares = lax.psum(jnp.sum(signal * signal, axis=1), "prefix")
    normed = (signal * lax.rsqrt(squares[:, None] / MODEL_WIDTH + EPSILON) * pre_gain).astype(
        jnp.bfloat16
    )
    weights_all = jnp.concatenate([w_query, key_projection, value_projection], axis=1)
    step_ids = jnp.arange(steps, dtype=jnp.int32)
    group_positions = (
        (prompt_total + suffix_len[:, None] + step_ids[None, :]).reshape(-1).astype(jnp.float32)
    )
    first_row = lax.axis_index("prefix") * members
    own_lengths = lax.dynamic_slice_in_dim(suffix_len, first_row, members)
    own_positions = lax.dynamic_slice_in_dim(group_positions, first_row * steps, own_count)
    scale = (MODEL_WIDTH // QUERY_HEADS) ** (-0.5)
    own_proj = lax.psum_scatter(
        jnp.dot(normed, weights_all, preferred_element_type=jnp.float32),
        "prefix",
        scatter_dimension=0,
        tiled=True,
    )
    own_queries = (apply_rotation(own_proj[:, :query_cols], own_positions, heads) * scale).astype(
        jnp.bfloat16
    )
    group_queries = lax.all_gather(own_queries, "prefix", axis=0, tiled=True)
    latest_keys = apply_rotation(
        own_proj[:, query_cols : query_cols + kv_cols], own_positions, kv_heads
    ).astype(jnp.bfloat16)
    latest_values = own_proj[:, query_cols + kv_cols :].astype(jnp.bfloat16)
    summed, totals = shared_attention(
        group_queries,
        lax.all_gather(prompt_keys, "prefill", axis=0, tiled=True),
        lax.all_gather(prompt_values, "prefill", axis=0, tiled=True),
    )
    prompt_totals = totals
    far_sums, far_totals = (
        lax.psum_scatter(summed, "prefix", scatter_dimension=0, tiled=True),
        lax.psum_scatter(prompt_totals, "prefix", scatter_dimension=0, tiled=True),
    )
    near_sums, near_totals = own_attention(
        own_queries,
        suffix_key_cache,
        suffix_value_cache,
        latest_keys,
        latest_values,
        own_lengths,
        steps,
    )
    totals = far_totals + near_totals
    sums = (far_sums + near_sums).reshape(own_count, heads, HEAD_SIZE)
    mixed = (sums / totals[:, :, None]).reshape(own_count, query_cols).astype(jnp.bfloat16)
    head_terms = jnp.dot(
        lax.all_gather(mixed, "prefix", axis=0, tiled=True),
        w_out,
        preferred_element_type=jnp.float32,
    )
    attended = lax.psum(head_terms, "tensor")
    out_squares = lax.psum(jnp.sum(attended * attended, axis=1), "prefix")
    branch = attended * lax.rsqrt(out_squares[:, None] / MODEL_WIDTH + EPSILON) * post_gain
    return (signal + branch).astype(jnp.bfloat16).reshape(group_rows, steps, local_width)


def paired(values, axis, mask):
    size = lax.axis_size(axis)
    return lax.ppermute(values, axis, [(i, i ^ mask) for i in range(size)])


def call(
    kernel,
    prefetch,
    operands,
    out_shape,
    in_specs,
    out_specs,
    grid,
    scratch,
    flops,
    moved,
    limit=VMEM_LIMIT,
):
    return pl.pallas_call(
        kernel,
        out_shape=out_shape,
        grid_spec=pltpu.PrefetchScalarGridSpec(
            num_scalar_prefetch=len(prefetch),
            grid=grid,
            in_specs=in_specs,
            out_specs=out_specs,
            scratch_shapes=scratch,
        ),
        compiler_params=pltpu.CompilerParams(vmem_limit_bytes=limit),
        cost_estimate=pl.CostEstimate(flops=flops, bytes_accessed=moved, transcendentals=0),
    )(*prefetch, *operands)


def whole(array):
    rank = len(array.shape)
    return pl.BlockSpec(array.shape, lambda *_: (0,) * rank)


def corner(array):
    rank = len(array.shape)
    return pl.BlockSpec(
        (1,) * (rank - 2) + (32 // array.dtype.itemsize, LANES), lambda *_: (0,) * rank
    )


def shape(dims, dtype):
    return jax.ShapeDtypeStruct(dims, dtype)


def dot_last(left, right):
    return lax.dot_general(left, right, (((1,), (1,)), ((), ())), preferred_element_type=jnp.float32)


def dot_first(left, right):
    return lax.dot_general(left, right, (((0,), (0,)), ((), ())), preferred_element_type=jnp.float32)


def capped_weight(scores):
    return jnp.exp2(jnp.tanh(scores * (1.0 / SOFTCAP)) * (SOFTCAP * LOG2_E))


def split_rows(rows):
    high = rows.astype(jnp.bfloat16).astype(jnp.float32)
    return jnp.concatenate([high, rows - high], axis=0).astype(jnp.bfloat16)


def joined_row(block, index):
    pair = block.astype(jnp.float32)
    return pair[index : index + 1] + pair[8 + index : 9 + index]


def down_rows(row):
    return jnp.broadcast_to(row, (LANES, row.shape[1])).T


def lower_half(tiles):
    return lax.broadcasted_iota(jnp.int32, tiles.shape, 1) < tiles.shape[1] // 2


def interleave(first, second):
    low = lower_half(first)
    half = first.shape[1] // 2
    return (
        jnp.where(low, first, pltpu.roll(second, half, 1)),
        jnp.where(low, pltpu.roll(first, half, 1), second),
    )


def rotated(values, cosine, sine):
    return values * cosine + pltpu.roll(values, HEAD_SIZE // 2, 1) * sine


def flat_rows(ref):
    members, steps, width = ref.shape
    return ref[...].astype(jnp.float32).reshape(members * steps, width)


def gain_row(ref):
    return ref[...].reshape(1, ref.shape[0])


def query_projection_kernel(place, x_ref, gain_ref, w_ref, *refs):
    *sent, own_ref, squares_ref, scaled_ref = refs
    step = pl.program_id(0)
    rows = scaled_ref.shape[0]

    @pl.when(step == 0)
    def _():
        x = flat_rows(x_ref)
        scaled_ref[...] = (x * gain_row(gain_ref)).astype(jnp.bfloat16)
        total = jnp.sum(x * x, axis=1, keepdims=True)
        across = jnp.broadcast_to(total, (rows, LANES)).T[:8]
        squares_ref[...] = across
        tail = split_rows(across)
        for ref in sent:
            ref[rows:, :] = jnp.zeros((16, ref.shape[1]), jnp.bfloat16)
            ref[rows:, :rows] = tail

    product = jnp.dot(scaled_ref[...], w_ref[...], preferred_element_type=jnp.float32)
    for index, ref in enumerate(sent):

        @pl.when(step == index)
        def _():
            ref[:rows, :] = product.astype(jnp.bfloat16)

    @pl.when(step == len(sent))
    def _():
        own_ref[...] = product


def query_projection(place, x, gain, weights, parts):
    members, steps, width = x.shape
    rows = members * steps
    columns = weights.shape[1] // parts
    outs = [shape((rows + 16, columns), jnp.bfloat16)] * (parts - 1) + [
        shape((rows, columns), jnp.float32),
        shape((8, rows), jnp.float32),
        shape((rows, width), jnp.bfloat16),
    ]
    return call(
        query_projection_kernel,
        (place,),
        (x, gain, weights),
        outs,
        [
            whole(x),
            whole(gain),
            pl.BlockSpec((width, columns), lambda i, p: (0, p[0] ^ ((i + 1) % parts))),
        ],
        [whole(a) for a in outs],
        (parts,),
        [],
        2 * rows * width * weights.shape[1],
        2 * width * weights.shape[1],
        LARGE_VMEM_LIMIT,
    )


def cache_columns_kernel(place, k_ref, v_ref, token_ref, *outs):
    step = pl.program_id(0)
    width = k_ref.shape[1]
    for index, ref in enumerate(outs):

        @pl.when(step == index)
        def _():
            ref[:, :width] = k_ref[...]
            ref[:, width:] = v_ref[...]


def cache_columns(place, keys, values, head, heads, parts, token):
    tokens = keys.shape[0]
    chosen = pl.BlockSpec(
        (tokens, HEAD_SIZE), lambda i, p: (0, (p[0] ^ (i + 1)) * heads + head)
    )
    outs = [shape((tokens, 2 * HEAD_SIZE), jnp.bfloat16)] * (parts - 1)
    return call(
        cache_columns_kernel,
        (place,),
        (keys, values, token),
        outs,
        [chosen, chosen, corner(token)],
        [whole(a) for a in outs],
        (parts - 1,),
        [],
        0,
        8 * (parts - 1) * tokens * HEAD_SIZE,
    )


def pair_projection_kernel(place, scaled_ref, k_ref, v_ref, *refs):
    parts = len(refs) // 2 + 1
    queries, (own_ref, *outs) = refs[: parts - 1], refs[parts - 1 :]
    rows = scaled_ref.shape[0]
    columns = k_ref.shape[1]
    step = pl.program_id(0)
    terms = [
        jnp.dot(scaled_ref[...], w_ref[...], preferred_element_type=jnp.float32)
        for w_ref in (k_ref, v_ref)
    ]

    def store(ref):
        for index, term in enumerate(terms):
            ref[:rows, index * columns : (index + 1) * columns] = term.astype(ref.dtype)

    for index, (query_ref, ref) in enumerate(zip(queries, outs)):

        @pl.when(step == index)
        def _():
            store(ref)
            tall = ref.shape[0] - rows
            for piece in range(query_ref.shape[0] // tall):
                at = slice(piece * HEAD_SIZE, (piece + 1) * HEAD_SIZE)
                ref[rows:, at] = query_ref[piece * tall : (piece + 1) * tall, :]

    @pl.when(step == parts - 1)
    def _():
        store(own_ref)


def pair_projection(place, scaled, key_weights, value_weights, queries):
    parts = len(queries) + 1
    rows, width = scaled.shape
    columns = key_weights.shape[1] // parts
    tall = queries[0].shape[0] * HEAD_SIZE // (2 * columns)
    chosen = pl.BlockSpec((width, columns), lambda i, p: (0, p[0] ^ ((i + 1) % parts)))
    outs = [shape((rows, 2 * columns), jnp.float32)] + [
        shape((rows + tall, 2 * columns), jnp.bfloat16)
    ] * (parts - 1)
    return call(
        pair_projection_kernel,
        (place,),
        (scaled, key_weights, value_weights, *queries),
        outs,
        [whole(scaled), chosen, chosen] + [whole(a) for a in queries],
        [whole(a) for a in outs],
        (parts,),
        [],
        4 * rows * width * key_weights.shape[1],
        4 * width * key_weights.shape[1],
    )


def query_rope_kernel(parts, place, own_ref, *refs):
    received, (squares_ref, cos_ref, sin_ref, query_ref, *rest) = refs[: parts - 1], refs[parts - 1 :]
    *suffix_refs, inverse_ref, held = rest
    rows, columns = own_ref.shape
    squares = squares_ref[0:1, :]
    total = own_ref[...]
    for ref in received:
        squares = squares + joined_row(ref[rows:, :rows], 0)
        total = total + ref[:rows, :].astype(jnp.float32)
    inverse = lax.rsqrt(down_rows(squares) / MODEL_WIDTH + EPSILON)
    inverse_ref[...] = inverse
    scale = (MODEL_WIDTH // QUERY_HEADS) ** (-0.5)
    cosine = cos_ref[...] * inverse * scale
    sine = sin_ref[...] * inverse * scale
    pair = 2 * HEAD_SIZE
    for head in range(columns // pair):
        tiles = []
        for member in range(2):
            at = head * pair + member * HEAD_SIZE
            turned = rotated(total[:, at : at + HEAD_SIZE], cosine, sine)
            tiles.append(turned.reshape(rows // 8, 8, HEAD_SIZE))
        even, odd = interleave(*tiles)
        held[head * 2 * rows : (head + 1) * 2 * rows, :] = jnp.stack([even, odd], axis=1).reshape(
            2 * rows, HEAD_SIZE
        )
    query_ref[...] = held[...].astype(jnp.bfloat16)
    share = 2 * rows // parts
    for mask, ref in enumerate(suffix_refs):
        for head in range(columns // pair):
            first = pl.multiple_of(head * 2 * rows + (place[0] ^ mask) * share, share)
            ref[head * share : (head + 1) * share, :] = held[pl.ds(first, share), :].astype(
                jnp.bfloat16
            )


def query_rope(place, own, received, squares, cosine, sine, parts):
    rows, columns = own.shape
    count = rows * columns // HEAD_SIZE
    operands = (own, *received, squares, cosine, sine)
    outs = (
        [shape((count, HEAD_SIZE), jnp.bfloat16)]
        + [shape((count // parts, HEAD_SIZE), jnp.bfloat16)] * parts
        + [shape((rows, LANES), jnp.float32)]
    )
    return call(
        functools.partial(query_rope_kernel, parts),
        (place,),
        operands,
        outs,
        [whole(a) for a in operands],
        [whole(a) for a in outs],
        (1,),
        [pltpu.VMEM((count, HEAD_SIZE), jnp.float32)],
        10 * rows * columns,
        12 * rows * columns,
    )


def attend(query, pairs):
    result = None
    for key, value in pairs:
        weight = capped_weight(dot_last(query, key)).astype(jnp.bfloat16)
        ones = jnp.ones((value.shape[0], LANES), jnp.bfloat16)
        term = jnp.dot(
            weight, jnp.concatenate([value, ones], axis=1), preferred_element_type=jnp.float32
        )
        result = term if result is None else result + term
    return result


def cached_pairs(k_ref, v_ref, received):
    return [(k_ref[...], v_ref[...])] + [
        (ref[:, :HEAD_SIZE], ref[:, HEAD_SIZE:]) for ref in received
    ]


def total_rows(totals):
    return [
        totals[at : at + LANES].T[0:1] for at in range(0, totals.shape[0], LANES)
    ]


def prompt_first_kernel(chunks, place, *refs):
    queries, refs = refs[:chunks], refs[chunks:]
    k_ref, v_ref, *received = refs[: -2 * chunks]
    outs = refs[-2 * chunks :]
    for index, query_ref in enumerate(queries):
        sum_ref, total_ref = outs[2 * index : 2 * index + 2]
        result = attend(query_ref[...], cached_pairs(k_ref, v_ref, received))
        sum_ref[...] = result[:, :HEAD_SIZE].astype(sum_ref.dtype)
        if index == 0:
            total_ref[...] = result[:, HEAD_SIZE:]
        else:
            total_ref[...] = jnp.zeros(total_ref.shape, jnp.float32)
            for row, values in enumerate(total_rows(result[:, HEAD_SIZE:])):
                total_ref[row : row + 1, :] = values


def prompt_first(place, queries, prompt_keys, prompt_values, received, heads):
    count = queries[0].shape[0] // heads
    tokens = prompt_keys.shape[0]
    chosen = pl.BlockSpec((tokens, HEAD_SIZE), lambda i, p: (0, p[0] * heads))
    outs = [shape((count, HEAD_SIZE), jnp.float32)] * 2 + [
        shape((count, HEAD_SIZE), jnp.bfloat16),
        shape((8, LANES), jnp.float32),
    ] * (len(queries) - 1)
    parts = len(received) + 1
    return call(
        functools.partial(prompt_first_kernel, len(queries)),
        (place,),
        (*queries, prompt_keys, prompt_values, *received),
        outs,
        [pl.BlockSpec((count, HEAD_SIZE), lambda *_: (0, 0))] * len(queries)
        + [chosen, chosen]
        + [whole(a) for a in received],
        [whole(a) for a in outs],
        (1,),
        [],
        6 * len(queries) * count * parts * tokens * HEAD_SIZE,
        4 * parts * tokens * HEAD_SIZE,
    )


def prompt_second_kernel(place, q_ref, k_ref, v_ref, *refs):
    *received, sum_ref, total_ref, token_ref, out_ref, held = refs
    count = q_ref.shape[0]
    result = attend(q_ref[...], cached_pairs(k_ref, v_ref, received))
    out_ref[:count, :] = sum_ref[...]
    out_ref[count : 2 * count, :] = result[:, :HEAD_SIZE].astype(jnp.bfloat16)
    held[...] = total_ref[...]
    for row, values in enumerate(total_rows(result[:, HEAD_SIZE:])):
        at = count // LANES + row
        held[at : at + 1, :] = values
    out_ref[2 * count :, :] = split_rows(held[...])


def prompt_second(place, queries, prompt_keys, prompt_values, received, first, heads, token):
    count = queries.shape[0] // heads
    tokens = prompt_keys.shape[0]
    chosen = pl.BlockSpec((tokens, HEAD_SIZE), lambda i, p: (0, p[0] * heads + 1))
    out = shape((heads * count + 16, HEAD_SIZE), jnp.bfloat16)
    parts = len(received) + 1
    return call(
        prompt_second_kernel,
        (place,),
        (queries, prompt_keys, prompt_values, *received, *first, token),
        out,
        [pl.BlockSpec((count, HEAD_SIZE), lambda *_: (1, 0)), chosen, chosen]
        + [whole(a) for a in (*received, *first)]
        + [corner(token)],
        whole(out),
        (1,),
        [pltpu.VMEM((8, LANES), jnp.float32)],
        6 * count * parts * tokens * HEAD_SIZE,
        4 * parts * tokens * HEAD_SIZE,
    )


def own_kernel(parts, place, q_ref, k_ref, v_ref, *refs):
    received, refs = refs[: parts - 1], refs[parts - 1 :]
    first_sum, first_total, pair_ref, *refs = refs
    terms, refs = refs[: parts - 1], refs[parts - 1 :]
    inverse_ref, cos_ref, sin_ref, *_, sum_ref, total_ref = refs
    count = first_sum.shape[0]
    rows = inverse_ref.shape[0]
    inverse = inverse_ref[...]
    cosine = cos_ref[...] * inverse
    sine = sin_ref[...] * inverse
    pair = pair_ref[...]
    for ref in terms:
        pair = pair + ref[:rows, :].astype(jnp.float32)
    heads = pair.shape[1] // (2 * HEAD_SIZE)
    query_row = lax.broadcasted_iota(jnp.int32, (count, rows), 0)
    key_row = lax.broadcasted_iota(jnp.int32, (count, rows), 1)
    same = query_row // 8 == key_row // 4
    valid = same & (key_row % 4 <= query_row % 4)
    ones = jnp.ones((rows, LANES), jnp.bfloat16)
    for head in range(heads):
        at = slice(head * count, (head + 1) * count)
        query = q_ref[at, :]
        key = rotated(pair[:, head * HEAD_SIZE : (head + 1) * HEAD_SIZE], cosine, sine)
        value_at = (heads + head) * HEAD_SIZE
        value = pair[:, value_at : value_at + HEAD_SIZE] * inverse
        weight = capped_weight(dot_last(query, key.astype(jnp.bfloat16)))
        weight = jnp.where(valid, weight, 0.0).astype(jnp.bfloat16)
        result = jnp.dot(
            weight,
            jnp.concatenate([value.astype(jnp.bfloat16), ones], axis=1),
            preferred_element_type=jnp.float32,
        )
        if head == 0:
            sum_ref[at, :] = first_sum[...] + result[:, :HEAD_SIZE]
            total_ref[at, :] = first_total[...] + result[:, HEAD_SIZE:]
        else:
            result = result + attend(query, cached_pairs(k_ref, v_ref, received))
            sum_ref[at, :] = result[:, :HEAD_SIZE]
            total_ref[at, :] = result[:, HEAD_SIZE:]


def own_attention_sums(
    place, queries, prompt_keys, prompt_values, received, first, pair, terms, tables, tokens_after
):
    count = first[0].shape[0]
    heads = queries.shape[0] // count
    tokens = prompt_keys.shape[0]
    parts = len(received) + 1
    chosen = pl.BlockSpec((tokens, HEAD_SIZE), lambda i, p: (0, p[0] * heads + 1))
    operands = (*received, *first, pair, *terms, *tables)
    outs = [shape(queries.shape, jnp.float32)] * 2
    return call(
        functools.partial(own_kernel, parts),
        (place,),
        (queries, prompt_keys, prompt_values, *operands, *tokens_after),
        outs,
        [whole(queries), chosen, chosen]
        + [whole(a) for a in operands]
        + [corner(a) for a in tokens_after],
        [whole(a) for a in outs],
        (1,),
        [],
        6 * count * parts * tokens * HEAD_SIZE,
        4 * parts * tokens * HEAD_SIZE,
    )


def suffix_kernel(parts, place, lengths, own_ref, *refs):
    received, (k_ref, v_ref, _), refs = refs[: parts - 1], refs[parts - 1 : parts + 2], refs[parts + 2 :]
    outs, (query_held, spread, result, sums, totals, packed) = refs[: parts + 1], refs[parts + 1 :]
    member = pl.program_id(0)
    members = pl.num_programs(0)
    slots, columns = k_ref.shape[1:]
    heads = columns // HEAD_SIZE
    near = heads // parts
    here = place[0]

    @pl.when(member == 0)
    def _():
        spread[...] = jnp.zeros(spread.shape, jnp.float32)
        packed[...] = jnp.zeros(packed.shape, jnp.float32)
        query_held[0] = own_ref[...].astype(jnp.float32)
        count = own_ref.shape[0]
        for mask, ref in enumerate(received, start=1):
            pieces = ref.shape[1] // HEAD_SIZE
            tall = count // pieces
            for piece in range(pieces):
                at = slice(piece * HEAD_SIZE, (piece + 1) * HEAD_SIZE)
                query_held[mask, piece * tall : (piece + 1) * tall, :] = ref[
                    ref.shape[0] - tall :, at
                ].astype(jnp.float32)

    def places(mask, head):
        owner = here ^ mask
        row = pl.ds(pl.multiple_of((owner * near + head) * 8, 8), 8)
        column = pl.ds(pl.multiple_of((owner * near + head) * HEAD_SIZE, HEAD_SIZE), HEAD_SIZE)
        local = pl.ds(pl.multiple_of(head * members * 8 + member * 8, 8), 8)
        return row, column, local

    for mask in range(parts):
        for head in range(near):
            row, column, local = places(mask, head)
            spread[row, column] = query_held[mask, local, :]
    weight = capped_weight(dot_last(k_ref[0], spread[...].astype(jnp.bfloat16)))
    valid = lax.broadcasted_iota(jnp.int32, weight.shape, 0) < lengths[here * members + member]
    weight = jnp.where(valid, weight, 0.0).astype(jnp.bfloat16)
    result[:, :columns] = dot_first(weight, v_ref[0])
    result[:, columns:] = dot_first(weight, jnp.ones((slots, LANES), jnp.bfloat16))
    for mask in range(parts):
        for head in range(near):
            row, column, local = places(mask, head)
            sums[mask, local, :] = result[row, column]
            totals[mask, local, :] = result[row, columns:]

    @pl.when(member == members - 1)
    def _():
        count = sums.shape[1]
        outs[0][...] = sums[0]
        outs[1][...] = totals[0]
        for mask in range(1, parts):
            ref = outs[mask + 1]
            ref[:count, :] = sums[mask].astype(jnp.bfloat16)
            packed[0:1, :] = totals[mask].T[0:1]
            ref[count:, :] = split_rows(packed[...])


def suffix_attention(place, lengths, own, received, cache_keys, cache_values, token):
    parts = len(received) + 1
    members, slots, columns = cache_keys.shape
    count = own.shape[0]
    spread_rows = 8 * columns // HEAD_SIZE
    operands = (own, *received, cache_keys, cache_values, token)
    outs = [shape((count, HEAD_SIZE), jnp.float32)] * 2 + [
        shape((count + 16, HEAD_SIZE), jnp.bfloat16)
    ] * (parts - 1)
    cache = pl.BlockSpec((1, slots, columns), lambda i, p, n: (i, 0, 0))
    return call(
        functools.partial(suffix_kernel, parts),
        (place, lengths),
        operands,
        outs,
        [whole(own)] + [whole(a) for a in received] + [cache, cache, corner(token)],
        [whole(a) for a in outs],
        (members,),
        [
            pltpu.VMEM((parts, count, HEAD_SIZE), jnp.float32),
            pltpu.VMEM((spread_rows, columns), jnp.float32),
            pltpu.VMEM((spread_rows, columns + LANES), jnp.float32),
            pltpu.VMEM((parts, count, HEAD_SIZE), jnp.float32),
            pltpu.VMEM((parts, count, HEAD_SIZE), jnp.float32),
            pltpu.VMEM((8, LANES), jnp.float32),
        ],
        4 * members * spread_rows * slots * columns,
        4 * members * slots * columns,
    )


def mix_kernel(parts, far, place, sum_ref, total_ref, *refs):
    prompt, refs = refs[:far], refs[far:]
    near_sum, near_total, *suffix = refs[: parts + 1]
    out_ref, sums, totals = refs[parts + 1 :]
    count = sum_ref.shape[0]
    rows = out_ref.shape[0]
    heads = count // (2 * rows)
    total = sum_ref[...]
    for ref in prompt:
        total = total + ref[:count, :].astype(jnp.float32)
    sums[...] = total
    for block in range(count // LANES):
        at = slice(block * LANES, (block + 1) * LANES)
        total = total_ref[at, :]
        for ref in prompt:
            total = total + down_rows(joined_row(ref[count:, :], block))
        totals[at, :] = total
    share = 2 * rows // parts
    for mask in range(parts):
        if mask == 0:
            near, near_weight = near_sum[...], near_total[...]
        else:
            ref = suffix[mask - 1]
            near = ref[: count // parts, :].astype(jnp.float32)
            near_weight = down_rows(joined_row(ref[count // parts :, :], 0))
        for head in range(heads):
            first = pl.multiple_of(head * 2 * rows + (place[0] ^ mask) * share, share)
            at = pl.ds(first, share)
            local = slice(head * share, (head + 1) * share)
            sums[at, :] = sums[at, :] + near[local]
            totals[at, :] = totals[at, :] + near_weight[local]
    mixed = sums[...] / totals[...]
    for head in range(heads):
        tiles = mixed[head * 2 * rows : (head + 1) * 2 * rows].reshape(rows // 8, 2, 8, HEAD_SIZE)
        for member, part in enumerate(interleave(tiles[:, 0], tiles[:, 1])):
            at = (2 * head + member) * HEAD_SIZE
            out_ref[:, at : at + HEAD_SIZE] = part.reshape(rows, HEAD_SIZE).astype(jnp.bfloat16)


def mix(place, sums, totals, prompt, suffix, rows):
    count = sums.shape[0]
    operands = (sums, totals, *prompt, *suffix)
    out = shape((rows, count // rows * HEAD_SIZE), jnp.bfloat16)
    return call(
        functools.partial(mix_kernel, len(suffix) - 1, len(prompt)),
        (place,),
        operands,
        out,
        [whole(a) for a in operands],
        whole(out),
        (1,),
        [pltpu.VMEM((count, HEAD_SIZE), jnp.float32)] * 2,
        10 * count * HEAD_SIZE,
        8 * count * HEAD_SIZE,
    )


def output_kernel(masks, started, place, *refs):
    inputs, refs = refs[: len(masks)], refs[len(masks) :]
    w_ref, out_ref = refs[0], refs[-1]
    step = pl.program_id(0)
    for index, ref in enumerate(inputs):

        @pl.when(step == index)
        def _():
            term = jnp.dot(ref[...], w_ref[...], preferred_element_type=jnp.float32)
            if index > 0:
                out_ref[...] += term
            elif started:
                out_ref[...] = refs[1][...] + term
            else:
                out_ref[...] = term


def output_projection(place, masks, mixed, weights, started=None):
    rows, depth = mixed[0].shape
    width = weights.shape[1]
    chosen = pl.BlockSpec(
        (depth, width), lambda i, p: (p[0] ^ (i + masks[0]), 0)
    )
    out = shape((rows, width), jnp.float32)
    more = () if started is None else (started,)
    return call(
        functools.partial(output_kernel, masks, started is not None),
        (place,),
        (*mixed, weights, *more),
        out,
        [whole(a) for a in mixed] + [chosen] + [whole(a) for a in more],
        whole(out),
        (len(masks),),
        [],
        2 * len(masks) * rows * depth * width,
        2 * len(masks) * depth * width,
    )


def attended_kernel(place, here_ref, there_ref, out_ref, squares_ref):
    attended = here_ref[...] + there_ref[...]
    out_ref[...] = attended
    total = jnp.sum(attended * attended, axis=1, keepdims=True)
    squares_ref[...] = jnp.broadcast_to(total, (total.shape[0], LANES)).T[:8]


def attended_squares(place, here, there):
    outs = [shape(here.shape, jnp.float32), shape((8, here.shape[0]), jnp.float32)]
    return call(
        attended_kernel,
        (place,),
        (here, there),
        outs,
        [whole(here), whole(there)],
        [whole(a) for a in outs],
        (1,),
        [],
        4 * here.size,
        12 * here.size,
    )


def finish_kernel(place, x_ref, attended_ref, gain_ref, *refs):
    *squares, out_ref = refs
    total = squares[0][0:1, :]
    for ref in squares[1:]:
        total = total + ref[0:1, :]
    inverse = lax.rsqrt(down_rows(total) / MODEL_WIDTH + EPSILON)
    for at in range(0, x_ref.shape[2], LANES):
        lanes = slice(at, at + LANES)
        branch = attended_ref[:, lanes] * inverse * gain_ref[lanes].reshape(1, LANES)
        x = x_ref[:, :, lanes].astype(jnp.float32)
        out_ref[:, :, lanes] = (x + branch.reshape(x.shape)).astype(jnp.bfloat16)


def finish(place, x, attended, gain, squares):
    operands = (x, attended, gain, *squares)
    out = shape(x.shape, jnp.bfloat16)
    return call(
        finish_kernel,
        (place,),
        operands,
        out,
        [whole(a) for a in operands],
        whole(out),
        (1,),
        [],
        4 * x.size,
        8 * x.size,
    )


def by_heads(
    hidden_in,
    pre_gain,
    w_query,
    key_projection,
    value_projection,
    w_out,
    post_gain,
    prompt_keys,
    prompt_values,
    suffix_key_cache,
    suffix_value_cache,
    suffix_len,
):
    group_rows, steps, _ = hidden_in.shape
    rows = group_rows * steps
    parts = lax.axis_size("prefix")
    groups = lax.axis_size("prefill")
    heads = prompt_keys.shape[1] // HEAD_SIZE // parts
    prompt_total = prompt_keys.shape[0] * groups * parts
    place = lax.axis_index("prefix").astype(jnp.int32).reshape(1)
    near = range(1, parts)
    far = range(1, groups)

    def swapped(arrays, axis):
        return [paired(a, axis, m) for m, a in enumerate(arrays, start=1)]

    *sent, own, squares, scaled = query_projection(place, hidden_in, pre_gain, w_query, parts)
    received = swapped(sent, "prefix")
    first_head = swapped(
        cache_columns(place, prompt_keys, prompt_values, 0, heads, parts, squares), "prefix"
    )

    positions = (
        (prompt_total + suffix_len[:, None] + jnp.arange(steps, dtype=jnp.int32)[None, :])
        .reshape(-1)
        .astype(jnp.float32)
    )
    half = HEAD_SIZE // 2
    freq = 10000.0 ** (-2.0 * jnp.arange(half, dtype=jnp.float32) / HEAD_SIZE)
    angle = positions[:, None] * freq[None, :]
    cosine, sine = jnp.cos(angle), jnp.sin(angle)
    cosine = jnp.concatenate([cosine, cosine], axis=1)
    sine = jnp.concatenate([-sine, sine], axis=1)

    queries, *split_queries, inverse = query_rope(
        place, own, received, squares, cosine, sine, parts
    )
    far_queries = [paired(queries, "prefill", m) for m in far]
    pair, *sent = pair_projection(
        place, scaled, key_projection, value_projection, split_queries[1:]
    )
    terms = swapped(sent, "prefix")
    second_head = swapped(
        cache_columns(place, prompt_keys, prompt_values, 1, heads, parts, pair), "prefix"
    )

    first = prompt_first(
        place, [queries, *far_queries], prompt_keys, prompt_values, first_head, heads
    )
    near_sums, near_totals, *sent = suffix_attention(
        place, suffix_len, split_queries[0], terms, suffix_key_cache, suffix_value_cache, first[1]
    )
    suffix = [near_sums, near_totals, *swapped(sent, "prefix")]
    packed = [
        prompt_second(
            place,
            far_queries[m - 1],
            prompt_keys,
            prompt_values,
            second_head,
            first[2 * m : 2 * m + 2],
            heads,
            near_totals,
        )
        for m in far
    ]
    prompt_results = swapped(packed, "prefill")
    sums, totals = own_attention_sums(
        place,
        queries,
        prompt_keys,
        prompt_values,
        second_head,
        first[:2],
        pair,
        terms,
        (inverse, cosine, sine),
        packed,
    )
    mixed = mix(place, sums, totals, prompt_results, suffix, rows)
    others = [paired(mixed, "prefix", m) for m in near]
    head_terms = output_projection(place, (0,), [mixed], w_out)
    head_terms = output_projection(place, tuple(near), others, w_out, head_terms)
    attended, squares = attended_squares(place, head_terms, paired(head_terms, "tensor", 1))
    squares = [squares] + [paired(squares, "prefix", m) for m in near]
    return finish(place, hidden_in, attended, post_gain, squares)


def heads_divide(mesh):
    sizes = [mesh.shape[name] for name in ("prefill", "prefix", "tensor")]
    key_heads = QUERY_HEADS // 2 // sizes[2]
    return key_heads == 2 * sizes[1] and sizes[1] == 4 and sizes[2] == 2 and sizes[0] in (2, 4)


def solution(mesh):
    return jax.shard_map(
        by_heads if heads_divide(mesh) else per_device,
        mesh=mesh,
        in_specs=(
            P("prefill", None, "prefix"),
            P("prefix"),
            P("prefix", "tensor"),
            P("prefix", "tensor"),
            P("prefix", "tensor"),
            P("tensor", "prefix"),
            P("prefix"),
            P(("prefill", "prefix"), "tensor"),
            P(("prefill", "prefix"), "tensor"),
            P(("prefill", "prefix"), None, "tensor"),
            P(("prefill", "prefix"), None, "tensor"),
            P("prefill"),
        ),
        out_specs=P("prefill", None, "prefix"),
        check_vma=False,
    )
```

```python
import functools

import jax
import jax.numpy as jnp
from jax import lax
from jax.experimental import pallas as pl
from jax.experimental.pallas import tpu as pltpu
from jax.sharding import PartitionSpec as P

MODEL_WIDTH = 4608
QUERY_HEADS = 32
HEAD_SIZE = 128


SOFTCAP = 50.0
EPSILON = 1e-06
SPREAD_AT = 2
LOG2_E = 1.4426950408889634
LANES = 128
VMEM_LIMIT = 24 * 1024 * 1024
FIRST_LIMIT = 59 * 1024 * 1024
ROPE_LIMIT = 59 * 1024 * 1024
PAIR_LIMIT = 59 * 1024 * 1024
SUFFIX_LIMIT = 24 * 1024 * 1024
QUERY_SCALE = (MODEL_WIDTH // QUERY_HEADS) ** (-0.5)


def apply_rotation(values, token_positions, heads):
    width = values.shape[1] // heads
    half = width // 2
    freq = 10000.0 ** (-2.0 * jnp.arange(half, dtype=jnp.float32) / width)
    angle = token_positions[:, None] * freq[None, :]
    cosine = jnp.cos(angle)[:, None, :]
    sine = jnp.sin(angle)[:, None, :]
    parts = values.reshape(values.shape[0], heads, width)
    first = parts[:, :, :half]
    second = parts[:, :, half:]
    turned = jnp.concatenate(
        [first * cosine - second * sine, second * cosine + first * sine], axis=2
    )
    return turned.reshape(values.shape[0], heads * width)


def soft_weight(scores):
    return jnp.exp(SOFTCAP * jnp.tanh(scores / SOFTCAP))


def shared_attention(queries, keys, values):
    count = queries.shape[0]
    kv_heads = keys.shape[1] // HEAD_SIZE
    heads_per_group = queries.shape[1] // keys.shape[1]
    grouped = queries.reshape(count, kv_heads, heads_per_group, HEAD_SIZE)
    key_head_rows = keys.reshape(keys.shape[0], kv_heads, HEAD_SIZE)
    value_head_rows = values.reshape(values.shape[0], kv_heads, HEAD_SIZE)
    scores = jnp.einsum(
        "nkgd,mkd->nkgm", grouped, key_head_rows, preferred_element_type=jnp.float32
    )
    weights = soft_weight(scores)
    totals = jnp.sum(weights, axis=3).reshape(count, kv_heads * heads_per_group)
    summed = jnp.einsum(
        "nkgm,mkd->nkgd",
        weights.astype(jnp.bfloat16),
        value_head_rows,
        preferred_element_type=jnp.float32,
    )
    return (summed.reshape(count, kv_heads * heads_per_group * HEAD_SIZE), totals)


def own_attention(
    queries, cached_key_rows, cached_value_rows, latest_keys, latest_values, lengths, steps
):
    members = lengths.shape[0]
    slots = cached_key_rows.shape[1]
    kv_heads = cached_key_rows.shape[2] // HEAD_SIZE
    heads_per_group = queries.shape[1] // cached_key_rows.shape[2]
    grouped = queries.reshape(members, steps, kv_heads, heads_per_group, HEAD_SIZE)
    cache_k = cached_key_rows.reshape(members, slots, kv_heads, HEAD_SIZE)
    cache_v = cached_value_rows.reshape(members, slots, kv_heads, HEAD_SIZE)
    valid = jnp.arange(slots, dtype=jnp.int32)[None, :] < lengths[:, None]
    cache_scores = jnp.einsum(
        "rjkgd,rmkd->rjkgm", grouped, cache_k, preferred_element_type=jnp.float32
    )
    cache_weights = jnp.where(valid[:, None, None, None, :], soft_weight(cache_scores), 0.0)
    new_k = latest_keys.reshape(members, steps, kv_heads, HEAD_SIZE)
    new_v = latest_values.reshape(members, steps, kv_heads, HEAD_SIZE)
    step_ids = jnp.arange(steps, dtype=jnp.int32)
    causal = step_ids[None, :] <= step_ids[:, None]
    new_scores = jnp.einsum("rjkgd,rikd->rjkgi", grouped, new_k, preferred_element_type=jnp.float32)
    new_weights = jnp.where(causal[None, :, None, None, :], soft_weight(new_scores), 0.0)
    totals = jnp.sum(cache_weights, axis=4) + jnp.sum(new_weights, axis=4)
    summed = jnp.einsum(
        "rjkgm,rmkd->rjkgd",
        cache_weights.astype(jnp.bfloat16),
        cache_v,
        preferred_element_type=jnp.float32,
    )
    summed = summed + jnp.einsum(
        "rjkgi,rikd->rjkgd",
        new_weights.astype(jnp.bfloat16),
        new_v,
        preferred_element_type=jnp.float32,
    )
    flat_rows = members * steps
    return (
        summed.reshape(flat_rows, kv_heads * heads_per_group * HEAD_SIZE),
        totals.reshape(flat_rows, kv_heads * heads_per_group),
    )


def per_device(
    hidden_in,
    pre_gain,
    w_query,
    key_projection,
    value_projection,
    w_out,
    post_gain,
    prompt_keys,
    prompt_values,
    suffix_key_cache,
    suffix_value_cache,
    suffix_len,
):
    group_rows, steps, local_width = hidden_in.shape
    members = suffix_key_cache.shape[0]
    query_cols = w_query.shape[1]
    kv_cols = key_projection.shape[1]
    heads = query_cols // HEAD_SIZE
    kv_heads = kv_cols // HEAD_SIZE
    own_count = members * steps
    prompt_total = prompt_keys.shape[0] * lax.axis_size("prefill") * lax.axis_size("prefix")
    signal = hidden_in.astype(jnp.float32).reshape(group_rows * steps, local_width)
    squares = lax.psum(jnp.sum(signal * signal, axis=1), "prefix")
    normed = (signal * lax.rsqrt(squares[:, None] / MODEL_WIDTH + EPSILON) * pre_gain).astype(
        jnp.bfloat16
    )
    weights_all = jnp.concatenate([w_query, key_projection, value_projection], axis=1)
    step_ids = jnp.arange(steps, dtype=jnp.int32)
    group_positions = (
        (prompt_total + suffix_len[:, None] + step_ids[None, :]).reshape(-1).astype(jnp.float32)
    )
    first_row = lax.axis_index("prefix") * members
    own_lengths = lax.dynamic_slice_in_dim(suffix_len, first_row, members)
    own_positions = lax.dynamic_slice_in_dim(group_positions, first_row * steps, own_count)
    scale = (MODEL_WIDTH // QUERY_HEADS) ** (-0.5)
    own_proj = lax.psum_scatter(
        jnp.dot(normed, weights_all, preferred_element_type=jnp.float32),
        "prefix",
        scatter_dimension=0,
        tiled=True,
    )
    own_queries = (apply_rotation(own_proj[:, :query_cols], own_positions, heads) * scale).astype(
        jnp.bfloat16
    )
    group_queries = lax.all_gather(own_queries, "prefix", axis=0, tiled=True)
    latest_keys = apply_rotation(
        own_proj[:, query_cols : query_cols + kv_cols], own_positions, kv_heads
    ).astype(jnp.bfloat16)
    latest_values = own_proj[:, query_cols + kv_cols :].astype(jnp.bfloat16)
    summed, totals = shared_attention(
        group_queries,
        lax.all_gather(prompt_keys, "prefill", axis=0, tiled=True),
        lax.all_gather(prompt_values, "prefill", axis=0, tiled=True),
    )
    prompt_totals = totals
    far_sums, far_totals = (
        lax.psum_scatter(summed, "prefix", scatter_dimension=0, tiled=True),
        lax.psum_scatter(prompt_totals, "prefix", scatter_dimension=0, tiled=True),
    )
    near_sums, near_totals = own_attention(
        own_queries,
        suffix_key_cache,
        suffix_value_cache,
        latest_keys,
        latest_values,
        own_lengths,
        steps,
    )
    totals = far_totals + near_totals
    sums = (far_sums + near_sums).reshape(own_count, heads, HEAD_SIZE)
    mixed = (sums / totals[:, :, None]).reshape(own_count, query_cols).astype(jnp.bfloat16)
    head_terms = jnp.dot(
        lax.all_gather(mixed, "prefix", axis=0, tiled=True),
        w_out,
        preferred_element_type=jnp.float32,
    )
    attended = lax.psum(head_terms, "tensor")
    out_squares = lax.psum(jnp.sum(attended * attended, axis=1), "prefix")
    branch = attended * lax.rsqrt(out_squares[:, None] / MODEL_WIDTH + EPSILON) * post_gain
    return (signal + branch).astype(jnp.bfloat16).reshape(group_rows, steps, local_width)


def paired(values, axis, mask):
    size = lax.axis_size(axis)
    return lax.ppermute(values, axis, [(i, i ^ mask) for i in range(size)])


def call(
    kernel,
    prefetch,
    operands,
    out_shape,
    in_specs,
    out_specs,
    grid,
    scratch,
    flops,
    moved,
    limit=VMEM_LIMIT,
):
    return pl.pallas_call(
        kernel,
        out_shape=out_shape,
        grid_spec=pltpu.PrefetchScalarGridSpec(
            num_scalar_prefetch=len(prefetch),
            grid=grid,
            in_specs=in_specs,
            out_specs=out_specs,
            scratch_shapes=scratch,
        ),
        compiler_params=pltpu.CompilerParams(vmem_limit_bytes=limit),
        cost_estimate=pl.CostEstimate(flops=flops, bytes_accessed=moved, transcendentals=0),
    )(*prefetch, *operands)


def whole(array):
    rank = len(array.shape)
    return pl.BlockSpec(array.shape, lambda *_: (0,) * rank)


def corner(array):
    rank = len(array.shape)
    return pl.BlockSpec(
        (1,) * (rank - 2) + (32 // array.dtype.itemsize, LANES), lambda *_: (0,) * rank
    )


def shape(dims, dtype):
    return jax.ShapeDtypeStruct(dims, dtype)


def dot_last(left, right):
    return lax.dot_general(left, right, (((1,), (1,)), ((), ())), preferred_element_type=jnp.float32)


def dot_first(left, right):
    return lax.dot_general(left, right, (((0,), (0,)), ((), ())), preferred_element_type=jnp.float32)


def capped_weight(scores):
    return jnp.exp2(jnp.tanh(scores * (1.0 / SOFTCAP)) * (SOFTCAP * LOG2_E))


def split_rows(rows):
    high = rows.astype(jnp.bfloat16).astype(jnp.float32)
    return jnp.concatenate([high, rows - high], axis=0).astype(jnp.bfloat16)


def joined_row(block, index):
    pair = block.astype(jnp.float32)
    return pair[index : index + 1] + pair[8 + index : 9 + index]


def down_rows(row):
    return jnp.broadcast_to(row, (LANES, row.shape[1])).T


def lower_half(tiles):
    return lax.broadcasted_iota(jnp.int32, tiles.shape, 1) < tiles.shape[1] // 2


def interleave(first, second):
    low = lower_half(first)
    half = first.shape[1] // 2
    return (
        jnp.where(low, first, pltpu.roll(second, half, 1)),
        jnp.where(low, pltpu.roll(first, half, 1), second),
    )


def rotated(values, cosine, sine):
    return values * cosine + pltpu.roll(values, HEAD_SIZE // 2, 1) * sine


def gain_row(ref):
    return ref[...].reshape(1, ref.shape[0])


def copy_in(source, target, semaphore):
    copy = pltpu.make_async_copy(source, target, semaphore)
    copy.start()
    return copy


def block_of(place, mask, width):
    return pl.ds(pl.multiple_of((place[0] ^ mask) * width, width), width)


def query_projection_kernel(parts, place, gain_ref, x_hbm, w_hbm, keys_hbm, values_hbm, *refs):
    blocks, refs = refs[: parts - 1], refs[parts - 1 :]
    *sent, own_ref, squares_ref, scaled_ref, x_ref, w_ref, block_ref, semaphores, block_semaphores = refs
    rows, columns = own_ref.shape
    masks = (*range(1, len(sent) + 1), 0)
    x_copy = copy_in(x_hbm, x_ref, semaphores.at[len(masks)])
    w_copies = [
        copy_in(w_hbm.at[:, block_of(place, mask, columns)], w_ref.at[mask], semaphores.at[mask])
        for mask in masks
    ]
    width = blocks[0].shape[1] // 2
    block_copies = [
        copy_in(
            source.at[:, block_of(place, mask, width)],
            block_ref.at[mask - 1, :, half * width : (half + 1) * width],
            block_semaphores.at[mask - 1, half],
        )
        for mask in range(1, parts)
        for half, source in enumerate((keys_hbm, values_hbm))
    ]
    x_copy.wait()
    x = x_ref[...].astype(jnp.float32).reshape(rows, x_ref.shape[2])
    scaled_ref[...] = (x * gain_row(gain_ref)).astype(jnp.bfloat16)
    total = jnp.sum(x * x, axis=1, keepdims=True)
    across = jnp.broadcast_to(total, (rows, LANES)).T[:8]
    squares_ref[...] = across
    tail = split_rows(across)
    for ref in sent:
        ref[rows:, :] = jnp.zeros((16, ref.shape[1]), jnp.bfloat16)
        ref[rows:, :rows] = tail
    for mask, copy, ref in zip(masks, w_copies, (*sent, own_ref)):
        copy.wait()
        if mask == SPREAD_AT:
            for block_copy in block_copies:
                block_copy.wait()
            block_copies = [
                copy_in(block_ref.at[index], target, block_semaphores.at[index, 0])
                for index, target in enumerate(blocks)
            ]
        product = jnp.dot(scaled_ref[...], w_ref[mask], preferred_element_type=jnp.float32)
        ref[:rows, :] = product.astype(ref.dtype)
    for copy in block_copies:
        copy.wait()


def query_projection(place, x, gain, weights, keys, values, parts):
    members, steps, width = x.shape
    rows = members * steps
    columns = weights.shape[1] // parts
    blocks = [shape((keys.shape[0], 2 * keys.shape[1] // parts), keys.dtype)] * (parts - 1)
    outs = [shape((rows + 16, columns), jnp.bfloat16)] * (parts - 1) + [
        shape((rows, columns), jnp.float32),
        shape((8, rows), jnp.float32),
        shape((rows, width), jnp.bfloat16),
    ]
    far = pl.BlockSpec(memory_space=pl.ANY)
    return call(
        functools.partial(query_projection_kernel, parts),
        (place,),
        (gain, x, weights, keys, values),
        blocks + outs,
        [whole(gain), far, far, far, far],
        [far] * (parts - 1) + [whole(a) for a in outs],
        (1,),
        [
            pltpu.VMEM(x.shape, x.dtype),
            pltpu.VMEM((parts, width, columns), weights.dtype),
            pltpu.VMEM((parts - 1, *blocks[0].shape), keys.dtype),
            pltpu.SemaphoreType.DMA((parts + 1,)),
            pltpu.SemaphoreType.DMA((parts - 1, 2)),
        ],
        2 * rows * width * weights.shape[1],
        2 * width * weights.shape[1],
        FIRST_LIMIT,
    )


def pair_projection_kernel(place, scaled_ref, k_hbm, v_hbm, *refs):
    parts = len(refs) // 2
    queries, (own_ref, *outs), (w_ref, semaphores) = (
        refs[: parts - 1],
        refs[parts - 1 : 2 * parts - 1],
        refs[2 * parts - 1 :],
    )
    rows, width = own_ref.shape
    columns = width // 2
    masks = (*range(1, parts), 0)
    copies = {}
    for mask in masks:
        at = block_of(place, mask, columns)
        copies[mask] = [
            copy_in(
                source.at[:, at],
                w_ref.at[mask, :, half * columns : (half + 1) * columns],
                semaphores.at[mask, half],
            )
            for half, source in enumerate((k_hbm, v_hbm))
        ]
    for ref, out_ref in zip(queries, outs):
        tall = out_ref.shape[0] - rows
        for piece in range(ref.shape[0] // tall):
            out_ref[rows:, head_lanes(piece)] = ref[piece * tall : (piece + 1) * tall, :]
    for mask in masks:
        for copy in copies[mask]:
            copy.wait()
        term = jnp.dot(scaled_ref[...], w_ref[mask], preferred_element_type=jnp.float32)
        target = outs[mask - 1] if mask else own_ref
        target[:rows, :] = term.astype(target.dtype)


def pair_projection(place, scaled, key_weights, value_weights, queries):
    parts = len(queries) + 1
    rows, width = scaled.shape
    columns = key_weights.shape[1] // parts
    far = pl.BlockSpec(memory_space=pl.ANY)
    tall = queries[0].size // (2 * columns)
    outs = [shape((rows, 2 * columns), jnp.float32)] + [
        shape((rows + tall, 2 * columns), jnp.bfloat16)
    ] * (parts - 1)
    return call(
        pair_projection_kernel,
        (place,),
        (scaled, key_weights, value_weights, *queries),
        outs,
        [whole(scaled), far, far] + [whole(a) for a in queries],
        [whole(a) for a in outs],
        (1,),
        [
            pltpu.VMEM((parts, width, 2 * columns), key_weights.dtype),
            pltpu.SemaphoreType.DMA((parts, 2)),
        ],
        4 * rows * width * key_weights.shape[1],
        4 * width * key_weights.shape[1],
        PAIR_LIMIT,
    )


def paired_heads(values, cosine, sine):
    tiles = [
        rotated(values[:, at : at + HEAD_SIZE], cosine, sine).reshape(-1, 8, HEAD_SIZE)
        for at in (0, HEAD_SIZE)
    ]
    return jnp.stack(interleave(*tiles), axis=1).reshape(2 * values.shape[0], HEAD_SIZE)


def query_rope_kernel(parts, place, own_ref, *refs):
    received, refs = refs[: parts - 1], refs[parts - 1 :]
    squares_ref, cos_ref, sin_ref, query_ref, *suffix_refs, inverse_ref, held = refs
    rows, columns = own_ref.shape
    squares = squares_ref[0:1, :]
    total = own_ref[...]
    for ref in received:
        squares = squares + joined_row(ref[rows:, :rows], 0)
        total = total + ref[:rows, :].astype(jnp.float32)
    inverse = lax.rsqrt(down_rows(squares) / MODEL_WIDTH + EPSILON)
    inverse_ref[...] = inverse
    cosine = cos_ref[...] * inverse * QUERY_SCALE
    sine = sin_ref[...] * inverse * QUERY_SCALE
    pair = 2 * HEAD_SIZE
    share = 2 * rows // parts
    for head in range(columns // pair):
        at = slice(head * 2 * rows, (head + 1) * 2 * rows)
        held[...] = paired_heads(total[:, head * pair : (head + 1) * pair], cosine, sine)
        query_ref[at, :] = held[...].astype(jnp.bfloat16)
        for mask, ref in enumerate(suffix_refs):
            ref[head * share : (head + 1) * share, :] = held[
                block_of(place, mask, share), :
            ].astype(jnp.bfloat16)


def query_rope(place, own, received, squares, cosine, sine, parts):
    rows, columns = own.shape
    count = rows * columns // HEAD_SIZE
    operands = (own, *received, squares, cosine, sine)
    outs = (
        [shape((count, HEAD_SIZE), jnp.bfloat16)]
        + [shape((count // parts, HEAD_SIZE), jnp.bfloat16)] * parts
        + [shape((rows, LANES), jnp.float32)]
    )
    return call(
        functools.partial(query_rope_kernel, parts),
        (place,),
        operands,
        outs,
        [whole(a) for a in operands],
        [whole(a) for a in outs],
        (1,),
        [pltpu.VMEM((2 * rows, HEAD_SIZE), jnp.float32)],
        10 * rows * columns,
        12 * rows * columns,
        ROPE_LIMIT,
    )


def attend(query, pairs):
    result = None
    for key, value in pairs:
        weight = capped_weight(dot_last(query, key)).astype(jnp.bfloat16)
        ones = jnp.ones((value.shape[0], LANES), jnp.bfloat16)
        term = jnp.dot(
            weight, jnp.concatenate([value, ones], axis=1), preferred_element_type=jnp.float32
        )
        result = term if result is None else result + term
    return result


def total_rows(totals):
    return [totals[at : at + LANES].T[0:1] for at in range(0, totals.shape[0], LANES)]


def head_lanes(head):
    return slice(head * HEAD_SIZE, (head + 1) * HEAD_SIZE)


def received_pair(ref, head, heads):
    return ref[:, head_lanes(head)], ref[:, head_lanes(heads + head)]


def prompt_first_kernel(chunks, place, *refs):
    queries, refs = refs[:chunks], refs[chunks:]
    k_ref, v_ref, *received = refs[: -2 * chunks]
    outs = refs[-2 * chunks :]
    heads = k_ref.shape[1] // HEAD_SIZE
    count = queries[0].shape[0] // heads
    for index, query_ref in enumerate(queries):
        sum_ref, total_ref = outs[2 * index : 2 * index + 2]
        for head in range(heads):
            at = slice(head * count, (head + 1) * count)
            pairs = [(k_ref[:, head_lanes(head)], v_ref[:, head_lanes(head)])]
            pairs += [received_pair(ref, head, heads) for ref in received]
            result = attend(query_ref[at, :], pairs)
            sum_ref[at, :] = result[:, :HEAD_SIZE]
            total_ref[at, :] = result[:, HEAD_SIZE:]


def prompt_first(place, queries, prompt_keys, prompt_values, received, parts):
    tokens = prompt_keys.shape[0]
    chosen = pl.BlockSpec((tokens, prompt_keys.shape[1] // parts), lambda i, p: (0, p[0]))
    outs = [shape(queries[0].shape, jnp.float32)] * (2 * len(queries))
    return call(
        functools.partial(prompt_first_kernel, len(queries)),
        (place,),
        (*queries, prompt_keys, prompt_values, *received),
        outs,
        [whole(a) for a in queries] + [chosen, chosen] + [whole(a) for a in received],
        [whole(a) for a in outs],
        (1,),
        [],
        6 * len(queries) * queries[0].size * (len(received) + 1) * tokens,
        4 * parts * tokens * HEAD_SIZE,
    )


def prompt_last_kernel(place, q_ref, *refs):
    *blocks, sum_ref, total_ref, out_ref, held = refs
    heads = blocks[0].shape[1] // (2 * HEAD_SIZE)
    count = q_ref.shape[0] // heads
    held[...] = jnp.zeros(held.shape, jnp.float32)
    for head in range(heads):
        at = slice(head * count, (head + 1) * count)
        result = attend(q_ref[at, :], [received_pair(ref, head, heads) for ref in blocks])
        out_ref[at, :] = (sum_ref[at, :] + result[:, :HEAD_SIZE]).astype(jnp.bfloat16)
        for row, values in enumerate(total_rows(total_ref[at, :] + result[:, HEAD_SIZE:])):
            to = head * count // LANES + row
            held[to : to + 1, :] = values
    out_ref[heads * count :, :] = split_rows(held[...])


def prompt_last(place, queries, blocks, first):
    out = shape((queries.shape[0] + 16, HEAD_SIZE), jnp.bfloat16)
    operands = (queries, *blocks, *first)
    return call(
        prompt_last_kernel,
        (place,),
        operands,
        out,
        [whole(a) for a in operands],
        whole(out),
        (1,),
        [pltpu.VMEM((8, LANES), jnp.float32)],
        6 * queries.size * len(blocks) * blocks[0].shape[0],
        2 * len(blocks) * blocks[0].size,
    )


def own_kernel(parts, place, q_ref, k_ref, v_ref, *refs):
    blocks, refs = refs[: parts - 1], refs[parts - 1 :]
    pair_ref, refs = refs[0], refs[1:]
    received, refs = refs[: parts - 1], refs[parts - 1 :]
    inverse_ref, cos_ref, sin_ref = refs[:3]
    sum_ref, total_ref = refs[-2:]
    heads = k_ref.shape[1] // HEAD_SIZE
    count = q_ref.shape[0] // heads
    rows = inverse_ref.shape[0]
    inverse = inverse_ref[...]
    cosine = cos_ref[...] * inverse
    sine = sin_ref[...] * inverse

    def new_terms(index):
        term = pair_ref[:, head_lanes(index)]
        for ref in received:
            term = term + ref[:rows, head_lanes(index)].astype(jnp.float32)
        return term

    query_row = lax.broadcasted_iota(jnp.int32, (count, rows), 0)
    key_row = lax.broadcasted_iota(jnp.int32, (count, rows), 1)
    same = query_row // 8 == key_row // 4
    valid = same & (key_row % 4 <= query_row % 4)
    ones = jnp.ones((rows, LANES), jnp.bfloat16)
    for head in range(heads):
        at = slice(head * count, (head + 1) * count)
        query = q_ref[at, :]
        key = rotated(new_terms(head), cosine, sine)
        value = new_terms(heads + head) * inverse
        weight = capped_weight(dot_last(query, key.astype(jnp.bfloat16)))
        weight = jnp.where(valid, weight, 0.0).astype(jnp.bfloat16)
        result = jnp.dot(
            weight,
            jnp.concatenate([value.astype(jnp.bfloat16), ones], axis=1),
            preferred_element_type=jnp.float32,
        )
        pairs = [(k_ref[:, head_lanes(head)], v_ref[:, head_lanes(head)])]
        pairs += [received_pair(ref, head, heads) for ref in blocks]
        result = result + attend(query, pairs)
        sum_ref[at, :] = result[:, :HEAD_SIZE]
        total_ref[at, :] = result[:, HEAD_SIZE:]


def own_sums(
    place, queries, prompt_keys, prompt_values, blocks, pair, received, tables, tokens_after
):
    parts = len(blocks) + 1
    tokens = prompt_keys.shape[0]
    chosen = pl.BlockSpec((tokens, prompt_keys.shape[1] // parts), lambda i, p: (0, p[0]))
    operands = (*blocks, pair, *received, *tables)
    outs = [shape(queries.shape, jnp.float32)] * 2
    return call(
        functools.partial(own_kernel, parts),
        (place,),
        (queries, prompt_keys, prompt_values, *operands, *tokens_after),
        outs,
        [whole(queries), chosen, chosen]
        + [whole(a) for a in operands]
        + [corner(a) for a in tokens_after],
        [whole(a) for a in outs],
        (1,),
        [],
        6 * queries.size * parts * tokens,
        4 * parts * tokens * HEAD_SIZE,
    )


def suffix_kernel(parts, place, lengths, own_ref, *refs):
    received, (k_hbm, v_hbm), refs = (
        refs[: parts - 1],
        refs[parts - 1 : parts + 1],
        refs[-(parts + 8) :],
    )
    outs, refs = refs[: parts + 1], refs[parts + 1 :]
    query_held, k_ref, v_ref, sums, totals, packed, semaphores = refs
    members, slots, columns = k_ref.shape
    heads = columns // HEAD_SIZE
    near = heads // parts
    here = place[0]
    copies = [
        [
            copy_in(source.at[member], ref.at[member], semaphores.at[member, half])
            for half, (source, ref) in enumerate(((k_hbm, k_ref), (v_hbm, v_ref)))
        ]
        for member in range(members)
    ]
    packed[...] = jnp.zeros(packed.shape, jnp.float32)
    count = members * 8
    for mask, ref in enumerate((own_ref, *received)):
        for head in range(near):
            target = query_held.at[(here ^ mask) * near + head]
            if mask == 0:
                target[...] = ref[head * count : (head + 1) * count, :].astype(jnp.float32)
                continue
            tall = own_ref.shape[0] * HEAD_SIZE // ref.shape[1]
            for half in range(count // tall):
                target[half * tall : (half + 1) * tall, :] = ref[
                    ref.shape[0] - tall :, head_lanes(head * count // tall + half)
                ].astype(jnp.float32)

    for member in range(members):
        tile = slice(member * 8, (member + 1) * 8)
        for copy in copies[member]:
            copy.wait()
        scores = jnp.concatenate(
            [
                dot_last(
                    query_held[head, tile, :].astype(jnp.bfloat16),
                    k_ref[member, :, head_lanes(head)],
                )
                for head in range(heads)
            ],
            axis=0,
        )
        valid = lax.broadcasted_iota(jnp.int32, scores.shape, 1) < lengths[here * members + member]
        weight = jnp.where(valid, capped_weight(scores), 0.0)
        total = jnp.broadcast_to(jnp.sum(weight, axis=1, keepdims=True), (heads * 8, LANES))
        weight = weight.astype(jnp.bfloat16)
        for head in range(heads):
            rows = slice(head * 8, (head + 1) * 8)
            sums[head, tile, :] = jnp.dot(
                weight[rows],
                v_ref[member, :, head_lanes(head)],
                preferred_element_type=jnp.float32,
            )
            totals[head, tile, :] = total[rows]

    for mask in range(parts):
        for head in range(near):
            at = slice(head * count, (head + 1) * count)
            index = (here ^ mask) * near + head
            if mask == 0:
                outs[0][at, :] = sums[index]
                outs[1][at, :] = totals[index]
            else:
                outs[mask + 1][at, :] = sums[index].astype(jnp.bfloat16)
        if mask > 0:
            both = jnp.concatenate(
                [totals[(here ^ mask) * near + head] for head in range(near)], axis=0
            )
            packed[0:1, :] = both.T[0:1]
            outs[mask + 1][near * count :, :] = split_rows(packed[...])


def suffix_attention(place, lengths, own, received, cache_keys, cache_values, tokens_after):
    parts = len(received) + 1
    members, slots, columns = cache_keys.shape
    heads = columns // HEAD_SIZE
    count = heads // parts * members * 8
    outs = [shape((count, HEAD_SIZE), jnp.float32)] * 2 + [
        shape((count + 16, HEAD_SIZE), jnp.bfloat16)
    ] * (parts - 1)
    far = pl.BlockSpec(memory_space=pl.ANY)
    return call(
        functools.partial(suffix_kernel, parts),
        (place, lengths),
        (own, *received, cache_keys, cache_values, *tokens_after),
        outs,
        [whole(own)]
        + [whole(a) for a in received]
        + [far, far]
        + [corner(a) for a in tokens_after],
        [whole(a) for a in outs],
        (1,),
        [
            pltpu.VMEM((heads, members * 8, HEAD_SIZE), jnp.float32),
            pltpu.VMEM(cache_keys.shape, cache_keys.dtype),
            pltpu.VMEM(cache_values.shape, cache_values.dtype),
            pltpu.VMEM((heads, members * 8, HEAD_SIZE), jnp.float32),
            pltpu.VMEM((heads, members * 8, HEAD_SIZE), jnp.float32),
            pltpu.VMEM((8, LANES), jnp.float32),
            pltpu.SemaphoreType.DMA((members, 2)),
        ],
        4 * members * 8 * slots * columns,
        4 * members * slots * columns,
        SUFFIX_LIMIT,
    )


def mix_kernel(parts, far, place, sum_ref, total_ref, *refs):
    prompt, refs = refs[:far], refs[far:]
    near_sum, near_total, *suffix = refs[: parts + 1]
    out_ref, sums, totals = refs[parts + 1 :]
    count = sum_ref.shape[0]
    rows = out_ref.shape[0]
    heads = count // (2 * rows)
    total = sum_ref[...]
    for ref in prompt:
        total = total + ref[:count, :].astype(jnp.float32)
    sums[...] = total
    for block in range(count // LANES):
        at = slice(block * LANES, (block + 1) * LANES)
        total = total_ref[at, :]
        for ref in prompt:
            total = total + down_rows(joined_row(ref[count:, :], block))
        totals[at, :] = total
    share = 2 * rows // parts
    for mask in range(parts):
        if mask == 0:
            near, near_weight = near_sum[...], near_total[...]
        else:
            ref = suffix[mask - 1]
            near = ref[: count // parts, :].astype(jnp.float32)
            near_weight = down_rows(joined_row(ref[count // parts : count // parts + 16, :], 0))
        for head in range(heads):
            first = pl.multiple_of(head * 2 * rows + (place[0] ^ mask) * share, share)
            at = pl.ds(first, share)
            local = slice(head * share, (head + 1) * share)
            sums[at, :] = sums[at, :] + near[local]
            totals[at, :] = totals[at, :] + near_weight[local]
    mixed = sums[...] / totals[...]
    for head in range(heads):
        tiles = mixed[head * 2 * rows : (head + 1) * 2 * rows].reshape(rows // 8, 2, 8, HEAD_SIZE)
        for member, part in enumerate(interleave(tiles[:, 0], tiles[:, 1])):
            at = (2 * head + member) * HEAD_SIZE
            out_ref[:, at : at + HEAD_SIZE] = part.reshape(rows, HEAD_SIZE).astype(jnp.bfloat16)


def mix(place, sums, totals, prompt, suffix, rows):
    count = sums.shape[0]
    operands = (sums, totals, *prompt, *suffix)
    out = shape((rows, count // rows * HEAD_SIZE), jnp.bfloat16)
    return call(
        functools.partial(mix_kernel, len(suffix) - 1, len(prompt)),
        (place,),
        operands,
        out,
        [whole(a) for a in operands],
        whole(out),
        (1,),
        [pltpu.VMEM((count, HEAD_SIZE), jnp.float32)] * 2,
        10 * count * HEAD_SIZE,
        8 * count * HEAD_SIZE,
    )


def output_kernel(masks, started, place, *refs):
    inputs, refs = refs[: len(masks)], refs[len(masks) :]
    w_ref, out_ref = refs[0], refs[-1]
    step = pl.program_id(0)
    for index, ref in enumerate(inputs):

        @pl.when(step == index)
        def _():
            term = jnp.dot(ref[...], w_ref[...], preferred_element_type=jnp.float32)
            if index > 0:
                out_ref[...] += term
            elif started:
                out_ref[...] = refs[1][...] + term
            else:
                out_ref[...] = term


def output_projection(place, masks, mixed, weights, started=None):
    rows, depth = mixed[0].shape
    width = weights.shape[1]
    chosen = pl.BlockSpec(
        (depth, width), lambda i, p: (p[0] ^ (i + masks[0]), 0)
    )
    out = shape((rows, width), jnp.float32)
    more = () if started is None else (started,)
    return call(
        functools.partial(output_kernel, masks, started is not None),
        (place,),
        (*mixed, weights, *more),
        out,
        [whole(a) for a in mixed] + [chosen] + [whole(a) for a in more],
        whole(out),
        (len(masks),),
        [],
        2 * len(masks) * rows * depth * width,
        2 * len(masks) * depth * width,
    )


def attended_kernel(place, here_ref, there_ref, out_ref, squares_ref):
    attended = here_ref[...] + there_ref[...]
    out_ref[...] = attended
    total = jnp.sum(attended * attended, axis=1, keepdims=True)
    squares_ref[...] = jnp.broadcast_to(total, (total.shape[0], LANES)).T[:8]


def attended_squares(place, here, there):
    outs = [shape(here.shape, jnp.float32), shape((8, here.shape[0]), jnp.float32)]
    return call(
        attended_kernel,
        (place,),
        (here, there),
        outs,
        [whole(here), whole(there)],
        [whole(a) for a in outs],
        (1,),
        [],
        4 * here.size,
        12 * here.size,
    )


def finish_kernel(place, x_ref, attended_ref, gain_ref, *refs):
    *squares, out_ref = refs
    total = squares[0][0:1, :]
    for ref in squares[1:]:
        total = total + ref[0:1, :]
    inverse = lax.rsqrt(down_rows(total) / MODEL_WIDTH + EPSILON)
    for at in range(0, x_ref.shape[2], LANES):
        lanes = slice(at, at + LANES)
        branch = attended_ref[:, lanes] * inverse * gain_ref[lanes].reshape(1, LANES)
        x = x_ref[:, :, lanes].astype(jnp.float32)
        out_ref[:, :, lanes] = (x + branch.reshape(x.shape)).astype(jnp.bfloat16)


def finish(place, x, attended, gain, squares):
    operands = (x, attended, gain, *squares)
    out = shape(x.shape, jnp.bfloat16)
    return call(
        finish_kernel,
        (place,),
        operands,
        out,
        [whole(a) for a in operands],
        whole(out),
        (1,),
        [],
        4 * x.size,
        8 * x.size,
    )


def by_heads(
    hidden_in,
    pre_gain,
    w_query,
    key_projection,
    value_projection,
    w_out,
    post_gain,
    prompt_keys,
    prompt_values,
    suffix_key_cache,
    suffix_value_cache,
    suffix_len,
):
    group_rows, steps, _ = hidden_in.shape
    rows = group_rows * steps
    parts = lax.axis_size("prefix")
    groups = lax.axis_size("prefill")
    prompt_total = prompt_keys.shape[0] * groups * parts
    place = lax.axis_index("prefix").astype(jnp.int32).reshape(1)
    near = range(1, parts)
    far = range(1, groups)

    def swapped(arrays, axis):
        pairs = list(enumerate(arrays, start=1))
        moved = {m: paired(a, axis, m) for m, a in pairs[-1:] + pairs[:-1]}
        return [moved[m] for m, _ in pairs]

    *sent, own, squares, scaled = query_projection(
        place, hidden_in, pre_gain, w_query, prompt_keys, prompt_values, parts
    )
    received = swapped(sent[parts - 1 :], "prefix")
    blocks = swapped(sent[: parts - 1], "prefix")

    positions = (
        (prompt_total + suffix_len[:, None] + jnp.arange(steps, dtype=jnp.int32)[None, :])
        .reshape(-1)
        .astype(jnp.float32)
    )
    half = HEAD_SIZE // 2
    freq = 10000.0 ** (-2.0 * jnp.arange(half, dtype=jnp.float32) / HEAD_SIZE)
    angle = positions[:, None] * freq[None, :]
    cosine, sine = jnp.cos(angle), jnp.sin(angle)
    cosine = jnp.concatenate([cosine, cosine], axis=1)
    sine = jnp.concatenate([-sine, sine], axis=1)

    queries, *split_queries, inverse = query_rope(
        place, own, received, squares, cosine, sine, parts
    )
    held_back = lax.optimization_barrier((queries, blocks[0]))[0]
    far_queries = [paired(held_back if m == 1 else queries, "prefill", m) for m in far]
    pair, *sent = pair_projection(
        place, scaled, key_projection, value_projection, split_queries[1:]
    )
    returned = swapped(sent, "prefix")
    first = prompt_first(place, far_queries, prompt_keys, prompt_values, blocks[:1], parts)
    packed = [
        prompt_last(place, q, blocks[1:], first[2 * i : 2 * i + 2])
        for i, q in enumerate(far_queries)
    ]
    prompt_results = swapped(packed, "prefill")
    near_sums, near_totals, *sent = suffix_attention(
        place,
        suffix_len,
        split_queries[0],
        returned,
        suffix_key_cache,
        suffix_value_cache,
        packed,
    )
    suffix = [near_sums, near_totals, *swapped(sent, "prefix")]
    sums, totals = own_sums(
        place,
        queries,
        prompt_keys,
        prompt_values,
        blocks,
        pair,
        returned,
        (inverse, cosine, sine),
        [near_totals],
    )
    mixed = mix(place, sums, totals, prompt_results, suffix, rows)
    others = [paired(mixed, "prefix", m) for m in near]
    head_terms = output_projection(place, (0,), [mixed], w_out)
    head_terms = output_projection(place, tuple(near), others, w_out, head_terms)
    attended, squares = attended_squares(place, head_terms, paired(head_terms, "tensor", 1))
    squares = [squares] + [paired(squares, "prefix", m) for m in near]
    return finish(place, hidden_in, attended, post_gain, squares)


def heads_divide(mesh):
    sizes = [mesh.shape[name] for name in ("prefill", "prefix", "tensor")]
    key_heads = QUERY_HEADS // 2 // sizes[2]
    return key_heads == 2 * sizes[1] and sizes[1] == 4 and sizes[2] == 2 and sizes[0] in (2, 4)


def solution(mesh):
    return jax.shard_map(
        by_heads if heads_divide(mesh) else per_device,
        mesh=mesh,
        in_specs=(
            P("prefill", None, "prefix"),
            P("prefix"),
            P("prefix", "tensor"),
            P("prefix", "tensor"),
            P("prefix", "tensor"),
            P("tensor", "prefix"),
            P("prefix"),
            P(("prefill", "prefix"), "tensor"),
            P(("prefill", "prefix"), "tensor"),
            P(("prefill", "prefix"), None, "tensor"),
            P(("prefill", "prefix"), None, "tensor"),
            P("prefill"),
        ),
        out_specs=P("prefill", None, "prefix"),
        check_vma=False,
    )
```

```python
import functools

import jax
import jax.numpy as jnp
from jax import lax
from jax.experimental import pallas as pl
from jax.experimental.pallas import tpu as pltpu
from jax.sharding import PartitionSpec as P

MODEL_WIDTH = 4608
QUERY_HEADS = 32
HEAD_SIZE = 128


SOFTCAP = 50.0
EPSILON = 1e-06
LOG2_E = 1.4426950408889634
LANES = 128
VMEM_LIMIT = 24 * 1024 * 1024
FIRST_LIMIT = 59 * 1024 * 1024
ROPE_LIMIT = 24 * 1024 * 1024
PAIR_LIMIT = 24 * 1024 * 1024
SUFFIX_LIMIT = 24 * 1024 * 1024
QUERY_SCALE = (MODEL_WIDTH // QUERY_HEADS) ** (-0.5)


def apply_rotation(values, token_positions, heads):
    width = values.shape[1] // heads
    half = width // 2
    freq = 10000.0 ** (-2.0 * jnp.arange(half, dtype=jnp.float32) / width)
    angle = token_positions[:, None] * freq[None, :]
    cosine = jnp.cos(angle)[:, None, :]
    sine = jnp.sin(angle)[:, None, :]
    parts = values.reshape(values.shape[0], heads, width)
    first = parts[:, :, :half]
    second = parts[:, :, half:]
    turned = jnp.concatenate(
        [first * cosine - second * sine, second * cosine + first * sine], axis=2
    )
    return turned.reshape(values.shape[0], heads * width)


def soft_weight(scores):
    return jnp.exp(SOFTCAP * jnp.tanh(scores / SOFTCAP))


def shared_attention(queries, keys, values):
    count = queries.shape[0]
    kv_heads = keys.shape[1] // HEAD_SIZE
    heads_per_group = queries.shape[1] // keys.shape[1]
    grouped = queries.reshape(count, kv_heads, heads_per_group, HEAD_SIZE)
    key_head_rows = keys.reshape(keys.shape[0], kv_heads, HEAD_SIZE)
    value_head_rows = values.reshape(values.shape[0], kv_heads, HEAD_SIZE)
    scores = jnp.einsum(
        "nkgd,mkd->nkgm", grouped, key_head_rows, preferred_element_type=jnp.float32
    )
    weights = soft_weight(scores)
    totals = jnp.sum(weights, axis=3).reshape(count, kv_heads * heads_per_group)
    summed = jnp.einsum(
        "nkgm,mkd->nkgd",
        weights.astype(jnp.bfloat16),
        value_head_rows,
        preferred_element_type=jnp.float32,
    )
    return (summed.reshape(count, kv_heads * heads_per_group * HEAD_SIZE), totals)


def own_attention(
    queries, cached_key_rows, cached_value_rows, latest_keys, latest_values, lengths, steps
):
    members = lengths.shape[0]
    slots = cached_key_rows.shape[1]
    kv_heads = cached_key_rows.shape[2] // HEAD_SIZE
    heads_per_group = queries.shape[1] // cached_key_rows.shape[2]
    grouped = queries.reshape(members, steps, kv_heads, heads_per_group, HEAD_SIZE)
    cache_k = cached_key_rows.reshape(members, slots, kv_heads, HEAD_SIZE)
    cache_v = cached_value_rows.reshape(members, slots, kv_heads, HEAD_SIZE)
    valid = jnp.arange(slots, dtype=jnp.int32)[None, :] < lengths[:, None]
    cache_scores = jnp.einsum(
        "rjkgd,rmkd->rjkgm", grouped, cache_k, preferred_element_type=jnp.float32
    )
    cache_weights = jnp.where(valid[:, None, None, None, :], soft_weight(cache_scores), 0.0)
    new_k = latest_keys.reshape(members, steps, kv_heads, HEAD_SIZE)
    new_v = latest_values.reshape(members, steps, kv_heads, HEAD_SIZE)
    step_ids = jnp.arange(steps, dtype=jnp.int32)
    causal = step_ids[None, :] <= step_ids[:, None]
    new_scores = jnp.einsum("rjkgd,rikd->rjkgi", grouped, new_k, preferred_element_type=jnp.float32)
    new_weights = jnp.where(causal[None, :, None, None, :], soft_weight(new_scores), 0.0)
    totals = jnp.sum(cache_weights, axis=4) + jnp.sum(new_weights, axis=4)
    summed = jnp.einsum(
        "rjkgm,rmkd->rjkgd",
        cache_weights.astype(jnp.bfloat16),
        cache_v,
        preferred_element_type=jnp.float32,
    )
    summed = summed + jnp.einsum(
        "rjkgi,rikd->rjkgd",
        new_weights.astype(jnp.bfloat16),
        new_v,
        preferred_element_type=jnp.float32,
    )
    flat_rows = members * steps
    return (
        summed.reshape(flat_rows, kv_heads * heads_per_group * HEAD_SIZE),
        totals.reshape(flat_rows, kv_heads * heads_per_group),
    )


def per_device(
    hidden_in,
    pre_gain,
    w_query,
    key_projection,
    value_projection,
    w_out,
    post_gain,
    prompt_keys,
    prompt_values,
    suffix_key_cache,
    suffix_value_cache,
    suffix_len,
):
    group_rows, steps, local_width = hidden_in.shape
    members = suffix_key_cache.shape[0]
    query_cols = w_query.shape[1]
    kv_cols = key_projection.shape[1]
    heads = query_cols // HEAD_SIZE
    kv_heads = kv_cols // HEAD_SIZE
    own_count = members * steps
    prompt_total = prompt_keys.shape[0] * lax.axis_size("prefill") * lax.axis_size("prefix")
    signal = hidden_in.astype(jnp.float32).reshape(group_rows * steps, local_width)
    squares = lax.psum(jnp.sum(signal * signal, axis=1), "prefix")
    normed = (signal * lax.rsqrt(squares[:, None] / MODEL_WIDTH + EPSILON) * pre_gain).astype(
        jnp.bfloat16
    )
    weights_all = jnp.concatenate([w_query, key_projection, value_projection], axis=1)
    step_ids = jnp.arange(steps, dtype=jnp.int32)
    group_positions = (
        (prompt_total + suffix_len[:, None] + step_ids[None, :]).reshape(-1).astype(jnp.float32)
    )
    first_row = lax.axis_index("prefix") * members
    own_lengths = lax.dynamic_slice_in_dim(suffix_len, first_row, members)
    own_positions = lax.dynamic_slice_in_dim(group_positions, first_row * steps, own_count)
    scale = (MODEL_WIDTH // QUERY_HEADS) ** (-0.5)
    own_proj = lax.psum_scatter(
        jnp.dot(normed, weights_all, preferred_element_type=jnp.float32),
        "prefix",
        scatter_dimension=0,
        tiled=True,
    )
    own_queries = (apply_rotation(own_proj[:, :query_cols], own_positions, heads) * scale).astype(
        jnp.bfloat16
    )
    group_queries = lax.all_gather(own_queries, "prefix", axis=0, tiled=True)
    latest_keys = apply_rotation(
        own_proj[:, query_cols : query_cols + kv_cols], own_positions, kv_heads
    ).astype(jnp.bfloat16)
    latest_values = own_proj[:, query_cols + kv_cols :].astype(jnp.bfloat16)
    summed, totals = shared_attention(
        group_queries,
        lax.all_gather(prompt_keys, "prefill", axis=0, tiled=True),
        lax.all_gather(prompt_values, "prefill", axis=0, tiled=True),
    )
    prompt_totals = totals
    far_sums, far_totals = (
        lax.psum_scatter(summed, "prefix", scatter_dimension=0, tiled=True),
        lax.psum_scatter(prompt_totals, "prefix", scatter_dimension=0, tiled=True),
    )
    near_sums, near_totals = own_attention(
        own_queries,
        suffix_key_cache,
        suffix_value_cache,
        latest_keys,
        latest_values,
        own_lengths,
        steps,
    )
    totals = far_totals + near_totals
    sums = (far_sums + near_sums).reshape(own_count, heads, HEAD_SIZE)
    mixed = (sums / totals[:, :, None]).reshape(own_count, query_cols).astype(jnp.bfloat16)
    head_terms = jnp.dot(
        lax.all_gather(mixed, "prefix", axis=0, tiled=True),
        w_out,
        preferred_element_type=jnp.float32,
    )
    attended = lax.psum(head_terms, "tensor")
    out_squares = lax.psum(jnp.sum(attended * attended, axis=1), "prefix")
    branch = attended * lax.rsqrt(out_squares[:, None] / MODEL_WIDTH + EPSILON) * post_gain
    return (signal + branch).astype(jnp.bfloat16).reshape(group_rows, steps, local_width)


def paired(values, axis, mask):
    size = lax.axis_size(axis)
    return lax.ppermute(values, axis, [(i, i ^ mask) for i in range(size)])


def call(
    kernel,
    prefetch,
    operands,
    out_shape,
    in_specs,
    out_specs,
    grid,
    scratch,
    flops,
    moved,
    limit=VMEM_LIMIT,
):
    return pl.pallas_call(
        kernel,
        out_shape=out_shape,
        grid_spec=pltpu.PrefetchScalarGridSpec(
            num_scalar_prefetch=len(prefetch),
            grid=grid,
            in_specs=in_specs,
            out_specs=out_specs,
            scratch_shapes=scratch,
        ),
        compiler_params=pltpu.CompilerParams(vmem_limit_bytes=limit),
        cost_estimate=pl.CostEstimate(flops=flops, bytes_accessed=moved, transcendentals=0),
    )(*prefetch, *operands)


def whole(array):
    rank = len(array.shape)
    return pl.BlockSpec(array.shape, lambda *_: (0,) * rank)


def corner(array):
    rank = len(array.shape)
    return pl.BlockSpec(
        (1,) * (rank - 2) + (32 // array.dtype.itemsize, LANES), lambda *_: (0,) * rank
    )


def shape(dims, dtype):
    return jax.ShapeDtypeStruct(dims, dtype)


def dot_last(left, right):
    return lax.dot_general(left, right, (((1,), (1,)), ((), ())), preferred_element_type=jnp.float32)


def dot_first(left, right):
    return lax.dot_general(left, right, (((0,), (0,)), ((), ())), preferred_element_type=jnp.float32)


def capped_weight(scores):
    return jnp.exp2(jnp.tanh(scores * (1.0 / SOFTCAP)) * (SOFTCAP * LOG2_E))


def split_rows(rows):
    high = rows.astype(jnp.bfloat16).astype(jnp.float32)
    return jnp.concatenate([high, rows - high], axis=0).astype(jnp.bfloat16)


def joined_row(block, index):
    pair = block.astype(jnp.float32)
    return pair[index : index + 1] + pair[8 + index : 9 + index]


def down_rows(row):
    return jnp.broadcast_to(row, (LANES, row.shape[1])).T


def lower_half(tiles):
    return lax.broadcasted_iota(jnp.int32, tiles.shape, 1) < tiles.shape[1] // 2


def interleave(first, second):
    low = lower_half(first)
    half = first.shape[1] // 2
    return (
        jnp.where(low, first, pltpu.roll(second, half, 1)),
        jnp.where(low, pltpu.roll(first, half, 1), second),
    )


def rotated(values, cosine, sine):
    return values * cosine + pltpu.roll(values, HEAD_SIZE // 2, 1) * sine


def gain_row(ref):
    return ref[...].reshape(1, ref.shape[0])


def copy_in(source, target, semaphore):
    copy = pltpu.make_async_copy(source, target, semaphore)
    copy.start()
    return copy


def block_of(place, mask, width):
    return pl.ds(pl.multiple_of((place[0] ^ mask) * width, width), width)


def query_projection_kernel(place, gain_ref, x_hbm, w_hbm, *refs):
    *sent, own_ref, scaled_ref, x_ref, w_ref, semaphores = refs
    rows, columns = scaled_ref.shape[0], own_ref.shape[1]
    masks = (*range(1, len(sent) + 1), 0)
    x_copy = copy_in(x_hbm, x_ref, semaphores.at[len(masks)])
    w_copies = [
        copy_in(w_hbm.at[:, block_of(place, mask, columns)], w_ref.at[mask], semaphores.at[mask])
        for mask in masks
    ]
    x_copy.wait()
    x = x_ref[...].astype(jnp.float32).reshape(rows, x_ref.shape[2])
    scaled_ref[...] = (x * gain_row(gain_ref)).astype(jnp.bfloat16)
    total = jnp.sum(x * x, axis=1, keepdims=True)
    across = jnp.broadcast_to(total, (rows, LANES)).T[:8]
    own_ref[rows:, :] = jnp.zeros((8, columns), jnp.float32)
    own_ref[rows:, :rows] = across
    tail = split_rows(across)
    for ref in sent:
        ref[rows:, :] = jnp.zeros((16, ref.shape[1]), jnp.bfloat16)
        ref[rows:, :rows] = tail
    for mask, copy, ref in zip(masks, w_copies, (*sent, own_ref)):
        copy.wait()
        product = jnp.dot(scaled_ref[...], w_ref[mask], preferred_element_type=jnp.float32)
        ref[:rows, :] = product.astype(ref.dtype)


def query_projection(place, x, gain, weights, parts):
    members, steps, width = x.shape
    rows = members * steps
    columns = weights.shape[1] // parts
    outs = [shape((rows + 16, columns), jnp.bfloat16)] * (parts - 1) + [
        shape((rows + 8, columns), jnp.float32),
        shape((rows, width), jnp.bfloat16),
    ]
    far = pl.BlockSpec(memory_space=pl.ANY)
    return call(
        query_projection_kernel,
        (place,),
        (gain, x, weights),
        outs,
        [whole(gain), far, far],
        [whole(a) for a in outs],
        (1,),
        [
            pltpu.VMEM(x.shape, x.dtype),
            pltpu.VMEM((parts, width, columns), weights.dtype),
            pltpu.SemaphoreType.DMA((parts + 1,)),
        ],
        2 * rows * width * weights.shape[1],
        2 * width * weights.shape[1],
        FIRST_LIMIT,
    )


def owner_columns_kernel(place, keys_hbm, values_hbm, *refs):
    *outs, semaphores = refs
    width = outs[0].shape[1] // 2
    copies = [
        copy_in(
            source.at[:, block_of(place, mask, width)],
            ref.at[:, half * width : (half + 1) * width],
            semaphores.at[mask - 1, half],
        )
        for mask, ref in enumerate(outs, start=1)
        for half, source in enumerate((keys_hbm, values_hbm))
    ]
    for copy in copies:
        copy.wait()


def owner_columns(place, keys, values, parts):
    tokens = keys.shape[0]
    columns = keys.shape[1] // parts
    outs = [shape((tokens, 2 * columns), keys.dtype)] * (parts - 1)
    far = pl.BlockSpec(memory_space=pl.ANY)
    return call(
        owner_columns_kernel,
        (place,),
        (keys, values),
        outs,
        [far, far],
        [whole(a) for a in outs],
        (1,),
        [pltpu.SemaphoreType.DMA((parts - 1, 2))],
        20000000000,
        8 * (parts - 1) * tokens * columns,
    )


def pair_projection_kernel(place, scaled_ref, k_hbm, v_hbm, *refs):
    parts = len(refs) // 2
    queries, (own_ref, *outs), (w_ref, semaphores) = (
        refs[: parts - 1],
        refs[parts - 1 : 2 * parts - 1],
        refs[2 * parts - 1 :],
    )
    rows, width = own_ref.shape
    columns = width // 2
    masks = (*range(1, parts), 0)
    copies = {}
    for mask in masks:
        at = block_of(place, mask, columns)
        copies[mask] = [
            copy_in(
                source.at[:, at],
                w_ref.at[mask, :, half * columns : (half + 1) * columns],
                semaphores.at[mask, half],
            )
            for half, source in enumerate((k_hbm, v_hbm))
        ]
    for ref, out_ref in zip(queries, outs):
        tall = out_ref.shape[0] - rows
        for piece in range(ref.shape[0] // tall):
            out_ref[rows:, head_lanes(piece)] = ref[piece * tall : (piece + 1) * tall, :]
    for mask in masks:
        for copy in copies[mask]:
            copy.wait()
        term = jnp.dot(scaled_ref[...], w_ref[mask], preferred_element_type=jnp.float32)
        target = outs[mask - 1] if mask else own_ref
        target[:rows, :] = term.astype(target.dtype)


def pair_projection(place, scaled, key_weights, value_weights, queries):
    parts = len(queries) + 1
    rows, width = scaled.shape
    columns = key_weights.shape[1] // parts
    far = pl.BlockSpec(memory_space=pl.ANY)
    tall = queries[0].size // (2 * columns)
    outs = [shape((rows, 2 * columns), jnp.float32)] + [
        shape((rows + tall, 2 * columns), jnp.bfloat16)
    ] * (parts - 1)
    return call(
        pair_projection_kernel,
        (place,),
        (scaled, key_weights, value_weights, *queries),
        outs,
        [whole(scaled), far, far] + [whole(a) for a in queries],
        [whole(a) for a in outs],
        (1,),
        [
            pltpu.VMEM((parts, width, 2 * columns), key_weights.dtype),
            pltpu.SemaphoreType.DMA((parts, 2)),
        ],
        4 * rows * width * key_weights.shape[1],
        4 * width * key_weights.shape[1],
        PAIR_LIMIT,
    )


def paired_heads(values, cosine, sine):
    tiles = [
        rotated(values[:, at : at + HEAD_SIZE], cosine, sine).reshape(-1, 8, HEAD_SIZE)
        for at in (0, HEAD_SIZE)
    ]
    return jnp.stack(interleave(*tiles), axis=1).reshape(2 * values.shape[0], HEAD_SIZE)


def query_rope_kernel(parts, place, own_ref, *refs):
    received, refs = refs[: parts - 1], refs[parts - 1 :]
    cos_ref, sin_ref, query_ref, *suffix_refs, inverse_ref, held = refs
    rows, columns = cos_ref.shape[0], own_ref.shape[1]
    squares = own_ref[rows : rows + 1, :rows]
    total = own_ref[:rows, :]
    for ref in received:
        squares = squares + joined_row(ref[rows:, :rows], 0)
        total = total + ref[:rows, :].astype(jnp.float32)
    inverse = lax.rsqrt(down_rows(squares) / MODEL_WIDTH + EPSILON)
    inverse_ref[...] = inverse
    cosine = cos_ref[...] * inverse * QUERY_SCALE
    sine = sin_ref[...] * inverse * QUERY_SCALE
    pair = 2 * HEAD_SIZE
    share = 2 * rows // parts
    for head in range(columns // pair):
        at = slice(head * 2 * rows, (head + 1) * 2 * rows)
        held[...] = paired_heads(total[:, head * pair : (head + 1) * pair], cosine, sine)
        query_ref[at, :] = held[...].astype(jnp.bfloat16)
        for mask, ref in enumerate(suffix_refs):
            ref[head * share : (head + 1) * share, :] = held[
                block_of(place, mask, share), :
            ].astype(jnp.bfloat16)


def query_rope(place, own, received, cosine, sine, parts):
    rows, columns = cosine.shape[0], own.shape[1]
    count = rows * columns // HEAD_SIZE
    operands = (own, *received, cosine, sine)
    outs = (
        [shape((count, HEAD_SIZE), jnp.bfloat16)]
        + [shape((count // parts, HEAD_SIZE), jnp.bfloat16)] * parts
        + [shape((rows, LANES), jnp.float32)]
    )
    return call(
        functools.partial(query_rope_kernel, parts),
        (place,),
        operands,
        outs,
        [whole(a) for a in operands],
        [whole(a) for a in outs],
        (1,),
        [pltpu.VMEM((2 * rows, HEAD_SIZE), jnp.float32)],
        10000000000,
        12 * rows * columns,
        ROPE_LIMIT,
    )


def attend(query, pairs):
    result = None
    for key, value in pairs:
        weight = capped_weight(dot_last(query, key)).astype(jnp.bfloat16)
        ones = jnp.ones((value.shape[0], LANES), jnp.bfloat16)
        term = jnp.dot(
            weight, jnp.concatenate([value, ones], axis=1), preferred_element_type=jnp.float32
        )
        result = term if result is None else result + term
    return result


def total_rows(totals):
    return [totals[at : at + LANES].T[0:1] for at in range(0, totals.shape[0], LANES)]


def head_lanes(head):
    return slice(head * HEAD_SIZE, (head + 1) * HEAD_SIZE)


def received_pair(ref, head, heads):
    return ref[:, head_lanes(head)], ref[:, head_lanes(heads + head)]


def prompt_first_kernel(chunks, place, *refs):
    queries, refs = refs[:chunks], refs[chunks:]
    k_ref, v_ref, *received = refs[: -2 * chunks]
    outs = refs[-2 * chunks :]
    heads = k_ref.shape[1] // HEAD_SIZE
    count = queries[0].shape[0] // heads
    for index, query_ref in enumerate(queries):
        sum_ref, total_ref = outs[2 * index : 2 * index + 2]
        for head in range(heads):
            at = slice(head * count, (head + 1) * count)
            pairs = [(k_ref[:, head_lanes(head)], v_ref[:, head_lanes(head)])]
            pairs += [received_pair(ref, head, heads) for ref in received]
            result = attend(query_ref[at, :], pairs)
            sum_ref[at, :] = result[:, :HEAD_SIZE]
            total_ref[at, :] = result[:, HEAD_SIZE:]


def prompt_first(place, queries, prompt_keys, prompt_values, received, parts):
    tokens = prompt_keys.shape[0]
    chosen = pl.BlockSpec((tokens, prompt_keys.shape[1] // parts), lambda i, p: (0, p[0]))
    outs = [shape(queries[0].shape, jnp.float32)] * (2 * len(queries))
    return call(
        functools.partial(prompt_first_kernel, len(queries)),
        (place,),
        (*queries, prompt_keys, prompt_values, *received),
        outs,
        [whole(a) for a in queries] + [chosen, chosen] + [whole(a) for a in received],
        [whole(a) for a in outs],
        (1,),
        [],
        6 * len(queries) * queries[0].size * (len(received) + 1) * tokens,
        4 * parts * tokens * HEAD_SIZE,
    )


def prompt_last_kernel(place, q_ref, *refs):
    *blocks, sum_ref, total_ref, out_ref, held = refs
    heads = blocks[0].shape[1] // (2 * HEAD_SIZE)
    count = q_ref.shape[0] // heads
    held[...] = jnp.zeros(held.shape, jnp.float32)
    for head in range(heads):
        at = slice(head * count, (head + 1) * count)
        result = attend(q_ref[at, :], [received_pair(ref, head, heads) for ref in blocks])
        out_ref[at, :] = (sum_ref[at, :] + result[:, :HEAD_SIZE]).astype(jnp.bfloat16)
        for row, values in enumerate(total_rows(total_ref[at, :] + result[:, HEAD_SIZE:])):
            to = head * count // LANES + row
            held[to : to + 1, :] = values
    out_ref[heads * count :, :] = split_rows(held[...])


def prompt_last(place, queries, blocks, first):
    out = shape((queries.shape[0] + 16, HEAD_SIZE), jnp.bfloat16)
    operands = (queries, *blocks, *first)
    return call(
        prompt_last_kernel,
        (place,),
        operands,
        out,
        [whole(a) for a in operands],
        whole(out),
        (1,),
        [pltpu.VMEM((8, LANES), jnp.float32)],
        6 * queries.size * len(blocks) * blocks[0].shape[0],
        2 * len(blocks) * blocks[0].size,
    )


def own_kernel(parts, place, q_ref, k_ref, v_ref, *refs):
    blocks, refs = refs[: parts - 1], refs[parts - 1 :]
    pair_ref, refs = refs[0], refs[1:]
    received, refs = refs[: parts - 1], refs[parts - 1 :]
    inverse_ref, cos_ref, sin_ref = refs[:3]
    sum_ref, total_ref = refs[-2:]
    heads = k_ref.shape[1] // HEAD_SIZE
    count = q_ref.shape[0] // heads
    rows = inverse_ref.shape[0]
    inverse = inverse_ref[...]
    cosine = cos_ref[...] * inverse
    sine = sin_ref[...] * inverse

    def new_terms(index):
        term = pair_ref[:, head_lanes(index)]
        for ref in received:
            term = term + ref[:rows, head_lanes(index)].astype(jnp.float32)
        return term

    query_row = lax.broadcasted_iota(jnp.int32, (count, rows), 0)
    key_row = lax.broadcasted_iota(jnp.int32, (count, rows), 1)
    same = query_row // 8 == key_row // 4
    valid = same & (key_row % 4 <= query_row % 4)
    ones = jnp.ones((rows, LANES), jnp.bfloat16)
    for head in range(heads):
        at = slice(head * count, (head + 1) * count)
        query = q_ref[at, :]
        key = rotated(new_terms(head), cosine, sine)
        value = new_terms(heads + head) * inverse
        weight = capped_weight(dot_last(query, key.astype(jnp.bfloat16)))
        weight = jnp.where(valid, weight, 0.0).astype(jnp.bfloat16)
        result = jnp.dot(
            weight,
            jnp.concatenate([value.astype(jnp.bfloat16), ones], axis=1),
            preferred_element_type=jnp.float32,
        )
        pairs = [(k_ref[:, head_lanes(head)], v_ref[:, head_lanes(head)])]
        pairs += [received_pair(ref, head, heads) for ref in blocks]
        result = result + attend(query, pairs)
        sum_ref[at, :] = result[:, :HEAD_SIZE]
        total_ref[at, :] = result[:, HEAD_SIZE:]


def own_sums(
    place, queries, prompt_keys, prompt_values, blocks, pair, received, tables, tokens_after
):
    parts = len(blocks) + 1
    tokens = prompt_keys.shape[0]
    chosen = pl.BlockSpec((tokens, prompt_keys.shape[1] // parts), lambda i, p: (0, p[0]))
    operands = (*blocks, pair, *received, *tables)
    outs = [shape(queries.shape, jnp.float32)] * 2
    return call(
        functools.partial(own_kernel, parts),
        (place,),
        (queries, prompt_keys, prompt_values, *operands, *tokens_after),
        outs,
        [whole(queries), chosen, chosen]
        + [whole(a) for a in operands]
        + [corner(a) for a in tokens_after],
        [whole(a) for a in outs],
        (1,),
        [],
        6 * queries.size * parts * tokens,
        4 * parts * tokens * HEAD_SIZE,
    )


def diagonal(first, second):
    zero = jnp.zeros(first.shape, first.dtype)
    return jnp.concatenate(
        [
            jnp.concatenate([first, zero], axis=1),
            jnp.concatenate([zero, second], axis=1),
        ],
        axis=0,
    )


def suffix_kernel(parts, place, lengths, own_ref, *refs):
    received, (k_ref, v_ref), refs = (
        refs[: parts - 1],
        refs[parts - 1 : parts + 1],
        refs[-(parts + 5) :],
    )
    outs, refs = refs[: parts + 1], refs[parts + 1 :]
    query_held, sums, totals, packed = refs
    members, slots, columns = k_ref.shape
    heads = columns // HEAD_SIZE
    near = heads // parts
    here = place[0]
    packed[...] = jnp.zeros(packed.shape, jnp.float32)
    count = members * 8
    for mask, ref in enumerate((own_ref, *received)):
        for head in range(near):
            target = query_held.at[(here ^ mask) * near + head]
            if mask == 0:
                target[...] = ref[head * count : (head + 1) * count, :].astype(jnp.float32)
                continue
            tall = own_ref.shape[0] * HEAD_SIZE // ref.shape[1]
            for half in range(count // tall):
                target[half * tall : (half + 1) * tall, :] = ref[
                    ref.shape[0] - tall :, head_lanes(head * count // tall + half)
                ].astype(jnp.float32)

    for member in range(members):
        tile = slice(member * 8, (member + 1) * 8)
        pairs = [slice(at, at + 2 * HEAD_SIZE) for at in range(0, columns, 2 * HEAD_SIZE)]
        scores = jnp.concatenate(
            [
                dot_last(
                    diagonal(
                        query_held[2 * index, tile, :], query_held[2 * index + 1, tile, :]
                    ).astype(jnp.bfloat16),
                    k_ref[member, :, lanes],
                )
                for index, lanes in enumerate(pairs)
            ],
            axis=0,
        )
        valid = lax.broadcasted_iota(jnp.int32, scores.shape, 1) < lengths[here * members + member]
        weight = jnp.where(valid, capped_weight(scores), 0.0)
        total = jnp.broadcast_to(jnp.sum(weight, axis=1, keepdims=True), (heads * 8, LANES))
        weight = weight.astype(jnp.bfloat16)
        for index, lanes in enumerate(pairs):
            result = jnp.dot(
                weight[16 * index : 16 * (index + 1)],
                v_ref[member, :, lanes],
                preferred_element_type=jnp.float32,
            )
            sums[2 * index, tile, :] = result[:8, :HEAD_SIZE]
            sums[2 * index + 1, tile, :] = result[8:, HEAD_SIZE:]
        for head in range(heads):
            totals[head, tile, :] = total[head * 8 : (head + 1) * 8]

    for mask in range(parts):
        for head in range(near):
            at = slice(head * count, (head + 1) * count)
            index = (here ^ mask) * near + head
            if mask == 0:
                outs[0][at, :] = sums[index]
                outs[1][at, :] = totals[index]
            else:
                outs[mask + 1][at, :] = sums[index].astype(jnp.bfloat16)
        if mask > 0:
            both = jnp.concatenate(
                [totals[(here ^ mask) * near + head] for head in range(near)], axis=0
            )
            packed[0:1, :] = both.T[0:1]
            outs[mask + 1][near * count :, :] = split_rows(packed[...])


def suffix_attention(place, lengths, own, received, cache_keys, cache_values, tokens_after):
    parts = len(received) + 1
    members, slots, columns = cache_keys.shape
    heads = columns // HEAD_SIZE
    count = heads // parts * members * 8
    outs = [shape((count, HEAD_SIZE), jnp.float32)] * 2 + [
        shape((count + 16, HEAD_SIZE), jnp.bfloat16)
    ] * (parts - 1)
    far = pl.BlockSpec(memory_space=pltpu.VMEM)
    return call(
        functools.partial(suffix_kernel, parts),
        (place, lengths),
        (own, *received, cache_keys, cache_values, *tokens_after),
        outs,
        [whole(own)]
        + [whole(a) for a in received]
        + [far, far]
        + [corner(a) for a in tokens_after],
        [whole(a) for a in outs],
        (1,),
        [
            pltpu.VMEM((heads, members * 8, HEAD_SIZE), jnp.float32),
            pltpu.VMEM((heads, members * 8, HEAD_SIZE), jnp.float32),
            pltpu.VMEM((heads, members * 8, HEAD_SIZE), jnp.float32),
            pltpu.VMEM((8, LANES), jnp.float32),
        ],
        4 * members * 8 * slots * columns,
        4 * members * slots * columns,
        SUFFIX_LIMIT,
    )


def mix_kernel(parts, far, place, sum_ref, total_ref, *refs):
    prompt, refs = refs[:far], refs[far:]
    near_sum, near_total, *suffix = refs[: parts + 1]
    out_ref, sums, totals = refs[parts + 1 :]
    count = sum_ref.shape[0]
    rows = out_ref.shape[0]
    heads = count // (2 * rows)
    total = sum_ref[...]
    for ref in prompt:
        total = total + ref[:count, :].astype(jnp.float32)
    sums[...] = total
    for block in range(count // LANES):
        at = slice(block * LANES, (block + 1) * LANES)
        total = total_ref[at, :]
        for ref in prompt:
            total = total + down_rows(joined_row(ref[count:, :], block))
        totals[at, :] = total
    share = 2 * rows // parts
    for mask in range(parts):
        if mask == 0:
            near, near_weight = near_sum[...], near_total[...]
        else:
            ref = suffix[mask - 1]
            near = ref[: count // parts, :].astype(jnp.float32)
            near_weight = down_rows(joined_row(ref[count // parts : count // parts + 16, :], 0))
        for head in range(heads):
            first = pl.multiple_of(head * 2 * rows + (place[0] ^ mask) * share, share)
            at = pl.ds(first, share)
            local = slice(head * share, (head + 1) * share)
            sums[at, :] = sums[at, :] + near[local]
            totals[at, :] = totals[at, :] + near_weight[local]
    mixed = sums[...] / totals[...]
    for head in range(heads):
        tiles = mixed[head * 2 * rows : (head + 1) * 2 * rows].reshape(rows // 8, 2, 8, HEAD_SIZE)
        for member, part in enumerate(interleave(tiles[:, 0], tiles[:, 1])):
            at = (2 * head + member) * HEAD_SIZE
            out_ref[:, at : at + HEAD_SIZE] = part.reshape(rows, HEAD_SIZE).astype(jnp.bfloat16)


def mix(place, sums, totals, prompt, suffix, rows):
    count = sums.shape[0]
    operands = (sums, totals, *prompt, *suffix)
    out = shape((rows, count // rows * HEAD_SIZE), jnp.bfloat16)
    return call(
        functools.partial(mix_kernel, len(suffix) - 1, len(prompt)),
        (place,),
        operands,
        out,
        [whole(a) for a in operands],
        whole(out),
        (1,),
        [pltpu.VMEM((count, HEAD_SIZE), jnp.float32)] * 2,
        10 * count * HEAD_SIZE,
        8 * count * HEAD_SIZE,
    )


def output_kernel(masks, started, place, *refs):
    inputs, refs = refs[: len(masks)], refs[len(masks) :]
    w_ref, out_ref = refs[0], refs[-1]
    step = pl.program_id(0)
    for index, ref in enumerate(inputs):

        @pl.when(step == index)
        def _():
            term = jnp.dot(ref[...], w_ref[...], preferred_element_type=jnp.float32)
            if index > 0:
                out_ref[...] += term
            elif started:
                out_ref[...] = refs[1][...] + term
            else:
                out_ref[...] = term


def output_projection(place, masks, mixed, weights, started=None):
    rows, depth = mixed[0].shape
    width = weights.shape[1]
    chosen = pl.BlockSpec(
        (depth, width), lambda i, p: (p[0] ^ (i + masks[0]), 0)
    )
    out = shape((rows, width), jnp.float32)
    more = () if started is None else (started,)
    return call(
        functools.partial(output_kernel, masks, started is not None),
        (place,),
        (*mixed, weights, *more),
        out,
        [whole(a) for a in mixed] + [chosen] + [whole(a) for a in more],
        whole(out),
        (len(masks),),
        [],
        2 * len(masks) * rows * depth * width,
        2 * len(masks) * depth * width,
    )


def attended_kernel(place, here_ref, there_ref, out_ref, squares_ref):
    attended = here_ref[...] + there_ref[...].astype(jnp.float32)
    out_ref[...] = attended
    total = jnp.sum(attended * attended, axis=1, keepdims=True)
    squares_ref[...] = jnp.broadcast_to(total, (total.shape[0], LANES)).T[:8]


def attended_squares(place, here, there):
    outs = [shape(here.shape, jnp.float32), shape((8, here.shape[0]), jnp.float32)]
    return call(
        attended_kernel,
        (place,),
        (here, there),
        outs,
        [whole(here), whole(there)],
        [whole(a) for a in outs],
        (1,),
        [],
        4 * here.size,
        12 * here.size,
    )


def finish_kernel(place, x_ref, attended_ref, gain_ref, *refs):
    *squares, out_ref = refs
    total = squares[0][0:1, :]
    for ref in squares[1:]:
        total = total + ref[0:1, :]
    inverse = lax.rsqrt(down_rows(total) / MODEL_WIDTH + EPSILON)
    for at in range(0, x_ref.shape[2], LANES):
        lanes = slice(at, at + LANES)
        branch = attended_ref[:, lanes] * inverse * gain_ref[lanes].reshape(1, LANES)
        x = x_ref[:, :, lanes].astype(jnp.float32)
        out_ref[:, :, lanes] = (x + branch.reshape(x.shape)).astype(jnp.bfloat16)


def finish(place, x, attended, gain, squares):
    operands = (x, attended, gain, *squares)
    out = shape(x.shape, jnp.bfloat16)
    return call(
        finish_kernel,
        (place,),
        operands,
        out,
        [whole(a) for a in operands],
        whole(out),
        (1,),
        [],
        4 * x.size,
        8 * x.size,
    )


def by_heads(
    hidden_in,
    pre_gain,
    w_query,
    key_projection,
    value_projection,
    w_out,
    post_gain,
    prompt_keys,
    prompt_values,
    suffix_key_cache,
    suffix_value_cache,
    suffix_len,
):
    group_rows, steps, _ = hidden_in.shape
    rows = group_rows * steps
    parts = lax.axis_size("prefix")
    groups = lax.axis_size("prefill")
    prompt_total = prompt_keys.shape[0] * groups * parts
    place = lax.axis_index("prefix").astype(jnp.int32).reshape(1)
    near = range(1, parts)
    far = range(1, groups)

    def swapped(arrays, axis):
        pairs = list(enumerate(arrays, start=1))
        moved = {m: paired(a, axis, m) for m, a in pairs[-1:] + pairs[:-1]}
        return [moved[m] for m, _ in pairs]

    *sent, own, scaled = query_projection(place, hidden_in, pre_gain, w_query, parts)
    received = swapped(sent, "prefix")
    keys, values, _ = lax.optimization_barrier((prompt_keys, prompt_values, own))
    blocks = swapped(owner_columns(place, keys, values, parts), "prefix")

    positions = (
        (prompt_total + suffix_len[:, None] + jnp.arange(steps, dtype=jnp.int32)[None, :])
        .reshape(-1)
        .astype(jnp.float32)
    )
    half = HEAD_SIZE // 2
    freq = 10000.0 ** (-2.0 * jnp.arange(half, dtype=jnp.float32) / HEAD_SIZE)
    angle = positions[:, None] * freq[None, :]
    cosine, sine = jnp.cos(angle), jnp.sin(angle)
    cosine = jnp.concatenate([cosine, cosine], axis=1)
    sine = jnp.concatenate([-sine, sine], axis=1)

    queries, *split_queries, inverse = query_rope(
        place, own, received, cosine, sine, parts
    )
    pair, *sent = pair_projection(
        place, scaled, key_projection, value_projection, split_queries[1:]
    )
    held_back = lax.optimization_barrier((queries, blocks[0], pair))[0]
    far_queries = [paired(held_back if m == 1 else queries, "prefill", m) for m in far]
    returned = swapped(sent, "prefix")
    first = prompt_first(place, far_queries, prompt_keys, prompt_values, blocks[:1], parts)
    packed = [
        prompt_last(place, q, blocks[1:], first[2 * i : 2 * i + 2])
        for i, q in enumerate(far_queries)
    ]
    prompt_results = swapped(packed, "prefill")
    near_sums, near_totals, *sent = suffix_attention(
        place,
        suffix_len,
        split_queries[0],
        returned,
        suffix_key_cache,
        suffix_value_cache,
        packed,
    )
    suffix = [near_sums, near_totals, *swapped(sent, "prefix")]
    sums, totals = own_sums(
        place,
        queries,
        prompt_keys,
        prompt_values,
        blocks,
        pair,
        returned,
        (inverse, cosine, sine),
        [near_totals, prompt_results[2]],
    )
    mixed = mix(place, sums, totals, prompt_results, suffix, rows)
    others = [paired(mixed, "prefix", m) for m in near]
    head_terms = output_projection(place, (0,), [mixed], w_out)
    for mask, other in zip(near, others):
        head_terms = output_projection(place, (mask,), [other], w_out, head_terms)
    attended, squares = attended_squares(
        place, head_terms, paired(head_terms.astype(jnp.bfloat16), "tensor", 1)
    )
    squares = [squares] + [paired(squares, "prefix", m) for m in near]
    return finish(place, hidden_in, attended, post_gain, squares)


def heads_divide(mesh):
    sizes = [mesh.shape[name] for name in ("prefill", "prefix", "tensor")]
    key_heads = QUERY_HEADS // 2 // sizes[2]
    return key_heads == 2 * sizes[1] and sizes[1] == 4 and sizes[2] == 2 and sizes[0] in (2, 4)


def solution(mesh):
    return jax.shard_map(
        by_heads if heads_divide(mesh) else per_device,
        mesh=mesh,
        in_specs=(
            P("prefill", None, "prefix"),
            P("prefix"),
            P("prefix", "tensor"),
            P("prefix", "tensor"),
            P("prefix", "tensor"),
            P("tensor", "prefix"),
            P("prefix"),
            P(("prefill", "prefix"), "tensor"),
            P(("prefill", "prefix"), "tensor"),
            P(("prefill", "prefix"), None, "tensor"),
            P(("prefill", "prefix"), None, "tensor"),
            P("prefill"),
        ),
        out_specs=P("prefill", None, "prefix"),
        check_vma=False,
    )
```

```python
import functools

import jax
import jax.numpy as jnp
from jax import lax
from jax.experimental import pallas as pl
from jax.experimental.pallas import tpu as pltpu
from jax.sharding import PartitionSpec as P

MODEL_WIDTH = 4608
QUERY_HEADS = 32
HEAD_SIZE = 128


SOFTCAP = 50.0
EPSILON = 1e-06
LOG2_E = 1.4426950408889634
LANES = 128
VMEM_LIMIT = 24 * 1024 * 1024
FIRST_LIMIT = 59 * 1024 * 1024
ROPE_LIMIT = 24 * 1024 * 1024
PAIR_LIMIT = 24 * 1024 * 1024
SUFFIX_LIMIT = 24 * 1024 * 1024
QUERY_SCALE = (MODEL_WIDTH // QUERY_HEADS) ** (-0.5)


def apply_rotation(values, token_positions, heads):
    width = values.shape[1] // heads
    half = width // 2
    freq = 10000.0 ** (-2.0 * jnp.arange(half, dtype=jnp.float32) / width)
    angle = token_positions[:, None] * freq[None, :]
    cosine = jnp.cos(angle)[:, None, :]
    sine = jnp.sin(angle)[:, None, :]
    parts = values.reshape(values.shape[0], heads, width)
    first = parts[:, :, :half]
    second = parts[:, :, half:]
    turned = jnp.concatenate(
        [first * cosine - second * sine, second * cosine + first * sine], axis=2
    )
    return turned.reshape(values.shape[0], heads * width)


def soft_weight(scores):
    return jnp.exp(SOFTCAP * jnp.tanh(scores / SOFTCAP))


def shared_attention(queries, keys, values):
    count = queries.shape[0]
    kv_heads = keys.shape[1] // HEAD_SIZE
    heads_per_group = queries.shape[1] // keys.shape[1]
    grouped = queries.reshape(count, kv_heads, heads_per_group, HEAD_SIZE)
    key_head_rows = keys.reshape(keys.shape[0], kv_heads, HEAD_SIZE)
    value_head_rows = values.reshape(values.shape[0], kv_heads, HEAD_SIZE)
    scores = jnp.einsum(
        "nkgd,mkd->nkgm", grouped, key_head_rows, preferred_element_type=jnp.float32
    )
    weights = soft_weight(scores)
    totals = jnp.sum(weights, axis=3).reshape(count, kv_heads * heads_per_group)
    summed = jnp.einsum(
        "nkgm,mkd->nkgd",
        weights.astype(jnp.bfloat16),
        value_head_rows,
        preferred_element_type=jnp.float32,
    )
    return (summed.reshape(count, kv_heads * heads_per_group * HEAD_SIZE), totals)


def own_attention(
    queries, cached_key_rows, cached_value_rows, latest_keys, latest_values, lengths, steps
):
    members = lengths.shape[0]
    slots = cached_key_rows.shape[1]
    kv_heads = cached_key_rows.shape[2] // HEAD_SIZE
    heads_per_group = queries.shape[1] // cached_key_rows.shape[2]
    grouped = queries.reshape(members, steps, kv_heads, heads_per_group, HEAD_SIZE)
    cache_k = cached_key_rows.reshape(members, slots, kv_heads, HEAD_SIZE)
    cache_v = cached_value_rows.reshape(members, slots, kv_heads, HEAD_SIZE)
    valid = jnp.arange(slots, dtype=jnp.int32)[None, :] < lengths[:, None]
    cache_scores = jnp.einsum(
        "rjkgd,rmkd->rjkgm", grouped, cache_k, preferred_element_type=jnp.float32
    )
    cache_weights = jnp.where(valid[:, None, None, None, :], soft_weight(cache_scores), 0.0)
    new_k = latest_keys.reshape(members, steps, kv_heads, HEAD_SIZE)
    new_v = latest_values.reshape(members, steps, kv_heads, HEAD_SIZE)
    step_ids = jnp.arange(steps, dtype=jnp.int32)
    causal = step_ids[None, :] <= step_ids[:, None]
    new_scores = jnp.einsum("rjkgd,rikd->rjkgi", grouped, new_k, preferred_element_type=jnp.float32)
    new_weights = jnp.where(causal[None, :, None, None, :], soft_weight(new_scores), 0.0)
    totals = jnp.sum(cache_weights, axis=4) + jnp.sum(new_weights, axis=4)
    summed = jnp.einsum(
        "rjkgm,rmkd->rjkgd",
        cache_weights.astype(jnp.bfloat16),
        cache_v,
        preferred_element_type=jnp.float32,
    )
    summed = summed + jnp.einsum(
        "rjkgi,rikd->rjkgd",
        new_weights.astype(jnp.bfloat16),
        new_v,
        preferred_element_type=jnp.float32,
    )
    flat_rows = members * steps
    return (
        summed.reshape(flat_rows, kv_heads * heads_per_group * HEAD_SIZE),
        totals.reshape(flat_rows, kv_heads * heads_per_group),
    )


def per_device(
    hidden_in,
    pre_gain,
    w_query,
    key_projection,
    value_projection,
    w_out,
    post_gain,
    prompt_keys,
    prompt_values,
    suffix_key_cache,
    suffix_value_cache,
    suffix_len,
):
    group_rows, steps, local_width = hidden_in.shape
    members = suffix_key_cache.shape[0]
    query_cols = w_query.shape[1]
    kv_cols = key_projection.shape[1]
    heads = query_cols // HEAD_SIZE
    kv_heads = kv_cols // HEAD_SIZE
    own_count = members * steps
    prompt_total = prompt_keys.shape[0] * lax.axis_size("prefill") * lax.axis_size("prefix")
    signal = hidden_in.astype(jnp.float32).reshape(group_rows * steps, local_width)
    squares = lax.psum(jnp.sum(signal * signal, axis=1), "prefix")
    normed = (signal * lax.rsqrt(squares[:, None] / MODEL_WIDTH + EPSILON) * pre_gain).astype(
        jnp.bfloat16
    )
    weights_all = jnp.concatenate([w_query, key_projection, value_projection], axis=1)
    step_ids = jnp.arange(steps, dtype=jnp.int32)
    group_positions = (
        (prompt_total + suffix_len[:, None] + step_ids[None, :]).reshape(-1).astype(jnp.float32)
    )
    first_row = lax.axis_index("prefix") * members
    own_lengths = lax.dynamic_slice_in_dim(suffix_len, first_row, members)
    own_positions = lax.dynamic_slice_in_dim(group_positions, first_row * steps, own_count)
    scale = (MODEL_WIDTH // QUERY_HEADS) ** (-0.5)
    own_proj = lax.psum_scatter(
        jnp.dot(normed, weights_all, preferred_element_type=jnp.float32),
        "prefix",
        scatter_dimension=0,
        tiled=True,
    )
    own_queries = (apply_rotation(own_proj[:, :query_cols], own_positions, heads) * scale).astype(
        jnp.bfloat16
    )
    group_queries = lax.all_gather(own_queries, "prefix", axis=0, tiled=True)
    latest_keys = apply_rotation(
        own_proj[:, query_cols : query_cols + kv_cols], own_positions, kv_heads
    ).astype(jnp.bfloat16)
    latest_values = own_proj[:, query_cols + kv_cols :].astype(jnp.bfloat16)
    summed, totals = shared_attention(
        group_queries,
        lax.all_gather(prompt_keys, "prefill", axis=0, tiled=True),
        lax.all_gather(prompt_values, "prefill", axis=0, tiled=True),
    )
    prompt_totals = totals
    far_sums, far_totals = (
        lax.psum_scatter(summed, "prefix", scatter_dimension=0, tiled=True),
        lax.psum_scatter(prompt_totals, "prefix", scatter_dimension=0, tiled=True),
    )
    near_sums, near_totals = own_attention(
        own_queries,
        suffix_key_cache,
        suffix_value_cache,
        latest_keys,
        latest_values,
        own_lengths,
        steps,
    )
    totals = far_totals + near_totals
    sums = (far_sums + near_sums).reshape(own_count, heads, HEAD_SIZE)
    mixed = (sums / totals[:, :, None]).reshape(own_count, query_cols).astype(jnp.bfloat16)
    head_terms = jnp.dot(
        lax.all_gather(mixed, "prefix", axis=0, tiled=True),
        w_out,
        preferred_element_type=jnp.float32,
    )
    attended = lax.psum(head_terms, "tensor")
    out_squares = lax.psum(jnp.sum(attended * attended, axis=1), "prefix")
    branch = attended * lax.rsqrt(out_squares[:, None] / MODEL_WIDTH + EPSILON) * post_gain
    return (signal + branch).astype(jnp.bfloat16).reshape(group_rows, steps, local_width)


def paired(values, axis, mask):
    size = lax.axis_size(axis)
    return lax.ppermute(values, axis, [(i, i ^ mask) for i in range(size)])


def call(
    kernel,
    prefetch,
    operands,
    out_shape,
    in_specs,
    out_specs,
    grid,
    scratch,
    flops,
    moved,
    limit=VMEM_LIMIT,
):
    return pl.pallas_call(
        kernel,
        out_shape=out_shape,
        grid_spec=pltpu.PrefetchScalarGridSpec(
            num_scalar_prefetch=len(prefetch),
            grid=grid,
            in_specs=in_specs,
            out_specs=out_specs,
            scratch_shapes=scratch,
        ),
        compiler_params=pltpu.CompilerParams(vmem_limit_bytes=limit),
        cost_estimate=pl.CostEstimate(flops=flops, bytes_accessed=moved, transcendentals=0),
    )(*prefetch, *operands)


def whole(array):
    rank = len(array.shape)
    return pl.BlockSpec(array.shape, lambda *_: (0,) * rank)


def corner(array):
    rank = len(array.shape)
    return pl.BlockSpec(
        (1,) * (rank - 2) + (32 // array.dtype.itemsize, LANES), lambda *_: (0,) * rank
    )


def shape(dims, dtype):
    return jax.ShapeDtypeStruct(dims, dtype)


def dot_last(left, right):
    return lax.dot_general(left, right, (((1,), (1,)), ((), ())), preferred_element_type=jnp.float32)


def dot_first(left, right):
    return lax.dot_general(left, right, (((0,), (0,)), ((), ())), preferred_element_type=jnp.float32)


def capped_weight(scores):
    return jnp.exp2(jnp.tanh(scores * (1.0 / SOFTCAP)) * (SOFTCAP * LOG2_E))


def split_rows(rows):
    high = rows.astype(jnp.bfloat16).astype(jnp.float32)
    return jnp.concatenate([high, rows - high], axis=0).astype(jnp.bfloat16)


def joined_row(block, index):
    pair = block.astype(jnp.float32)
    return pair[index : index + 1] + pair[8 + index : 9 + index]


def down_rows(row):
    return jnp.broadcast_to(row, (LANES, row.shape[1])).T


def lower_half(tiles):
    return lax.broadcasted_iota(jnp.int32, tiles.shape, 1) < tiles.shape[1] // 2


def interleave(first, second):
    low = lower_half(first)
    half = first.shape[1] // 2
    return (
        jnp.where(low, first, pltpu.roll(second, half, 1)),
        jnp.where(low, pltpu.roll(first, half, 1), second),
    )


def rotated(values, cosine, sine):
    return values * cosine + pltpu.roll(values, HEAD_SIZE // 2, 1) * sine


def gain_row(ref):
    return ref[...].reshape(1, ref.shape[0])


def copy_in(source, target, semaphore):
    copy = pltpu.make_async_copy(source, target, semaphore)
    copy.start()
    return copy


def block_of(place, mask, width):
    return pl.ds(pl.multiple_of((place[0] ^ mask) * width, width), width)


def query_projection_kernel(place, gain_ref, x_hbm, w_hbm, *refs):
    *sent, own_ref, scaled_ref, x_ref, w_ref, semaphores = refs
    rows, columns = scaled_ref.shape[0], own_ref.shape[1]
    masks = (*range(1, len(sent) + 1), 0)
    x_copy = copy_in(x_hbm, x_ref, semaphores.at[len(masks)])
    w_copies = [
        copy_in(w_hbm.at[:, block_of(place, mask, columns)], w_ref.at[mask], semaphores.at[mask])
        for mask in masks
    ]
    x_copy.wait()
    x = x_ref[...].astype(jnp.float32).reshape(rows, x_ref.shape[2])
    scaled_ref[...] = (x * gain_row(gain_ref)).astype(jnp.bfloat16)
    total = jnp.sum(x * x, axis=1, keepdims=True)
    across = jnp.broadcast_to(total, (rows, LANES)).T[:8]
    own_ref[rows:, :] = jnp.zeros((8, columns), jnp.float32)
    own_ref[rows:, :rows] = across
    tail = split_rows(across)
    for ref in sent:
        ref[ref.shape[0] - 16 :, :] = tail
    for mask, copy, ref in zip(masks, w_copies, (*sent, own_ref)):
        copy.wait()
        product = jnp.dot(scaled_ref[...], w_ref[mask], preferred_element_type=jnp.float32)
        if mask == 0:
            own_ref[:rows, :] = product
            continue
        for head in range(columns // HEAD_SIZE):
            at = slice(head * rows, (head + 1) * rows)
            ref[at, :] = product[:, head_lanes(head)].astype(ref.dtype)


def query_projection(place, x, gain, weights, parts):
    members, steps, width = x.shape
    rows = members * steps
    columns = weights.shape[1] // parts
    outs = [shape((rows * columns // HEAD_SIZE + 16, HEAD_SIZE), jnp.bfloat16)] * (parts - 1) + [
        shape((rows + 8, columns), jnp.float32),
        shape((rows, width), jnp.bfloat16),
    ]
    far = pl.BlockSpec(memory_space=pl.ANY)
    return call(
        query_projection_kernel,
        (place,),
        (gain, x, weights),
        outs,
        [whole(gain), far, far],
        [whole(a) for a in outs],
        (1,),
        [
            pltpu.VMEM(x.shape, x.dtype),
            pltpu.VMEM((parts, width, columns), weights.dtype),
            pltpu.SemaphoreType.DMA((parts + 1,)),
        ],
        2 * rows * width * weights.shape[1],
        2 * width * weights.shape[1],
        FIRST_LIMIT,
    )


def owner_columns_kernel(place, keys_hbm, values_hbm, *refs):
    *outs, semaphores = refs
    width = outs[0].shape[1] // 2
    copies = [
        copy_in(
            source.at[:, block_of(place, mask, width)],
            ref.at[:, half * width : (half + 1) * width],
            semaphores.at[mask - 1, half],
        )
        for mask, ref in enumerate(outs, start=1)
        for half, source in enumerate((keys_hbm, values_hbm))
    ]
    for copy in copies:
        copy.wait()


def owner_columns(place, keys, values, parts):
    tokens = keys.shape[0]
    columns = keys.shape[1] // parts
    outs = [shape((tokens, 2 * columns), keys.dtype)] * (parts - 1)
    far = pl.BlockSpec(memory_space=pl.ANY)
    return call(
        owner_columns_kernel,
        (place,),
        (keys, values),
        outs,
        [far, far],
        [whole(a) for a in outs],
        (1,),
        [pltpu.SemaphoreType.DMA((parts - 1, 2))],
        20000000000,
        8 * (parts - 1) * tokens * columns,
    )


def pair_projection_kernel(place, scaled_ref, k_hbm, v_hbm, *refs):
    parts = len(refs) // 2
    queries, (own_ref, *outs), (w_ref, semaphores) = (
        refs[: parts - 1],
        refs[parts - 1 : 2 * parts - 1],
        refs[2 * parts - 1 :],
    )
    rows, width = own_ref.shape
    columns = width // 2
    masks = (*range(1, parts), 0)
    copies = {}
    for mask in masks:
        at = block_of(place, mask, columns)
        copies[mask] = [
            copy_in(
                source.at[:, at],
                w_ref.at[mask, :, half * columns : (half + 1) * columns],
                semaphores.at[mask, half],
            )
            for half, source in enumerate((k_hbm, v_hbm))
        ]
    for ref, out_ref in zip(queries, outs):
        tall = out_ref.shape[0] - rows
        for piece in range(ref.shape[0] // tall):
            out_ref[rows:, head_lanes(piece)] = ref[piece * tall : (piece + 1) * tall, :]
    for mask in masks:
        for copy in copies[mask]:
            copy.wait()
        term = jnp.dot(scaled_ref[...], w_ref[mask], preferred_element_type=jnp.float32)
        target = outs[mask - 1] if mask else own_ref
        target[:rows, :] = term.astype(target.dtype)


def pair_projection(place, scaled, key_weights, value_weights, queries):
    parts = len(queries) + 1
    rows, width = scaled.shape
    columns = key_weights.shape[1] // parts
    far = pl.BlockSpec(memory_space=pl.ANY)
    tall = queries[0].size // (2 * columns)
    outs = [shape((rows, 2 * columns), jnp.float32)] + [
        shape((rows + tall, 2 * columns), jnp.bfloat16)
    ] * (parts - 1)
    return call(
        pair_projection_kernel,
        (place,),
        (scaled, key_weights, value_weights, *queries),
        outs,
        [whole(scaled), far, far] + [whole(a) for a in queries],
        [whole(a) for a in outs],
        (1,),
        [
            pltpu.VMEM((parts, width, 2 * columns), key_weights.dtype),
            pltpu.SemaphoreType.DMA((parts, 2)),
        ],
        4 * rows * width * key_weights.shape[1],
        4 * width * key_weights.shape[1],
        PAIR_LIMIT,
    )


def paired_heads(values, cosine, sine):
    tiles = [
        rotated(values[:, at : at + HEAD_SIZE], cosine, sine).reshape(-1, 8, HEAD_SIZE)
        for at in (0, HEAD_SIZE)
    ]
    return jnp.stack(interleave(*tiles), axis=1).reshape(2 * values.shape[0], HEAD_SIZE)


def query_rope_kernel(parts, place, own_ref, *refs):
    received, refs = refs[: parts - 1], refs[parts - 1 :]
    cos_ref, sin_ref, query_ref, *suffix_refs, inverse_ref, held = refs
    rows, columns = cos_ref.shape[0], own_ref.shape[1]
    squares = own_ref[rows : rows + 1, :rows]
    for ref in received:
        squares = squares + joined_row(ref[ref.shape[0] - 16 :, :], 0)
    inverse = lax.rsqrt(down_rows(squares) / MODEL_WIDTH + EPSILON)
    inverse_ref[...] = inverse
    cosine = cos_ref[...] * inverse * QUERY_SCALE
    sine = sin_ref[...] * inverse * QUERY_SCALE
    pair = 2 * HEAD_SIZE
    share = 2 * rows // parts
    for head in range(columns // pair):
        at = slice(head * 2 * rows, (head + 1) * 2 * rows)
        totals = []
        for index in (2 * head, 2 * head + 1):
            total = own_ref[:rows, head_lanes(index)]
            for ref in received:
                total = total + ref[index * rows : (index + 1) * rows, :].astype(jnp.float32)
            totals.append(total)
        held[...] = paired_heads(jnp.concatenate(totals, axis=1), cosine, sine)
        query_ref[at, :] = held[...].astype(jnp.bfloat16)
        for mask, ref in enumerate(suffix_refs):
            ref[head * share : (head + 1) * share, :] = held[
                block_of(place, mask, share), :
            ].astype(jnp.bfloat16)


def query_rope(place, own, received, cosine, sine, parts):
    rows, columns = cosine.shape[0], own.shape[1]
    count = rows * columns // HEAD_SIZE
    operands = (own, *received, cosine, sine)
    outs = (
        [shape((count, HEAD_SIZE), jnp.bfloat16)]
        + [shape((count // parts, HEAD_SIZE), jnp.bfloat16)] * parts
        + [shape((rows, LANES), jnp.float32)]
    )
    return call(
        functools.partial(query_rope_kernel, parts),
        (place,),
        operands,
        outs,
        [whole(a) for a in operands],
        [whole(a) for a in outs],
        (1,),
        [pltpu.VMEM((2 * rows, HEAD_SIZE), jnp.float32)],
        10000000000,
        12 * rows * columns,
        ROPE_LIMIT,
    )


def attend(query, pairs):
    result = None
    for key, value in pairs:
        weight = capped_weight(dot_last(query, key)).astype(jnp.bfloat16)
        ones = jnp.ones((value.shape[0], LANES), jnp.bfloat16)
        term = jnp.dot(
            weight, jnp.concatenate([value, ones], axis=1), preferred_element_type=jnp.float32
        )
        result = term if result is None else result + term
    return result


def total_rows(totals):
    return [totals[at : at + LANES].T[0:1] for at in range(0, totals.shape[0], LANES)]


def head_lanes(head):
    return slice(head * HEAD_SIZE, (head + 1) * HEAD_SIZE)


def received_pair(ref, head, heads):
    return ref[:, head_lanes(head)], ref[:, head_lanes(heads + head)]


def prompt_first_kernel(chunks, place, *refs):
    queries, refs = refs[:chunks], refs[chunks:]
    k_ref, v_ref, *received = refs[: -2 * chunks]
    outs = refs[-2 * chunks :]
    heads = k_ref.shape[1] // HEAD_SIZE
    count = queries[0].shape[0] // heads
    for index, query_ref in enumerate(queries):
        sum_ref, total_ref = outs[2 * index : 2 * index + 2]
        for head in range(heads):
            at = slice(head * count, (head + 1) * count)
            pairs = [(k_ref[:, head_lanes(head)], v_ref[:, head_lanes(head)])]
            pairs += [received_pair(ref, head, heads) for ref in received]
            result = attend(query_ref[at, :], pairs)
            sum_ref[at, :] = result[:, :HEAD_SIZE]
            total_ref[at, :] = result[:, HEAD_SIZE:]


def prompt_first(place, queries, prompt_keys, prompt_values, received, parts):
    tokens = prompt_keys.shape[0]
    chosen = pl.BlockSpec((tokens, prompt_keys.shape[1] // parts), lambda i, p: (0, p[0]))
    outs = [shape(queries[0].shape, jnp.float32)] * (2 * len(queries))
    return call(
        functools.partial(prompt_first_kernel, len(queries)),
        (place,),
        (*queries, prompt_keys, prompt_values, *received),
        outs,
        [whole(a) for a in queries] + [chosen, chosen] + [whole(a) for a in received],
        [whole(a) for a in outs],
        (1,),
        [],
        6 * len(queries) * queries[0].size * (len(received) + 1) * tokens,
        4 * parts * tokens * HEAD_SIZE,
    )


def prompt_last_kernel(place, q_ref, *refs):
    *blocks, sum_ref, total_ref, out_ref, held = refs
    heads = blocks[0].shape[1] // (2 * HEAD_SIZE)
    count = q_ref.shape[0] // heads
    held[...] = jnp.zeros(held.shape, jnp.float32)
    for head in range(heads):
        at = slice(head * count, (head + 1) * count)
        result = attend(q_ref[at, :], [received_pair(ref, head, heads) for ref in blocks])
        out_ref[at, :] = (sum_ref[at, :] + result[:, :HEAD_SIZE]).astype(jnp.bfloat16)
        for row, values in enumerate(total_rows(total_ref[at, :] + result[:, HEAD_SIZE:])):
            to = head * count // LANES + row
            held[to : to + 1, :] = values
    out_ref[heads * count :, :] = split_rows(held[...])


def prompt_last(place, queries, blocks, first):
    out = shape((queries.shape[0] + 16, HEAD_SIZE), jnp.bfloat16)
    operands = (queries, *blocks, *first)
    return call(
        prompt_last_kernel,
        (place,),
        operands,
        out,
        [whole(a) for a in operands],
        whole(out),
        (1,),
        [pltpu.VMEM((8, LANES), jnp.float32)],
        6 * queries.size * len(blocks) * blocks[0].shape[0],
        2 * len(blocks) * blocks[0].size,
    )


def own_kernel(parts, place, q_ref, k_ref, v_ref, *refs):
    blocks, refs = refs[: parts - 1], refs[parts - 1 :]
    pair_ref, refs = refs[0], refs[1:]
    received, refs = refs[: parts - 1], refs[parts - 1 :]
    inverse_ref, cos_ref, sin_ref = refs[:3]
    sum_ref, total_ref = refs[-2:]
    heads = k_ref.shape[1] // HEAD_SIZE
    count = q_ref.shape[0] // heads
    rows = inverse_ref.shape[0]
    inverse = inverse_ref[...]
    cosine = cos_ref[...] * inverse
    sine = sin_ref[...] * inverse

    def new_terms(index):
        term = pair_ref[:, head_lanes(index)]
        for ref in received:
            term = term + ref[:rows, head_lanes(index)].astype(jnp.float32)
        return term

    query_row = lax.broadcasted_iota(jnp.int32, (count, rows), 0)
    key_row = lax.broadcasted_iota(jnp.int32, (count, rows), 1)
    same = query_row // 8 == key_row // 4
    valid = same & (key_row % 4 <= query_row % 4)
    ones = jnp.ones((rows, LANES), jnp.bfloat16)
    for head in range(heads):
        at = slice(head * count, (head + 1) * count)
        query = q_ref[at, :]
        key = rotated(new_terms(head), cosine, sine)
        value = new_terms(heads + head) * inverse
        weight = capped_weight(dot_last(query, key.astype(jnp.bfloat16)))
        weight = jnp.where(valid, weight, 0.0).astype(jnp.bfloat16)
        result = jnp.dot(
            weight,
            jnp.concatenate([value.astype(jnp.bfloat16), ones], axis=1),
            preferred_element_type=jnp.float32,
        )
        pairs = [(k_ref[:, head_lanes(head)], v_ref[:, head_lanes(head)])]
        pairs += [received_pair(ref, head, heads) for ref in blocks]
        result = result + attend(query, pairs)
        sum_ref[at, :] = result[:, :HEAD_SIZE]
        total_ref[at, :] = result[:, HEAD_SIZE:]


def own_sums(
    place, queries, prompt_keys, prompt_values, blocks, pair, received, tables, tokens_after
):
    parts = len(blocks) + 1
    tokens = prompt_keys.shape[0]
    chosen = pl.BlockSpec((tokens, prompt_keys.shape[1] // parts), lambda i, p: (0, p[0]))
    operands = (*blocks, pair, *received, *tables)
    outs = [shape(queries.shape, jnp.float32)] * 2
    return call(
        functools.partial(own_kernel, parts),
        (place,),
        (queries, prompt_keys, prompt_values, *operands, *tokens_after),
        outs,
        [whole(queries), chosen, chosen]
        + [whole(a) for a in operands]
        + [corner(a) for a in tokens_after],
        [whole(a) for a in outs],
        (1,),
        [],
        6 * queries.size * parts * tokens,
        4 * parts * tokens * HEAD_SIZE,
    )


def diagonal(first, second):
    zero = jnp.zeros(first.shape, first.dtype)
    return jnp.concatenate(
        [
            jnp.concatenate([first, zero], axis=1),
            jnp.concatenate([zero, second], axis=1),
        ],
        axis=0,
    )


def suffix_kernel(parts, place, lengths, own_ref, *refs):
    received, (k_ref, v_ref), refs = (
        refs[: parts - 1],
        refs[parts - 1 : parts + 1],
        refs[-(parts + 5) :],
    )
    outs, refs = refs[: parts + 1], refs[parts + 1 :]
    query_held, sums, totals, packed = refs
    members, slots, columns = k_ref.shape
    heads = columns // HEAD_SIZE
    near = heads // parts
    here = place[0]
    packed[...] = jnp.zeros(packed.shape, jnp.float32)
    count = members * 8
    for mask, ref in enumerate((own_ref, *received)):
        for head in range(near):
            target = query_held.at[(here ^ mask) * near + head]
            if mask == 0:
                target[...] = ref[head * count : (head + 1) * count, :].astype(jnp.float32)
                continue
            tall = own_ref.shape[0] * HEAD_SIZE // ref.shape[1]
            for half in range(count // tall):
                target[half * tall : (half + 1) * tall, :] = ref[
                    ref.shape[0] - tall :, head_lanes(head * count // tall + half)
                ].astype(jnp.float32)

    for member in range(members):
        tile = slice(member * 8, (member + 1) * 8)
        pairs = [slice(at, at + 2 * HEAD_SIZE) for at in range(0, columns, 2 * HEAD_SIZE)]
        scores = jnp.concatenate(
            [
                dot_last(
                    diagonal(
                        query_held[2 * index, tile, :], query_held[2 * index + 1, tile, :]
                    ).astype(jnp.bfloat16),
                    k_ref[member, :, lanes],
                )
                for index, lanes in enumerate(pairs)
            ],
            axis=0,
        )
        valid = lax.broadcasted_iota(jnp.int32, scores.shape, 1) < lengths[here * members + member]
        weight = jnp.where(valid, capped_weight(scores), 0.0)
        total = jnp.broadcast_to(jnp.sum(weight, axis=1, keepdims=True), (heads * 8, LANES))
        weight = weight.astype(jnp.bfloat16)
        for index, lanes in enumerate(pairs):
            result = jnp.dot(
                weight[16 * index : 16 * (index + 1)],
                v_ref[member, :, lanes],
                preferred_element_type=jnp.float32,
            )
            sums[2 * index, tile, :] = result[:8, :HEAD_SIZE]
            sums[2 * index + 1, tile, :] = result[8:, HEAD_SIZE:]
        for head in range(heads):
            totals[head, tile, :] = total[head * 8 : (head + 1) * 8]

    for mask in range(parts):
        for head in range(near):
            at = slice(head * count, (head + 1) * count)
            index = (here ^ mask) * near + head
            if mask == 0:
                outs[0][at, :] = sums[index]
                outs[1][at, :] = totals[index]
            else:
                outs[mask + 1][at, :] = sums[index].astype(jnp.bfloat16)
        if mask > 0:
            both = jnp.concatenate(
                [totals[(here ^ mask) * near + head] for head in range(near)], axis=0
            )
            packed[0:1, :] = both.T[0:1]
            outs[mask + 1][near * count :, :] = split_rows(packed[...])


def suffix_attention(place, lengths, own, received, cache_keys, cache_values, tokens_after):
    parts = len(received) + 1
    members, slots, columns = cache_keys.shape
    heads = columns // HEAD_SIZE
    count = heads // parts * members * 8
    outs = [shape((count, HEAD_SIZE), jnp.float32)] * 2 + [
        shape((count + 16, HEAD_SIZE), jnp.bfloat16)
    ] * (parts - 1)
    far = pl.BlockSpec(memory_space=pltpu.VMEM)
    return call(
        functools.partial(suffix_kernel, parts),
        (place, lengths),
        (own, *received, cache_keys, cache_values, *tokens_after),
        outs,
        [whole(own)]
        + [whole(a) for a in received]
        + [far, far]
        + [corner(a) for a in tokens_after],
        [whole(a) for a in outs],
        (1,),
        [
            pltpu.VMEM((heads, members * 8, HEAD_SIZE), jnp.float32),
            pltpu.VMEM((heads, members * 8, HEAD_SIZE), jnp.float32),
            pltpu.VMEM((heads, members * 8, HEAD_SIZE), jnp.float32),
            pltpu.VMEM((8, LANES), jnp.float32),
        ],
        4 * members * 8 * slots * columns,
        4 * members * slots * columns,
        SUFFIX_LIMIT,
    )


def mix_kernel(parts, far, place, sum_ref, total_ref, *refs):
    prompt, refs = refs[:far], refs[far:]
    near_sum, near_total, *suffix = refs[: parts + 1]
    out_ref, sums, totals = refs[parts + 1 :]
    count = sum_ref.shape[0]
    rows = out_ref.shape[0]
    heads = count // (2 * rows)
    total = sum_ref[...]
    for ref in prompt:
        total = total + ref[:count, :].astype(jnp.float32)
    sums[...] = total
    for block in range(count // LANES):
        at = slice(block * LANES, (block + 1) * LANES)
        total = total_ref[at, :]
        for ref in prompt:
            total = total + down_rows(joined_row(ref[count:, :], block))
        totals[at, :] = total
    share = 2 * rows // parts
    for mask in range(parts):
        if mask == 0:
            near, near_weight = near_sum[...], near_total[...]
        else:
            ref = suffix[mask - 1]
            near = ref[: count // parts, :].astype(jnp.float32)
            near_weight = down_rows(joined_row(ref[count // parts : count // parts + 16, :], 0))
        for head in range(heads):
            first = pl.multiple_of(head * 2 * rows + (place[0] ^ mask) * share, share)
            at = pl.ds(first, share)
            local = slice(head * share, (head + 1) * share)
            sums[at, :] = sums[at, :] + near[local]
            totals[at, :] = totals[at, :] + near_weight[local]
    mixed = sums[...] / totals[...]
    for head in range(heads):
        tiles = mixed[head * 2 * rows : (head + 1) * 2 * rows].reshape(rows // 8, 2, 8, HEAD_SIZE)
        for member, part in enumerate(interleave(tiles[:, 0], tiles[:, 1])):
            at = (2 * head + member) * HEAD_SIZE
            out_ref[:, at : at + HEAD_SIZE] = part.reshape(rows, HEAD_SIZE).astype(jnp.bfloat16)


def mix(place, sums, totals, prompt, suffix, rows):
    count = sums.shape[0]
    operands = (sums, totals, *prompt, *suffix)
    out = shape((rows, count // rows * HEAD_SIZE), jnp.bfloat16)
    return call(
        functools.partial(mix_kernel, len(suffix) - 1, len(prompt)),
        (place,),
        operands,
        out,
        [whole(a) for a in operands],
        whole(out),
        (1,),
        [pltpu.VMEM((count, HEAD_SIZE), jnp.float32)] * 2,
        10 * count * HEAD_SIZE,
        8 * count * HEAD_SIZE,
    )


def output_kernel(masks, started, place, *refs):
    inputs, refs = refs[: len(masks)], refs[len(masks) :]
    w_ref, out_ref = refs[0], refs[-1]
    step = pl.program_id(0)
    for index, ref in enumerate(inputs):

        @pl.when(step == index)
        def _():
            term = jnp.dot(ref[...], w_ref[...], preferred_element_type=jnp.float32)
            if index > 0:
                out_ref[...] += term
            elif started:
                out_ref[...] = refs[1][...] + term
            else:
                out_ref[...] = term


def output_projection(place, masks, mixed, weights, started=None):
    rows, depth = mixed[0].shape
    width = weights.shape[1]
    chosen = pl.BlockSpec(
        (depth, width), lambda i, p: (p[0] ^ (i + masks[0]), 0)
    )
    out = shape((rows, width), jnp.float32)
    more = () if started is None else (started,)
    return call(
        functools.partial(output_kernel, masks, started is not None),
        (place,),
        (*mixed, weights, *more),
        out,
        [whole(a) for a in mixed] + [chosen] + [whole(a) for a in more],
        whole(out),
        (len(masks),),
        [],
        2 * len(masks) * rows * depth * width,
        2 * len(masks) * depth * width,
    )


def attended_kernel(place, here_ref, there_ref, out_ref, squares_ref):
    attended = here_ref[...] + there_ref[...].astype(jnp.float32)
    out_ref[...] = attended
    total = jnp.sum(attended * attended, axis=1, keepdims=True)
    squares_ref[...] = jnp.broadcast_to(total, (total.shape[0], LANES)).T[:8]


def attended_squares(place, here, there):
    outs = [shape(here.shape, jnp.float32), shape((8, here.shape[0]), jnp.float32)]
    return call(
        attended_kernel,
        (place,),
        (here, there),
        outs,
        [whole(here), whole(there)],
        [whole(a) for a in outs],
        (1,),
        [],
        4 * here.size,
        12 * here.size,
    )


def finish_kernel(place, x_ref, attended_ref, gain_ref, *refs):
    *squares, out_ref = refs
    total = squares[0][0:1, :]
    for ref in squares[1:]:
        total = total + ref[0:1, :]
    inverse = lax.rsqrt(down_rows(total) / MODEL_WIDTH + EPSILON)
    for at in range(0, x_ref.shape[2], LANES):
        lanes = slice(at, at + LANES)
        branch = attended_ref[:, lanes] * inverse * gain_ref[lanes].reshape(1, LANES)
        x = x_ref[:, :, lanes].astype(jnp.float32)
        out_ref[:, :, lanes] = (x + branch.reshape(x.shape)).astype(jnp.bfloat16)


def finish(place, x, attended, gain, squares):
    operands = (x, attended, gain, *squares)
    out = shape(x.shape, jnp.bfloat16)
    return call(
        finish_kernel,
        (place,),
        operands,
        out,
        [whole(a) for a in operands],
        whole(out),
        (1,),
        [],
        4 * x.size,
        8 * x.size,
    )


def by_heads(
    hidden_in,
    pre_gain,
    w_query,
    key_projection,
    value_projection,
    w_out,
    post_gain,
    prompt_keys,
    prompt_values,
    suffix_key_cache,
    suffix_value_cache,
    suffix_len,
):
    group_rows, steps, _ = hidden_in.shape
    rows = group_rows * steps
    if rows != LANES or steps != 4:
        return per_device(
            hidden_in,
            pre_gain,
            w_query,
            key_projection,
            value_projection,
            w_out,
            post_gain,
            prompt_keys,
            prompt_values,
            suffix_key_cache,
            suffix_value_cache,
            suffix_len,
        )
    parts = lax.axis_size("prefix")
    groups = lax.axis_size("prefill")
    prompt_total = prompt_keys.shape[0] * groups * parts
    place = lax.axis_index("prefix").astype(jnp.int32).reshape(1)
    near = range(1, parts)
    far = range(1, groups)

    def swapped(arrays, axis):
        pairs = list(enumerate(arrays, start=1))
        moved = {m: paired(a, axis, m) for m, a in pairs[-1:] + pairs[:-1]}
        return [moved[m] for m, _ in pairs]

    *sent, own, scaled = query_projection(place, hidden_in, pre_gain, w_query, parts)
    received = swapped(sent, "prefix")
    keys, values, _ = lax.optimization_barrier((prompt_keys, prompt_values, own))
    blocks = swapped(owner_columns(place, keys, values, parts), "prefix")

    positions = (
        (prompt_total + suffix_len[:, None] + jnp.arange(steps, dtype=jnp.int32)[None, :])
        .reshape(-1)
        .astype(jnp.float32)
    )
    half = HEAD_SIZE // 2
    freq = 10000.0 ** (-2.0 * jnp.arange(half, dtype=jnp.float32) / HEAD_SIZE)
    angle = positions[:, None] * freq[None, :]
    cosine, sine = jnp.cos(angle), jnp.sin(angle)
    cosine = jnp.concatenate([cosine, cosine], axis=1)
    sine = jnp.concatenate([-sine, sine], axis=1)

    queries, *split_queries, inverse = query_rope(
        place, own, received, cosine, sine, parts
    )
    pair, *sent = pair_projection(
        place, scaled, key_projection, value_projection, split_queries[1:]
    )
    held_back = lax.optimization_barrier((queries, blocks[0], pair))[0]
    far_queries = [paired(held_back if m == 1 else queries, "prefill", m) for m in far]
    returned = swapped(sent, "prefix")
    first = prompt_first(place, far_queries, prompt_keys, prompt_values, blocks[:1], parts)
    packed = [
        prompt_last(place, q, blocks[1:], first[2 * i : 2 * i + 2])
        for i, q in enumerate(far_queries)
    ]
    prompt_results = swapped(packed, "prefill")
    near_sums, near_totals, *sent = suffix_attention(
        place,
        suffix_len,
        split_queries[0],
        returned,
        suffix_key_cache,
        suffix_value_cache,
        packed,
    )
    suffix = [near_sums, near_totals, *swapped(sent, "prefix")]
    sums, totals = own_sums(
        place,
        queries,
        prompt_keys,
        prompt_values,
        blocks,
        pair,
        returned,
        (inverse, cosine, sine),
        [near_totals, prompt_results[2]],
    )
    mixed = mix(place, sums, totals, prompt_results, suffix, rows)
    others = [paired(mixed, "prefix", m) for m in near]
    head_terms = output_projection(place, (0,), [mixed], w_out)
    for mask, other in zip(near, others):
        head_terms = output_projection(place, (mask,), [other], w_out, head_terms)
    attended, squares = attended_squares(
        place, head_terms, paired(head_terms.astype(jnp.bfloat16), "tensor", 1)
    )
    squares = [squares] + [paired(squares, "prefix", m) for m in near]
    return finish(place, hidden_in, attended, post_gain, squares)


def heads_divide(mesh):
    sizes = [mesh.shape[name] for name in ("prefill", "prefix", "tensor")]
    key_heads = QUERY_HEADS // 2 // sizes[2]
    return key_heads == 2 * sizes[1] and sizes[1] == 4 and sizes[2] == 2 and sizes[0] in (2, 4)


def solution(mesh):
    return jax.shard_map(
        by_heads if heads_divide(mesh) else per_device,
        mesh=mesh,
        in_specs=(
            P("prefill", None, "prefix"),
            P("prefix"),
            P("prefix", "tensor"),
            P("prefix", "tensor"),
            P("prefix", "tensor"),
            P("tensor", "prefix"),
            P("prefix"),
            P(("prefill", "prefix"), "tensor"),
            P(("prefill", "prefix"), "tensor"),
            P(("prefill", "prefix"), None, "tensor"),
            P(("prefill", "prefix"), None, "tensor"),
            P("prefill"),
        ),
        out_specs=P("prefill", None, "prefix"),
        check_vma=False,
    )
```

```python
import functools

import jax
import jax.numpy as jnp
from jax import lax
from jax.experimental import pallas as pl
from jax.experimental.pallas import tpu as pltpu
from jax.sharding import PartitionSpec as P

MODEL_WIDTH = 4608
QUERY_HEADS = 32
HEAD_SIZE = 128


SOFTCAP = 50.0
EPSILON = 1e-06
LOG2_E = 1.4426950408889634
LANES = 128
VMEM_LIMIT = 24 * 1024 * 1024
FIRST_LIMIT = 59 * 1024 * 1024
ROPE_LIMIT = 24 * 1024 * 1024
PAIR_LIMIT = 24 * 1024 * 1024
SUFFIX_LIMIT = 24 * 1024 * 1024
QUERY_SCALE = (MODEL_WIDTH // QUERY_HEADS) ** (-0.5)


def apply_rotation(values, token_positions, heads):
    width = values.shape[1] // heads
    half = width // 2
    freq = 10000.0 ** (-2.0 * jnp.arange(half, dtype=jnp.float32) / width)
    angle = token_positions[:, None] * freq[None, :]
    cosine = jnp.cos(angle)[:, None, :]
    sine = jnp.sin(angle)[:, None, :]
    parts = values.reshape(values.shape[0], heads, width)
    first = parts[:, :, :half]
    second = parts[:, :, half:]
    turned = jnp.concatenate(
        [first * cosine - second * sine, second * cosine + first * sine], axis=2
    )
    return turned.reshape(values.shape[0], heads * width)


def soft_weight(scores):
    return jnp.exp(SOFTCAP * jnp.tanh(scores / SOFTCAP))


def shared_attention(queries, keys, values):
    count = queries.shape[0]
    kv_heads = keys.shape[1] // HEAD_SIZE
    heads_per_group = queries.shape[1] // keys.shape[1]
    grouped = queries.reshape(count, kv_heads, heads_per_group, HEAD_SIZE)
    key_head_rows = keys.reshape(keys.shape[0], kv_heads, HEAD_SIZE)
    value_head_rows = values.reshape(values.shape[0], kv_heads, HEAD_SIZE)
    scores = jnp.einsum(
        "nkgd,mkd->nkgm", grouped, key_head_rows, preferred_element_type=jnp.float32
    )
    weights = soft_weight(scores)
    totals = jnp.sum(weights, axis=3).reshape(count, kv_heads * heads_per_group)
    summed = jnp.einsum(
        "nkgm,mkd->nkgd",
        weights.astype(jnp.bfloat16),
        value_head_rows,
        preferred_element_type=jnp.float32,
    )
    return (summed.reshape(count, kv_heads * heads_per_group * HEAD_SIZE), totals)


def own_attention(
    queries, cached_key_rows, cached_value_rows, latest_keys, latest_values, lengths, steps
):
    members = lengths.shape[0]
    slots = cached_key_rows.shape[1]
    kv_heads = cached_key_rows.shape[2] // HEAD_SIZE
    heads_per_group = queries.shape[1] // cached_key_rows.shape[2]
    grouped = queries.reshape(members, steps, kv_heads, heads_per_group, HEAD_SIZE)
    cache_k = cached_key_rows.reshape(members, slots, kv_heads, HEAD_SIZE)
    cache_v = cached_value_rows.reshape(members, slots, kv_heads, HEAD_SIZE)
    valid = jnp.arange(slots, dtype=jnp.int32)[None, :] < lengths[:, None]
    cache_scores = jnp.einsum(
        "rjkgd,rmkd->rjkgm", grouped, cache_k, preferred_element_type=jnp.float32
    )
    cache_weights = jnp.where(valid[:, None, None, None, :], soft_weight(cache_scores), 0.0)
    new_k = latest_keys.reshape(members, steps, kv_heads, HEAD_SIZE)
    new_v = latest_values.reshape(members, steps, kv_heads, HEAD_SIZE)
    step_ids = jnp.arange(steps, dtype=jnp.int32)
    causal = step_ids[None, :] <= step_ids[:, None]
    new_scores = jnp.einsum("rjkgd,rikd->rjkgi", grouped, new_k, preferred_element_type=jnp.float32)
    new_weights = jnp.where(causal[None, :, None, None, :], soft_weight(new_scores), 0.0)
    totals = jnp.sum(cache_weights, axis=4) + jnp.sum(new_weights, axis=4)
    summed = jnp.einsum(
        "rjkgm,rmkd->rjkgd",
        cache_weights.astype(jnp.bfloat16),
        cache_v,
        preferred_element_type=jnp.float32,
    )
    summed = summed + jnp.einsum(
        "rjkgi,rikd->rjkgd",
        new_weights.astype(jnp.bfloat16),
        new_v,
        preferred_element_type=jnp.float32,
    )
    flat_rows = members * steps
    return (
        summed.reshape(flat_rows, kv_heads * heads_per_group * HEAD_SIZE),
        totals.reshape(flat_rows, kv_heads * heads_per_group),
    )


def per_device(
    hidden_in,
    pre_gain,
    w_query,
    key_projection,
    value_projection,
    w_out,
    post_gain,
    prompt_keys,
    prompt_values,
    suffix_key_cache,
    suffix_value_cache,
    suffix_len,
):
    group_rows, steps, local_width = hidden_in.shape
    members = suffix_key_cache.shape[0]
    query_cols = w_query.shape[1]
    kv_cols = key_projection.shape[1]
    heads = query_cols // HEAD_SIZE
    kv_heads = kv_cols // HEAD_SIZE
    own_count = members * steps
    prompt_total = prompt_keys.shape[0] * lax.axis_size("prefill") * lax.axis_size("prefix")
    signal = hidden_in.astype(jnp.float32).reshape(group_rows * steps, local_width)
    squares = lax.psum(jnp.sum(signal * signal, axis=1), "prefix")
    normed = (signal * lax.rsqrt(squares[:, None] / MODEL_WIDTH + EPSILON) * pre_gain).astype(
        jnp.bfloat16
    )
    weights_all = jnp.concatenate([w_query, key_projection, value_projection], axis=1)
    step_ids = jnp.arange(steps, dtype=jnp.int32)
    group_positions = (
        (prompt_total + suffix_len[:, None] + step_ids[None, :]).reshape(-1).astype(jnp.float32)
    )
    first_row = lax.axis_index("prefix") * members
    own_lengths = lax.dynamic_slice_in_dim(suffix_len, first_row, members)
    own_positions = lax.dynamic_slice_in_dim(group_positions, first_row * steps, own_count)
    scale = (MODEL_WIDTH // QUERY_HEADS) ** (-0.5)
    own_proj = lax.psum_scatter(
        jnp.dot(normed, weights_all, preferred_element_type=jnp.float32),
        "prefix",
        scatter_dimension=0,
        tiled=True,
    )
    own_queries = (apply_rotation(own_proj[:, :query_cols], own_positions, heads) * scale).astype(
        jnp.bfloat16
    )
    group_queries = lax.all_gather(own_queries, "prefix", axis=0, tiled=True)
    latest_keys = apply_rotation(
        own_proj[:, query_cols : query_cols + kv_cols], own_positions, kv_heads
    ).astype(jnp.bfloat16)
    latest_values = own_proj[:, query_cols + kv_cols :].astype(jnp.bfloat16)
    summed, totals = shared_attention(
        group_queries,
        lax.all_gather(prompt_keys, "prefill", axis=0, tiled=True),
        lax.all_gather(prompt_values, "prefill", axis=0, tiled=True),
    )
    prompt_totals = totals
    far_sums, far_totals = (
        lax.psum_scatter(summed, "prefix", scatter_dimension=0, tiled=True),
        lax.psum_scatter(prompt_totals, "prefix", scatter_dimension=0, tiled=True),
    )
    near_sums, near_totals = own_attention(
        own_queries,
        suffix_key_cache,
        suffix_value_cache,
        latest_keys,
        latest_values,
        own_lengths,
        steps,
    )
    totals = far_totals + near_totals
    sums = (far_sums + near_sums).reshape(own_count, heads, HEAD_SIZE)
    mixed = (sums / totals[:, :, None]).reshape(own_count, query_cols).astype(jnp.bfloat16)
    head_terms = jnp.dot(
        lax.all_gather(mixed, "prefix", axis=0, tiled=True),
        w_out,
        preferred_element_type=jnp.float32,
    )
    attended = lax.psum(head_terms, "tensor")
    out_squares = lax.psum(jnp.sum(attended * attended, axis=1), "prefix")
    branch = attended * lax.rsqrt(out_squares[:, None] / MODEL_WIDTH + EPSILON) * post_gain
    return (signal + branch).astype(jnp.bfloat16).reshape(group_rows, steps, local_width)


def paired(values, axis, mask):
    size = lax.axis_size(axis)
    return lax.ppermute(values, axis, [(i, i ^ mask) for i in range(size)])


def call(
    kernel,
    prefetch,
    operands,
    out_shape,
    in_specs,
    out_specs,
    grid,
    scratch,
    flops,
    moved,
    limit=VMEM_LIMIT,
):
    return pl.pallas_call(
        kernel,
        out_shape=out_shape,
        grid_spec=pltpu.PrefetchScalarGridSpec(
            num_scalar_prefetch=len(prefetch),
            grid=grid,
            in_specs=in_specs,
            out_specs=out_specs,
            scratch_shapes=scratch,
        ),
        compiler_params=pltpu.CompilerParams(vmem_limit_bytes=limit),
        cost_estimate=pl.CostEstimate(flops=flops, bytes_accessed=moved, transcendentals=0),
    )(*prefetch, *operands)


def whole(array):
    rank = len(array.shape)
    return pl.BlockSpec(array.shape, lambda *_: (0,) * rank)


def corner(array):
    rank = len(array.shape)
    return pl.BlockSpec(
        (1,) * (rank - 2) + (32 // array.dtype.itemsize, LANES), lambda *_: (0,) * rank
    )


def shape(dims, dtype):
    return jax.ShapeDtypeStruct(dims, dtype)


def dot_last(left, right):
    return lax.dot_general(left, right, (((1,), (1,)), ((), ())), preferred_element_type=jnp.float32)


def dot_first(left, right):
    return lax.dot_general(left, right, (((0,), (0,)), ((), ())), preferred_element_type=jnp.float32)


def capped_weight(scores):
    return jnp.exp2(jnp.tanh(scores * (1.0 / SOFTCAP)) * (SOFTCAP * LOG2_E))


def split_rows(rows):
    high = rows.astype(jnp.bfloat16).astype(jnp.float32)
    return jnp.concatenate([high, rows - high], axis=0).astype(jnp.bfloat16)


def joined_row(block, index):
    pair = block.astype(jnp.float32)
    return pair[index : index + 1] + pair[8 + index : 9 + index]


def down_rows(row):
    return jnp.broadcast_to(row, (LANES, row.shape[1])).T


def lower_half(tiles):
    return lax.broadcasted_iota(jnp.int32, tiles.shape, 1) < tiles.shape[1] // 2


def interleave(first, second):
    low = lower_half(first)
    half = first.shape[1] // 2
    return (
        jnp.where(low, first, pltpu.roll(second, half, 1)),
        jnp.where(low, pltpu.roll(first, half, 1), second),
    )


def rotated(values, cosine, sine):
    return values * cosine + pltpu.roll(values, HEAD_SIZE // 2, 1) * sine


def gain_row(ref):
    return ref[...].reshape(1, ref.shape[0])


def copy_in(source, target, semaphore):
    copy = pltpu.make_async_copy(source, target, semaphore)
    copy.start()
    return copy


def block_of(place, mask, width):
    return pl.ds(pl.multiple_of((place[0] ^ mask) * width, width), width)


def query_projection_kernel(place, gain_ref, x_hbm, w_hbm, *refs):
    *sent, own_ref, scaled_ref, x_ref, w_ref, semaphores = refs
    rows, columns = scaled_ref.shape[0], own_ref.shape[1]
    masks = (*range(1, len(sent) + 1), 0)
    x_copy = copy_in(x_hbm, x_ref, semaphores.at[len(masks)])
    w_copies = [
        copy_in(w_hbm.at[:, block_of(place, mask, columns)], w_ref.at[mask], semaphores.at[mask])
        for mask in masks
    ]
    x_copy.wait()
    x = x_ref[...].astype(jnp.float32).reshape(rows, x_ref.shape[2])
    scaled_ref[...] = (x * gain_row(gain_ref)).astype(jnp.bfloat16)
    total = jnp.sum(x * x, axis=1, keepdims=True)
    across = jnp.broadcast_to(total, (rows, LANES)).T[:8]
    own_ref[rows:, :] = jnp.zeros((8, columns), jnp.float32)
    own_ref[rows:, :rows] = across
    tail = split_rows(across)
    for ref in sent:
        ref[ref.shape[0] - 16 :, :] = tail
    for mask, copy, ref in zip(masks, w_copies, (*sent, own_ref)):
        copy.wait()
        product = jnp.dot(scaled_ref[...], w_ref[mask], preferred_element_type=jnp.float32)
        if mask == 0:
            own_ref[:rows, :] = product
            continue
        for head in range(columns // HEAD_SIZE):
            at = slice(head * rows, (head + 1) * rows)
            ref[at, :] = product[:, head_lanes(head)].astype(ref.dtype)


def query_projection(place, x, gain, weights, parts):
    members, steps, width = x.shape
    rows = members * steps
    columns = weights.shape[1] // parts
    outs = [shape((rows * columns // HEAD_SIZE + 16, HEAD_SIZE), jnp.bfloat16)] * (parts - 1) + [
        shape((rows + 8, columns), jnp.float32),
        shape((rows, width), jnp.bfloat16),
    ]
    far = pl.BlockSpec(memory_space=pl.ANY)
    return call(
        query_projection_kernel,
        (place,),
        (gain, x, weights),
        outs,
        [whole(gain), far, far],
        [whole(a) for a in outs],
        (1,),
        [
            pltpu.VMEM(x.shape, x.dtype),
            pltpu.VMEM((parts, width, columns), weights.dtype),
            pltpu.SemaphoreType.DMA((parts + 1,)),
        ],
        2 * rows * width * weights.shape[1],
        2 * width * weights.shape[1],
        FIRST_LIMIT,
    )


def owner_columns_kernel(place, keys_hbm, values_hbm, *refs):
    *outs, semaphores = refs
    width = outs[0].shape[1] // 2
    copies = [
        copy_in(
            source.at[:, block_of(place, mask, width)],
            ref.at[:, half * width : (half + 1) * width],
            semaphores.at[mask - 1, half],
        )
        for mask, ref in enumerate(outs, start=1)
        for half, source in enumerate((keys_hbm, values_hbm))
    ]
    for copy in copies:
        copy.wait()


def owner_columns(place, keys, values, parts):
    tokens = keys.shape[0]
    columns = keys.shape[1] // parts
    outs = [shape((tokens, 2 * columns), keys.dtype)] * (parts - 1)
    far = pl.BlockSpec(memory_space=pl.ANY)
    return call(
        owner_columns_kernel,
        (place,),
        (keys, values),
        outs,
        [far, far],
        [whole(a) for a in outs],
        (1,),
        [pltpu.SemaphoreType.DMA((parts - 1, 2))],
        20000000000,
        8 * (parts - 1) * tokens * columns,
    )


def pair_projection_kernel(place, scaled_ref, k_hbm, v_hbm, *refs):
    parts = len(refs) // 2
    queries, (own_ref, *outs), (w_ref, semaphores) = (
        refs[: parts - 1],
        refs[parts - 1 : 2 * parts - 1],
        refs[2 * parts - 1 :],
    )
    rows, width = own_ref.shape
    columns = width // 2
    masks = (*range(1, parts), 0)
    copies = {}
    for mask in masks:
        at = block_of(place, mask, columns)
        copies[mask] = [
            copy_in(
                source.at[:, at],
                w_ref.at[mask, :, half * columns : (half + 1) * columns],
                semaphores.at[mask, half],
            )
            for half, source in enumerate((k_hbm, v_hbm))
        ]
    for ref, out_ref in zip(queries, outs):
        tall = out_ref.shape[0] - rows
        for piece in range(ref.shape[0] // tall):
            out_ref[rows:, head_lanes(piece)] = ref[piece * tall : (piece + 1) * tall, :]
    for mask in masks:
        for copy in copies[mask]:
            copy.wait()
        term = jnp.dot(scaled_ref[...], w_ref[mask], preferred_element_type=jnp.float32)
        target = outs[mask - 1] if mask else own_ref
        target[:rows, :] = term.astype(target.dtype)


def pair_projection(place, scaled, key_weights, value_weights, queries):
    parts = len(queries) + 1
    rows, width = scaled.shape
    columns = key_weights.shape[1] // parts
    far = pl.BlockSpec(memory_space=pl.ANY)
    tall = queries[0].size // (2 * columns)
    outs = [shape((rows, 2 * columns), jnp.float32)] + [
        shape((rows + tall, 2 * columns), jnp.bfloat16)
    ] * (parts - 1)
    return call(
        pair_projection_kernel,
        (place,),
        (scaled, key_weights, value_weights, *queries),
        outs,
        [whole(scaled), far, far] + [whole(a) for a in queries],
        [whole(a) for a in outs],
        (1,),
        [
            pltpu.VMEM((parts, width, 2 * columns), key_weights.dtype),
            pltpu.SemaphoreType.DMA((parts, 2)),
        ],
        4 * rows * width * key_weights.shape[1],
        4 * width * key_weights.shape[1],
        PAIR_LIMIT,
    )


def paired_heads(values, cosine, sine):
    tiles = [
        rotated(values[:, at : at + HEAD_SIZE], cosine, sine).reshape(-1, 8, HEAD_SIZE)
        for at in (0, HEAD_SIZE)
    ]
    return jnp.stack(interleave(*tiles), axis=1).reshape(2 * values.shape[0], HEAD_SIZE)


def query_rope_kernel(parts, place, own_ref, *refs):
    received, refs = refs[: parts - 1], refs[parts - 1 :]
    cos_ref, sin_ref, query_ref, *suffix_refs, inverse_ref, held = refs
    rows, columns = cos_ref.shape[0], own_ref.shape[1]
    squares = own_ref[rows : rows + 1, :rows]
    for ref in received:
        squares = squares + joined_row(ref[ref.shape[0] - 16 :, :], 0)
    inverse = lax.rsqrt(down_rows(squares) / MODEL_WIDTH + EPSILON)
    inverse_ref[...] = inverse
    cosine = cos_ref[...] * inverse * QUERY_SCALE
    sine = sin_ref[...] * inverse * QUERY_SCALE
    pair = 2 * HEAD_SIZE
    share = 2 * rows // parts
    for head in range(columns // pair):
        at = slice(head * 2 * rows, (head + 1) * 2 * rows)
        totals = []
        for index in (2 * head, 2 * head + 1):
            total = own_ref[:rows, head_lanes(index)]
            for ref in received:
                total = total + ref[index * rows : (index + 1) * rows, :].astype(jnp.float32)
            totals.append(total)
        held[...] = paired_heads(jnp.concatenate(totals, axis=1), cosine, sine)
        query_ref[at, :] = held[...].astype(jnp.bfloat16)
        for mask, ref in enumerate(suffix_refs):
            ref[head * share : (head + 1) * share, :] = held[
                block_of(place, mask, share), :
            ].astype(jnp.bfloat16)


def query_rope(place, own, received, cosine, sine, parts):
    rows, columns = cosine.shape[0], own.shape[1]
    count = rows * columns // HEAD_SIZE
    operands = (own, *received, cosine, sine)
    outs = (
        [shape((count, HEAD_SIZE), jnp.bfloat16)]
        + [shape((count // parts, HEAD_SIZE), jnp.bfloat16)] * parts
        + [shape((rows, LANES), jnp.float32)]
    )
    return call(
        functools.partial(query_rope_kernel, parts),
        (place,),
        operands,
        outs,
        [whole(a) for a in operands],
        [whole(a) for a in outs],
        (1,),
        [pltpu.VMEM((2 * rows, HEAD_SIZE), jnp.float32)],
        10000000000,
        12 * rows * columns,
        ROPE_LIMIT,
    )


def attend(query, pairs):
    result = None
    for key, value in pairs:
        weight = capped_weight(dot_last(query, key)).astype(jnp.bfloat16)
        ones = jnp.ones((value.shape[0], LANES), jnp.bfloat16)
        term = jnp.dot(
            weight, jnp.concatenate([value, ones], axis=1), preferred_element_type=jnp.float32
        )
        result = term if result is None else result + term
    return result


def total_rows(totals):
    return [totals[at : at + LANES].T[0:1] for at in range(0, totals.shape[0], LANES)]


def head_lanes(head):
    return slice(head * HEAD_SIZE, (head + 1) * HEAD_SIZE)


def received_pair(ref, head, heads):
    return ref[:, head_lanes(head)], ref[:, head_lanes(heads + head)]


def prompt_first_kernel(chunks, place, *refs):
    queries, refs = refs[:chunks], refs[chunks:]
    k_ref, v_ref, *received = refs[: -2 * chunks]
    outs = refs[-2 * chunks :]
    heads = k_ref.shape[1] // HEAD_SIZE
    count = queries[0].shape[0] // heads
    for index, query_ref in enumerate(queries):
        sum_ref, total_ref = outs[2 * index : 2 * index + 2]
        for head in range(heads):
            at = slice(head * count, (head + 1) * count)
            pairs = [(k_ref[:, head_lanes(head)], v_ref[:, head_lanes(head)])]
            pairs += [received_pair(ref, head, heads) for ref in received]
            result = attend(query_ref[at, :], pairs)
            sum_ref[at, :] = result[:, :HEAD_SIZE]
            total_ref[at, :] = result[:, HEAD_SIZE:]


def prompt_first(place, queries, prompt_keys, prompt_values, received, parts):
    tokens = prompt_keys.shape[0]
    chosen = pl.BlockSpec((tokens, prompt_keys.shape[1] // parts), lambda i, p: (0, p[0]))
    outs = [shape(queries[0].shape, jnp.float32)] * (2 * len(queries))
    return call(
        functools.partial(prompt_first_kernel, len(queries)),
        (place,),
        (*queries, prompt_keys, prompt_values, *received),
        outs,
        [whole(a) for a in queries] + [chosen, chosen] + [whole(a) for a in received],
        [whole(a) for a in outs],
        (1,),
        [],
        6 * len(queries) * queries[0].size * (len(received) + 1) * tokens,
        4 * parts * tokens * HEAD_SIZE,
    )


def prompt_last_kernel(place, q_ref, *refs):
    *blocks, sum_ref, total_ref, out_ref, held = refs
    heads = blocks[0].shape[1] // (2 * HEAD_SIZE)
    count = q_ref.shape[0] // heads
    held[...] = jnp.zeros(held.shape, jnp.float32)
    for head in range(heads):
        at = slice(head * count, (head + 1) * count)
        result = attend(q_ref[at, :], [received_pair(ref, head, heads) for ref in blocks])
        out_ref[at, :] = (sum_ref[at, :] + result[:, :HEAD_SIZE]).astype(jnp.bfloat16)
        for row, values in enumerate(total_rows(total_ref[at, :] + result[:, HEAD_SIZE:])):
            to = head * count // LANES + row
            held[to : to + 1, :] = values
    out_ref[heads * count :, :] = split_rows(held[...])


def prompt_last(place, queries, blocks, first):
    out = shape((queries.shape[0] + 16, HEAD_SIZE), jnp.bfloat16)
    operands = (queries, *blocks, *first)
    return call(
        prompt_last_kernel,
        (place,),
        operands,
        out,
        [whole(a) for a in operands],
        whole(out),
        (1,),
        [pltpu.VMEM((8, LANES), jnp.float32)],
        6 * queries.size * len(blocks) * blocks[0].shape[0],
        2 * len(blocks) * blocks[0].size,
    )


def own_kernel(parts, place, q_ref, k_ref, v_ref, *refs):
    blocks, refs = refs[: parts - 1], refs[parts - 1 :]
    pair_ref, refs = refs[0], refs[1:]
    received, refs = refs[: parts - 1], refs[parts - 1 :]
    inverse_ref, cos_ref, sin_ref = refs[:3]
    sum_ref, total_ref = refs[-2:]
    heads = k_ref.shape[1] // HEAD_SIZE
    count = q_ref.shape[0] // heads
    rows = inverse_ref.shape[0]
    inverse = inverse_ref[...]
    cosine = cos_ref[...] * inverse
    sine = sin_ref[...] * inverse

    def new_terms(index):
        term = pair_ref[:, head_lanes(index)]
        for ref in received:
            term = term + ref[:rows, head_lanes(index)].astype(jnp.float32)
        return term

    query_row = lax.broadcasted_iota(jnp.int32, (count, rows), 0)
    key_row = lax.broadcasted_iota(jnp.int32, (count, rows), 1)
    same = query_row // 8 == key_row // 4
    valid = same & (key_row % 4 <= query_row % 4)
    ones = jnp.ones((rows, LANES), jnp.bfloat16)
    for head in range(heads):
        at = slice(head * count, (head + 1) * count)
        query = q_ref[at, :]
        key = rotated(new_terms(head), cosine, sine)
        value = new_terms(heads + head) * inverse
        weight = capped_weight(dot_last(query, key.astype(jnp.bfloat16)))
        weight = jnp.where(valid, weight, 0.0).astype(jnp.bfloat16)
        result = jnp.dot(
            weight,
            jnp.concatenate([value.astype(jnp.bfloat16), ones], axis=1),
            preferred_element_type=jnp.float32,
        )
        pairs = [(k_ref[:, head_lanes(head)], v_ref[:, head_lanes(head)])]
        pairs += [received_pair(ref, head, heads) for ref in blocks]
        result = result + attend(query, pairs)
        sum_ref[at, :] = result[:, :HEAD_SIZE]
        total_ref[at, :] = result[:, HEAD_SIZE:]


def own_sums(
    place, queries, prompt_keys, prompt_values, blocks, pair, received, tables, tokens_after
):
    parts = len(blocks) + 1
    tokens = prompt_keys.shape[0]
    chosen = pl.BlockSpec((tokens, prompt_keys.shape[1] // parts), lambda i, p: (0, p[0]))
    operands = (*blocks, pair, *received, *tables)
    outs = [shape(queries.shape, jnp.float32)] * 2
    return call(
        functools.partial(own_kernel, parts),
        (place,),
        (queries, prompt_keys, prompt_values, *operands, *tokens_after),
        outs,
        [whole(queries), chosen, chosen]
        + [whole(a) for a in operands]
        + [corner(a) for a in tokens_after],
        [whole(a) for a in outs],
        (1,),
        [],
        6 * queries.size * parts * tokens,
        4 * parts * tokens * HEAD_SIZE,
    )


def diagonal(first, second):
    zero = jnp.zeros(first.shape, first.dtype)
    return jnp.concatenate(
        [
            jnp.concatenate([first, zero], axis=1),
            jnp.concatenate([zero, second], axis=1),
        ],
        axis=0,
    )


def suffix_kernel(parts, place, lengths, own_ref, *refs):
    received, (k_ref, v_ref), refs = (
        refs[: parts - 1],
        refs[parts - 1 : parts + 1],
        refs[-(parts + 5) :],
    )
    outs, refs = refs[: parts + 1], refs[parts + 1 :]
    query_held, sums, totals, packed = refs
    members, slots, columns = k_ref.shape
    heads = columns // HEAD_SIZE
    near = heads // parts
    here = place[0]
    packed[...] = jnp.zeros(packed.shape, jnp.float32)
    count = members * 8
    for mask, ref in enumerate((own_ref, *received)):
        for head in range(near):
            target = query_held.at[(here ^ mask) * near + head]
            if mask == 0:
                target[...] = ref[head * count : (head + 1) * count, :].astype(jnp.float32)
                continue
            tall = own_ref.shape[0] * HEAD_SIZE // ref.shape[1]
            for half in range(count // tall):
                target[half * tall : (half + 1) * tall, :] = ref[
                    ref.shape[0] - tall :, head_lanes(head * count // tall + half)
                ].astype(jnp.float32)

    pairs = [slice(at, at + 2 * HEAD_SIZE) for at in range(0, columns, 2 * HEAD_SIZE)]
    for start in range(0, members, 4):
        together = range(start, min(start + 4, members))
        tiles = [slice(member * 8, (member + 1) * 8) for member in together]
        scores = [
            jnp.concatenate(
                [
                    dot_last(
                        diagonal(
                            query_held[2 * index, tile, :], query_held[2 * index + 1, tile, :]
                        ).astype(jnp.bfloat16),
                        k_ref[member, :, lanes],
                    )
                    for index, lanes in enumerate(pairs)
                ],
                axis=0,
            )
            for member, tile in zip(together, tiles)
        ]
        weights = []
        for member, tile, score in zip(together, tiles, scores):
            length = lengths[here * members + member]
            valid = lax.broadcasted_iota(jnp.int32, score.shape, 1) < length
            weight = jnp.where(valid, capped_weight(score), 0.0)
            total = jnp.broadcast_to(jnp.sum(weight, axis=1, keepdims=True), (heads * 8, LANES))
            weights.append(weight.astype(jnp.bfloat16))
            for head in range(heads):
                totals[head, tile, :] = total[head * 8 : (head + 1) * 8]
        for member, tile, weight in zip(together, tiles, weights):
            for index, lanes in enumerate(pairs):
                result = jnp.dot(
                    weight[16 * index : 16 * (index + 1)],
                    v_ref[member, :, lanes],
                    preferred_element_type=jnp.float32,
                )
                sums[2 * index, tile, :] = result[:8, :HEAD_SIZE]
                sums[2 * index + 1, tile, :] = result[8:, HEAD_SIZE:]

    for mask in range(parts):
        for head in range(near):
            at = slice(head * count, (head + 1) * count)
            index = (here ^ mask) * near + head
            if mask == 0:
                outs[0][at, :] = sums[index]
                outs[1][at, :] = totals[index]
            else:
                outs[mask + 1][at, :] = sums[index].astype(jnp.bfloat16)
        if mask > 0:
            both = jnp.concatenate(
                [totals[(here ^ mask) * near + head] for head in range(near)], axis=0
            )
            packed[0:1, :] = both.T[0:1]
            outs[mask + 1][near * count :, :] = split_rows(packed[...])


def suffix_attention(place, lengths, own, received, cache_keys, cache_values, tokens_after):
    parts = len(received) + 1
    members, slots, columns = cache_keys.shape
    heads = columns // HEAD_SIZE
    count = heads // parts * members * 8
    outs = [shape((count, HEAD_SIZE), jnp.float32)] * 2 + [
        shape((count + 16, HEAD_SIZE), jnp.bfloat16)
    ] * (parts - 1)
    far = pl.BlockSpec(memory_space=pltpu.VMEM)
    return call(
        functools.partial(suffix_kernel, parts),
        (place, lengths),
        (own, *received, cache_keys, cache_values, *tokens_after),
        outs,
        [whole(own)]
        + [whole(a) for a in received]
        + [far, far]
        + [corner(a) for a in tokens_after],
        [whole(a) for a in outs],
        (1,),
        [
            pltpu.VMEM((heads, members * 8, HEAD_SIZE), jnp.float32),
            pltpu.VMEM((heads, members * 8, HEAD_SIZE), jnp.float32),
            pltpu.VMEM((heads, members * 8, HEAD_SIZE), jnp.float32),
            pltpu.VMEM((8, LANES), jnp.float32),
        ],
        4 * members * 8 * slots * columns,
        4 * members * slots * columns,
        SUFFIX_LIMIT,
    )


def mix_kernel(parts, far, place, sum_ref, total_ref, *refs):
    prompt, refs = refs[:far], refs[far:]
    near_sum, near_total, *suffix = refs[: parts + 1]
    out_ref, sums, totals = refs[parts + 1 :]
    count = sum_ref.shape[0]
    rows = out_ref.shape[0]
    heads = count // (2 * rows)
    total = sum_ref[...]
    for ref in prompt:
        total = total + ref[:count, :].astype(jnp.float32)
    sums[...] = total
    for block in range(count // LANES):
        at = slice(block * LANES, (block + 1) * LANES)
        total = total_ref[at, :]
        for ref in prompt:
            total = total + down_rows(joined_row(ref[count:, :], block))
        totals[at, :] = total
    share = 2 * rows // parts
    for mask in range(parts):
        if mask == 0:
            near, near_weight = near_sum[...], near_total[...]
        else:
            ref = suffix[mask - 1]
            near = ref[: count // parts, :].astype(jnp.float32)
            near_weight = down_rows(joined_row(ref[count // parts : count // parts + 16, :], 0))
        for head in range(heads):
            first = pl.multiple_of(head * 2 * rows + (place[0] ^ mask) * share, share)
            at = pl.ds(first, share)
            local = slice(head * share, (head + 1) * share)
            sums[at, :] = sums[at, :] + near[local]
            totals[at, :] = totals[at, :] + near_weight[local]
    mixed = sums[...] / totals[...]
    for head in range(heads):
        tiles = mixed[head * 2 * rows : (head + 1) * 2 * rows].reshape(rows // 8, 2, 8, HEAD_SIZE)
        for member, part in enumerate(interleave(tiles[:, 0], tiles[:, 1])):
            at = (2 * head + member) * HEAD_SIZE
            out_ref[:, at : at + HEAD_SIZE] = part.reshape(rows, HEAD_SIZE).astype(jnp.bfloat16)


def mix(place, sums, totals, prompt, suffix, rows):
    count = sums.shape[0]
    operands = (sums, totals, *prompt, *suffix)
    out = shape((rows, count // rows * HEAD_SIZE), jnp.bfloat16)
    return call(
        functools.partial(mix_kernel, len(suffix) - 1, len(prompt)),
        (place,),
        operands,
        out,
        [whole(a) for a in operands],
        whole(out),
        (1,),
        [pltpu.VMEM((count, HEAD_SIZE), jnp.float32)] * 2,
        10 * count * HEAD_SIZE,
        8 * count * HEAD_SIZE,
    )


def output_kernel(masks, started, place, *refs):
    inputs, refs = refs[: len(masks)], refs[len(masks) :]
    w_ref, out_ref = refs[0], refs[-1]
    step = pl.program_id(0)
    for index, ref in enumerate(inputs):

        @pl.when(step == index)
        def _():
            term = jnp.dot(ref[...], w_ref[...], preferred_element_type=jnp.float32)
            if index > 0:
                out_ref[...] += term
            elif started:
                out_ref[...] = refs[1][...] + term
            else:
                out_ref[...] = term


def output_projection(place, masks, mixed, weights, started=None):
    rows, depth = mixed[0].shape
    width = weights.shape[1]
    chosen = pl.BlockSpec(
        (depth, width), lambda i, p: (p[0] ^ (i + masks[0]), 0)
    )
    out = shape((rows, width), jnp.float32)
    more = () if started is None else (started,)
    return call(
        functools.partial(output_kernel, masks, started is not None),
        (place,),
        (*mixed, weights, *more),
        out,
        [whole(a) for a in mixed] + [chosen] + [whole(a) for a in more],
        whole(out),
        (len(masks),),
        [],
        2 * len(masks) * rows * depth * width,
        2 * len(masks) * depth * width,
    )


def attended_kernel(place, here_ref, there_ref, out_ref, squares_ref):
    attended = here_ref[...] + there_ref[...].astype(jnp.float32)
    out_ref[...] = attended
    total = jnp.sum(attended * attended, axis=1, keepdims=True)
    squares_ref[...] = jnp.broadcast_to(total, (total.shape[0], LANES)).T[:8]


def attended_squares(place, here, there):
    outs = [shape(here.shape, jnp.float32), shape((8, here.shape[0]), jnp.float32)]
    return call(
        attended_kernel,
        (place,),
        (here, there),
        outs,
        [whole(here), whole(there)],
        [whole(a) for a in outs],
        (1,),
        [],
        4 * here.size,
        12 * here.size,
    )


def finish_kernel(place, x_ref, attended_ref, gain_ref, *refs):
    *squares, out_ref = refs
    total = squares[0][0:1, :]
    for ref in squares[1:]:
        total = total + ref[0:1, :]
    inverse = lax.rsqrt(down_rows(total) / MODEL_WIDTH + EPSILON)
    for at in range(0, x_ref.shape[2], LANES):
        lanes = slice(at, at + LANES)
        branch = attended_ref[:, lanes] * inverse * gain_ref[lanes].reshape(1, LANES)
        x = x_ref[:, :, lanes].astype(jnp.float32)
        out_ref[:, :, lanes] = (x + branch.reshape(x.shape)).astype(jnp.bfloat16)


def finish(place, x, attended, gain, squares):
    operands = (x, attended, gain, *squares)
    out = shape(x.shape, jnp.bfloat16)
    return call(
        finish_kernel,
        (place,),
        operands,
        out,
        [whole(a) for a in operands],
        whole(out),
        (1,),
        [],
        4 * x.size,
        8 * x.size,
    )


def by_heads(
    hidden_in,
    pre_gain,
    w_query,
    key_projection,
    value_projection,
    w_out,
    post_gain,
    prompt_keys,
    prompt_values,
    suffix_key_cache,
    suffix_value_cache,
    suffix_len,
):
    group_rows, steps, _ = hidden_in.shape
    rows = group_rows * steps
    if rows != LANES or steps != 4:
        return per_device(
            hidden_in,
            pre_gain,
            w_query,
            key_projection,
            value_projection,
            w_out,
            post_gain,
            prompt_keys,
            prompt_values,
            suffix_key_cache,
            suffix_value_cache,
            suffix_len,
        )
    parts = lax.axis_size("prefix")
    groups = lax.axis_size("prefill")
    prompt_total = prompt_keys.shape[0] * groups * parts
    place = lax.axis_index("prefix").astype(jnp.int32).reshape(1)
    near = range(1, parts)
    far = range(1, groups)

    def swapped(arrays, axis):
        pairs = list(enumerate(arrays, start=1))
        moved = {m: paired(a, axis, m) for m, a in pairs[-1:] + pairs[:-1]}
        return [moved[m] for m, _ in pairs]

    *sent, own, scaled = query_projection(place, hidden_in, pre_gain, w_query, parts)
    received = swapped(sent, "prefix")
    keys, values, _ = lax.optimization_barrier((prompt_keys, prompt_values, own))
    blocks = swapped(owner_columns(place, keys, values, parts), "prefix")

    positions = (
        (prompt_total + suffix_len[:, None] + jnp.arange(steps, dtype=jnp.int32)[None, :])
        .reshape(-1)
        .astype(jnp.float32)
    )
    half = HEAD_SIZE // 2
    freq = 10000.0 ** (-2.0 * jnp.arange(half, dtype=jnp.float32) / HEAD_SIZE)
    angle = positions[:, None] * freq[None, :]
    cosine, sine = jnp.cos(angle), jnp.sin(angle)
    cosine = jnp.concatenate([cosine, cosine], axis=1)
    sine = jnp.concatenate([-sine, sine], axis=1)

    queries, *split_queries, inverse = query_rope(
        place, own, received, cosine, sine, parts
    )
    pair, *sent = pair_projection(
        place, scaled, key_projection, value_projection, split_queries[1:]
    )
    held_back = lax.optimization_barrier((queries, blocks[0], pair))[0]
    far_queries = [paired(held_back if m == 1 else queries, "prefill", m) for m in far]
    returned = swapped(sent, "prefix")
    first = prompt_first(place, far_queries, prompt_keys, prompt_values, blocks[:1], parts)
    packed = [
        prompt_last(place, q, blocks[1:], first[2 * i : 2 * i + 2])
        for i, q in enumerate(far_queries)
    ]
    prompt_results = swapped(packed, "prefill")
    near_sums, near_totals, *sent = suffix_attention(
        place,
        suffix_len,
        split_queries[0],
        returned,
        suffix_key_cache,
        suffix_value_cache,
        packed,
    )
    suffix = [near_sums, near_totals, *swapped(sent, "prefix")]
    sums, totals = own_sums(
        place,
        queries,
        prompt_keys,
        prompt_values,
        blocks,
        pair,
        returned,
        (inverse, cosine, sine),
        [near_totals, prompt_results[2]],
    )
    mixed = mix(place, sums, totals, prompt_results, suffix, rows)
    others = [paired(mixed, "prefix", m) for m in near]
    head_terms = output_projection(place, (0,), [mixed], w_out)
    for mask, other in zip(near, others):
        head_terms = output_projection(place, (mask,), [other], w_out, head_terms)
    attended, squares = attended_squares(
        place, head_terms, paired(head_terms.astype(jnp.bfloat16), "tensor", 1)
    )
    squares = [squares] + [paired(squares, "prefix", m) for m in near]
    return finish(place, hidden_in, attended, post_gain, squares)


def heads_divide(mesh):
    sizes = [mesh.shape[name] for name in ("prefill", "prefix", "tensor")]
    key_heads = QUERY_HEADS // 2 // sizes[2]
    return key_heads == 2 * sizes[1] and sizes[1] == 4 and sizes[2] == 2 and sizes[0] in (2, 4)


def solution(mesh):
    return jax.shard_map(
        by_heads if heads_divide(mesh) else per_device,
        mesh=mesh,
        in_specs=(
            P("prefill", None, "prefix"),
            P("prefix"),
            P("prefix", "tensor"),
            P("prefix", "tensor"),
            P("prefix", "tensor"),
            P("tensor", "prefix"),
            P("prefix"),
            P(("prefill", "prefix"), "tensor"),
            P(("prefill", "prefix"), "tensor"),
            P(("prefill", "prefix"), None, "tensor"),
            P(("prefill", "prefix"), None, "tensor"),
            P("prefill"),
        ),
        out_specs=P("prefill", None, "prefix"),
        check_vma=False,
    )
```
